32 devices in a mesh: dp: 8 (over z, y), sp: 4 (over x, core).
Axes of the slice: x: 2, y: 2, z: 4, core: 2. Of those that a mesh axis runs over, the one named last changes fastest.
Arguments:
- tokens: bfloat16 [8, 1024, 1024], P('dp', 'sp'), may hold values from -6 to 6
- cotangent: bfloat16 [8, 1024, 1024], P('dp', 'sp'), may hold values from -6 to 6
- w_qkv: bfloat16 [2, 3, 1024, 1024], P(None, None, ('dp', 'sp')), may hold values from -0.1875 to 0.1875
- w_out: bfloat16 [2, 1024, 1024], P(None, ('dp', 'sp')), may hold values from -0.75 to 0.75
- w_up: bfloat16 [2, 1024, 4096], P(None, ('dp', 'sp')), may hold values from -0.1875 to 0.1875
- w_down: bfloat16 [2, 4096, 1024], P(None, ('dp', 'sp')), may hold values from -0.125 to 0.125
- gains: bfloat16 [2, 2, 1024], P(None, None, ('dp', 'sp')), may hold values from 0.5 to 1.5
- piece_order: int32 [8, 4], P('dp'), may hold values from 0 to 3, each once within a row
- doc_lengths: int32 [8, 4], P('dp'), may hold values from 1 to 512, 1024 in all within a row
Outputs:
- output: bfloat16 [8, 1024, 1024], P('dp', 'sp')
- input_grad: float32 [8, 1024, 1024], P('dp', 'sp')
- grad_qkv: float32 [2, 3, 1024, 1024], P(None, None, ('dp', 'sp'))
- grad_out: float32 [2, 1024, 1024], P(None, ('dp', 'sp'))
- grad_up: float32 [2, 1024, 4096], P(None, ('dp', 'sp'))
- grad_down: float32 [2, 4096, 1024], P(None, ('dp', 'sp'))
- grad_gains: float32 [2, 2, 1024], P(None, None, ('dp', 'sp'))
The draws below stay inside these ranges and needn't reach their ends.
Inputs may be any that keep to these rules, and one draw needn't show every extreme that they name: Each row of piece_order names every index of sp once. `doc_lengths`: each row's lengths sum to 1024, and the longest is exactly 512.
All inputs are finite; a program needn't handle non-finite values.
Results may differ from the reference program's by a relative error of at most 0.019.
Values may be sent and summed in bfloat16 or wider, within the bound.
A program may use at most 320 MiB of HBM per device.

```python
import math
import jax
import jax.numpy as jnp
import numpy as np
from jax import lax

D = 1024
HEADS = 8
HD = 128
FF = 4096
LAYERS = 2
DOCS = 4
LOCAL_LEN = 256
ROW_LEN = 1024
ROWS = 8
N_SP = 4


def level_of(stream_key, shape, split, least, largest):
    factor_of = 1.0
    for dim, blocks in split:
        draws = jax.random.uniform(jax.random.fold_in(jax.random.fold_in(stream_key, 6), dim), (blocks,), jnp.float32, least / len(split), largest / len(split))
        factor_of = factor_of * jnp.repeat(jnp.exp(draws), shape[dim] // blocks).reshape((-1,) + (1,) * (len(shape) - 1 - dim))
    return factor_of


def length_profile(amount, total, bound, slope):
    weights = [(1 << 20) // math.isqrt(grade ** slope) + 1 for grade in range(2, amount + 1)]
    surplus, given = total - bound - (amount - 1), [1] * (amount - 1)
    while surplus > 0:
        candidates = [i for i in range(amount - 1) if given[i] < bound]
        mass, left = sum([weights[i] for i in candidates]), surplus
        for i in candidates:
            more = min(bound - given[i], max(1, left * weights[i] // mass), surplus)
            given[i] = given[i] + more
            surplus = surplus - more
    return np.array([bound] + given)


def uneven_parts(key, amount, total, reach, slope):
    if amount == 2:
        one = jax.random.randint(key, (), max(1, total - reach), min(reach, total - 1) + 1)
        return jnp.stack([one, total - one])
    tallies = jnp.asarray(length_profile(amount, total, reach, slope), jnp.int32)
    twos = (amount - 1) // 2
    source_of, receiver = tallies[1:1 + 2 * twos:2], tallies[2:2 + 2 * twos:2]
    room = jnp.minimum(source_of - 1, reach - receiver)
    moved = jax.random.randint(jax.random.fold_in(key, 1), (twos,), 0, 1 << 20) % (room + 1)
    tallies = tallies.at[1:1 + 2 * twos:2].set(source_of - moved).at[2:2 + 2 * twos:2].set(receiver + moved)
    return tallies[jax.random.permutation(jax.random.fold_in(key, 2), amount)]


def scatter_about(rng, shape, scale, bound, split=(), kind=jnp.bfloat16):
    array = scale * jax.random.normal(rng, shape, jnp.float32)
    if split:
        array = array * level_of(rng, shape, split, -0.22, 0.18)
    return jnp.clip(array, -bound, bound).astype(kind)


def setup_inputs(seed: int = 0) -> dict:
    key_of = jax.random.split(jax.random.key(seed), 10)
    tokens = scatter_about(key_of[0], (ROWS, ROW_LEN, D), 1.0, 6.0, ((0, 8), (1, 4)))
    cotangent = scatter_about(key_of[1], (ROWS, ROW_LEN, D), 1.0, 6.0, ((0, 8), (1, 4)))
    w_qkv = scatter_about(key_of[2], (LAYERS, 3, D, D), D ** -0.5, 0.1875, ((2, 32),))
    w_out = scatter_about(key_of[3], (LAYERS, D, D), (D // 16) ** -0.5, 0.75, ((1, 32),))
    w_up = scatter_about(key_of[4], (LAYERS, D, FF), D ** -0.5, 0.1875, ((1, 32),))
    w_down = scatter_about(key_of[5], (LAYERS, FF, D), (FF // 2) ** -0.5, 0.125, ((1, 32),))
    gains = jnp.clip(1.0 + 0.1 * jax.random.normal(key_of[6], (LAYERS, 2, D), jnp.float32), 0.5, 1.5).astype(jnp.bfloat16)
    piece_order = jax.vmap(lambda own: jax.random.permutation(own, N_SP))(jax.random.split(key_of[7], ROWS)).reshape((ROWS, N_SP)).astype(jnp.int32)
    doc_lengths = jax.vmap(lambda own: uneven_parts(own, DOCS, ROW_LEN, ROW_LEN // 2, 2))(jax.random.split(key_of[8], ROWS)).reshape((ROWS, DOCS)).astype(jnp.int32)
    return dict(tokens=tokens, cotangent=cotangent, w_qkv=w_qkv, w_out=w_out, w_up=w_up, w_down=w_down, gains=gains, piece_order=piece_order, doc_lengths=doc_lengths)


EPS = 1e-05
MASKED = -1e+30

@jax.custom_vjp
def low(v):
    return lax.optimization_barrier(v.astype(jnp.bfloat16)).astype(jnp.float32)

@jax.custom_vjp
def low_back(v):
    return v

def low_keep(v):
    return (low(v), None)

def low_pass(kept, grad):
    return (grad,)

def back_keep(v):
    return (v, None)

def back_low(kept, grad):
    return (low(grad),)
low.defvjp(low_keep, low_pass)
low_back.defvjp(back_keep, back_low)

def normed(stream, gain):
    center = stream - lax.optimization_barrier(jnp.mean(stream, axis=-1, keepdims=True))
    spread = lax.optimization_barrier(jnp.mean(center * center, axis=-1, keepdims=True))
    return center * lax.rsqrt(spread + EPS) * gain

def matmul(left, right):
    return jnp.dot(left, right, precision=lax.Precision.HIGHEST, preferred_element_type=jnp.float32)

def head_slopes():
    head_ids = jnp.arange(HEADS, dtype=jnp.int32).astype(jnp.float32)
    return jnp.exp2(jnp.float32(-8.0) * (head_ids + jnp.float32(1.0)) / jnp.float32(HEADS))

def attention(query, keys, values, positions, documents, slopes):
    length = query.shape[0]
    block = min(512, length)
    count = length // block

    def one_block(block_query, block_pos, block_doc):
        product = jnp.einsum('qhe,khe->hqk', block_query, keys, precision=lax.Precision.HIGHEST)
        distance = (block_pos[:, None] - positions[None, :]).astype(jnp.float32)
        scores = low_back(product * HD ** (-0.5) + -slopes[:, None, None] * distance[None])
        allowed = (positions[None, :] <= block_pos[:, None]) & (documents[None, :] == block_doc[:, None])
        masked = jnp.where(allowed[None], scores, jnp.full_like(scores, MASKED))
        top_score = lax.optimization_barrier(jnp.max(masked, axis=-1, keepdims=True))
        expo = jnp.where(allowed[None], jnp.exp(masked - top_score), jnp.zeros_like(scores))
        probs = low(expo / lax.optimization_barrier(jnp.sum(expo, axis=-1, keepdims=True)))
        return jnp.einsum('hqk,khe->qhe', probs, values, precision=lax.Precision.HIGHEST)
    checked = jax.checkpoint(one_block)
    blocks = lax.map(lambda parts: checked(parts[0], parts[1], parts[2]), (query.reshape(count, block, HEADS, HD), positions.reshape(count, block).astype(jnp.int32), documents.reshape(count, block).astype(jnp.int32)))
    return blocks.reshape(length, HEADS * HD)

def layer(stream, weights, positions, documents, slopes):
    w_qkv, w_out, w_up, w_down, gains = weights
    length = stream.shape[0]
    normed_in = low(normed(stream, gains[0]))
    query = low_back(low(matmul(normed_in, w_qkv[0])))
    keys = low_back(low(matmul(normed_in, w_qkv[1])))
    values = low_back(low(matmul(normed_in, w_qkv[2])))
    attended = attention(query.reshape(length, HEADS, HD), keys.reshape(length, HEADS, HD), values.reshape(length, HEADS, HD), positions, documents, slopes)
    attended = low_back(low(attended))
    mid = stream + low_back(matmul(attended, w_out))
    normed_mid = low(normed(mid, gains[1]))
    hidden = low(jax.nn.gelu(low_back(matmul(normed_mid, w_up)), approximate=False))
    return mid + low_back(matmul(hidden, w_down))

def reference(tokens, cotangent, w_qkv, w_out, w_up, w_down, gains, piece_order, doc_lengths):
    weights = tuple((w.astype(jnp.float32) for w in (w_qkv, w_out, w_up, w_down, gains)))
    slopes = head_slopes()

    def row_step(totals, row_data):
        row_tokens, row_cot, row_order, row_lengths = row_data
        offsets = jnp.arange(LOCAL_LEN, dtype=jnp.int32)
        positions = (row_order.astype(jnp.int32)[:, None] * jnp.int32(LOCAL_LEN) + offsets[None, :]).reshape(ROW_LEN).astype(jnp.int32)
        bounds = jnp.cumsum(row_lengths.astype(jnp.int32), dtype=jnp.int32).astype(jnp.int32)
        documents = lax.optimization_barrier(jnp.sum((positions[:, None] >= bounds[None, :]).astype(jnp.int32), axis=1, dtype=jnp.int32)).astype(jnp.int32)

        def forward(stream, params):
            for layer_id in range(LAYERS):
                stream = layer(stream, [p[layer_id] for p in params], positions, documents, slopes)
            return stream
        result, pull = jax.vjp(forward, row_tokens.astype(jnp.float32), weights)
        d_tokens, d_weights = pull(row_cot.astype(jnp.float32))
        totals = tuple((left + right for left, right in zip(totals, d_weights)))
        return (totals, (result.astype(jnp.bfloat16), d_tokens))
    zeros = tuple((jnp.zeros(w.shape, jnp.float32) for w in weights))
    totals, (results, d_inputs) = lax.scan(row_step, zeros, (tokens, cotangent, piece_order, doc_lengths))
    return (results, d_inputs, totals[0], totals[1], totals[2], totals[3], totals[4])
```

```python
import functools

import jax
import jax.numpy as jnp
from jax import lax
from jax.experimental import pallas as pl
from jax.experimental.pallas import tpu as pltpu
from jax.sharding import PartitionSpec as P

HEADS = 8
HD = 128
EPS = 1e-05
MASKED = -1e30
MESH = pl.DeviceIdType.MESH
BF = jnp.bfloat16
F32 = jnp.float32
QKV, OUT, UP, DOWN = range(4)


def nn(a, b):
    return lax.dot_general(a, b, (((1,), (0,)), ((), ())), preferred_element_type=F32)


def nt(a, b):
    return lax.dot_general(a, b, (((1,), (1,)), ((), ())), preferred_element_type=F32)


def tn(a, b):
    return lax.dot_general(a, b, (((0,), (0,)), ((), ())), preferred_element_type=F32)


class Dims:
    def __init__(self, dp_n, sp_n, layers, tok, width, ff, docs):
        self.dp_n, self.sp_n, self.layers, self.tok, self.width = dp_n, sp_n, layers, tok, width
        self.z_n = 4 if dp_n % 4 == 0 else 1
        self.y_n = dp_n // self.z_n
        self.x_n = sp_n // 2
        self.rows = width // (dp_n * sp_n)
        self.heads = HEADS // sp_n
        self.dh = width // sp_n
        self.hid = ff // sp_n
        self.hid_own = ff // (dp_n * sp_n)
        self.docs = docs
        self.chunk = min(256, tok)
        self.n_width = width // self.chunk
        self.n_hid = self.hid // self.chunk
        self.back = self.x_n
        self.pairs = [(i, b) for i in range(sp_n) for b in range(max(0, i - self.back), i + 1)]

    def block_shape(self, which):
        return {
            QKV: (self.sp_n, self.rows, 3 * self.dh),
            OUT: (self.rows, self.width),
            UP: (self.sp_n, self.rows, self.hid),
            DOWN: (self.hid_own, self.width),
        }[which]


class Place:
    def __init__(self, d):
        self.d = d
        self.r = lax.axis_index("dp")
        self.s = lax.axis_index("sp")
        self.z, self.y = self.r // d.y_n, self.r % d.y_n
        self.x, self.c = self.s // 2, self.s % 2
        self.partner = self.x * 2 + (self.c + 1) % 2

    def slot(self, step):
        return ((self.x + step // 2) % self.d.x_n) * 2 + (self.c + step % 2) % 2

    def zpeer(self, dz):
        return (self.z + dz) % self.d.z_n

    def ypeer(self, dy):
        return (self.y + dy) % self.d.y_n

    def dev(self, z, y):
        return (z * self.d.y_n + y, self.s)

    def moved(self):
        d = self.d
        flat = self.r * d.sp_n + self.s
        goal = (flat % d.dp_n, flat // d.dp_n)
        mine = self.s * d.dp_n + self.r
        source = (mine // d.sp_n, mine % d.sp_n)
        stays = flat == mine
        return goal, source, stays

    def barrier(self):
        d = self.d
        sem = pltpu.get_barrier_semaphore()
        peers = [(self.r, self.slot(t)) for t in range(1, d.sp_n)]
        peers += [self.dev(self.zpeer(k), self.y) for k in range(1, d.z_n)]
        peers += [self.dev(self.z, self.ypeer(k)) for k in range(1, d.y_n)]
        for peer in peers:
            pl.semaphore_signal(sem, inc=1, device_id=peer, device_id_type=MESH)
        goal, source, stays = self.moved()

        @pl.when(jnp.logical_not(stays))
        def _():
            pl.semaphore_signal(sem, inc=1, device_id=goal, device_id_type=MESH)
            pl.semaphore_signal(sem, inc=1, device_id=source, device_id_type=MESH)
            pl.semaphore_wait(sem, len(peers) + 2)

        @pl.when(stays)
        def _():
            pl.semaphore_wait(sem, len(peers))


def rcopy(src, dst, send, recv, device):
    return pltpu.make_async_remote_copy(
        src_ref=src, dst_ref=dst, send_sem=send, recv_sem=recv, device_id=device, device_id_type=MESH
    )


class Gather:
    def __init__(self, p, send, recv):
        self.p, self.send, self.recv = p, send, recv

    def copy(self, buf, slot, way, device_slot):
        p = self.p
        return rcopy(
            buf.at[slot], buf.at[slot], self.send.at[way, device_slot], self.recv.at[slot], (p.r, device_slot)
        )

    def start(self, buf):
        p = self.p
        for dx in range(1, p.d.x_n):
            self.copy(buf, p.s, 0, p.slot(2 * dx)).start()
        self.copy(buf, p.s, 0, p.partner).start()

    def forward(self, buf, slot):
        p = self.p
        return rcopy(
            buf.at[slot], buf.at[slot], self.send.at[1, slot], self.recv.at[slot], (p.r, p.partner)
        )

    def take(self, buf, step):
        p = self.p
        slot = p.slot(step)

        @pl.when(step > 0)
        def _():
            rcopy(
                buf.at[slot], buf.at[slot], self.send.at[0, slot], self.recv.at[slot], (p.r, p.partner)
            ).wait_recv()

        @pl.when((step > 0) & (step % 2 == 0))
        def _():
            self.forward(buf, slot).start()

        return slot

    def end(self, buf):
        p = self.p
        for dx in range(1, p.d.x_n):
            self.copy(buf, p.s, 0, p.slot(2 * dx)).wait_send()
            self.forward(buf, p.slot(2 * dx)).wait_send()
        self.copy(buf, p.s, 0, p.partner).wait_send()


class Scatter:
    def __init__(self, p, part, near, far, near_send, near_recv, far_send, far_recv):
        self.p, self.part, self.near, self.far = p, part, near, far
        self.near_send, self.near_recv, self.far_send, self.far_recv = near_send, near_recv, far_send, far_recv

    def near_copy(self, x):
        p = self.p
        return rcopy(
            self.part.at[x * 2 + (p.c + 1) % 2],
            self.near.at[x],
            self.near_send.at[x],
            self.near_recv.at[x],
            (p.r, p.partner),
        )

    def far_copy(self, x, source):
        p = self.p
        return rcopy(
            self.part.at[x * 2 + p.c], self.far.at[source], self.far_send.at[x], self.far_recv.at[source], (p.r, x * 2 + p.c)
        )

    def put(self, step):
        p = self.p

        @pl.when(step % 2 == 1)
        def _():
            self.near_copy(p.slot(step) // 2).start()

    def cross(self):
        p = self.p
        for dx in range(1, p.d.x_n):
            x = (p.x + dx) % p.d.x_n
            self.near_copy(x).wait_recv()
            slot = x * 2 + p.c

            @pl.loop(0, p.d.tok // 64)
            def _(i):
                rows = pl.ds(pl.multiple_of(i * 64, 64), 64)
                both = self.part[slot, rows].astype(F32) + self.near[x, rows].astype(F32)
                self.part[slot, rows] = both.astype(BF)

            self.far_copy(x, p.x).start()

    def arrive(self):
        p = self.p
        self.near_copy(p.x).wait_recv()
        for dx in range(1, p.d.x_n):
            x = (p.x + dx) % p.d.x_n
            self.far_copy(x, x).wait_recv()

    def total(self, rows):
        p = self.p
        value = self.part[p.s, rows].astype(F32) + self.near[p.x, rows].astype(F32)
        for dx in range(1, p.d.x_n):
            value = value + self.far[(p.x + dx) % p.d.x_n, rows].astype(F32)
        return value

    def end(self):
        p = self.p
        for dx in range(p.d.x_n):
            x = (p.x + dx) % p.d.x_n
            self.near_copy(x).wait_send()
            if dx:
                self.far_copy(x, p.x).wait_send()


class SmallSum:
    def __init__(self, p, first, sp_in, mid_a, z_in, mid_b, y_in, sp_sem, z_sem, y_sem):
        self.p = p
        self.bufs = ((first, sp_in, sp_sem), (mid_a, z_in, z_sem), (mid_b, y_in, y_sem))

    def plan(self, stage):
        p = self.p
        if stage == 0:
            return p.s, [(p.slot(t), (p.r, p.slot(t))) for t in range(1, p.d.sp_n)]
        if stage == 1:
            return p.z, [(p.zpeer(k), p.dev(p.zpeer(k), p.y)) for k in range(1, p.d.z_n)]
        return p.y, [(p.ypeer(k), p.dev(p.z, p.ypeer(k))) for k in range(1, p.d.y_n)]

    def start(self, stage):
        src, dst, sem = self.bufs[stage]
        own, peers = self.plan(stage)
        for index, device in peers:
            rcopy(src, dst.at[own], sem.at[0, index], sem.at[1, own], device).start()

    def finish(self, stage, result):
        src, dst, sem = self.bufs[stage]
        own, peers = self.plan(stage)
        value = src[...]
        for index, device in peers:
            rcopy(src, dst.at[index], sem.at[0, index], sem.at[1, index], device).wait_recv()
            value = value + dst[index]
        result[...] = value
        for index, device in peers:
            rcopy(src, dst.at[own], sem.at[0, index], sem.at[1, own], device).wait_send()


def small_scratch(d):
    return [
        ("sp_in", pltpu.VMEM((d.sp_n, 8, d.width), F32)),
        ("mid_a", pltpu.VMEM((8, d.width), F32)),
        ("z_in", pltpu.VMEM((d.z_n, 8, d.width), F32)),
        ("mid_b", pltpu.VMEM((8, d.width), F32)),
        ("y_in", pltpu.VMEM((d.y_n, 8, d.width), F32)),
        ("sp_sem", pltpu.SemaphoreType.DMA((2, d.sp_n))),
        ("z_sem", pltpu.SemaphoreType.DMA((2, d.z_n))),
        ("y_sem", pltpu.SemaphoreType.DMA((2, d.y_n))),
    ]


def comm_scratch(d):
    return [
        ("part", pltpu.VMEM((d.sp_n, d.tok, d.width), BF)),
        ("near", pltpu.VMEM((d.x_n, d.tok, d.width), BF)),
        ("far", pltpu.VMEM((d.x_n, d.tok, d.width), BF)),
        ("ag_send", pltpu.SemaphoreType.DMA((2, d.sp_n))),
        ("ag_recv", pltpu.SemaphoreType.DMA((d.sp_n,))),
        ("near_send", pltpu.SemaphoreType.DMA((d.x_n,))),
        ("near_recv", pltpu.SemaphoreType.DMA((d.x_n,))),
        ("far_send", pltpu.SemaphoreType.DMA((d.x_n,))),
        ("far_recv", pltpu.SemaphoreType.DMA((d.x_n,))),
    ]


SAVED = ("xin", "qkv", "att", "probs", "xmid", "hid", "slope", "stream", "mid")
ONCE = ("qkv", "att", "probs", "hid", "slope")
WEIGHTS = ("wqkv", "wout", "wup", "wdown")


def saved_shapes(d):
    full = (d.sp_n, d.tok, d.width)
    return {
        "xin": (full, BF),
        "qkv": ((d.sp_n, d.tok, 3 * d.dh), BF),
        "att": ((d.sp_n, d.tok, d.dh), BF),
        "probs": ((d.heads, len(d.pairs), d.tok, d.tok), BF),
        "xmid": (full, BF),
        "hid": ((d.sp_n, d.tok, d.hid), BF),
        "slope": ((d.sp_n, d.tok, d.hid), BF),
        "stream": ((d.tok, d.width), F32),
        "mid": ((d.tok, d.width), F32),
    }


def weight_shapes(d):
    return {name: ((d.z_n, d.y_n) + d.block_shape(i), BF) for i, name in enumerate(WEIGHTS)}


class Fetch:
    def __init__(self, p, o):
        self.p, self.o = p, o
        self.full = (o.wqkv, o.wout, o.wup, o.wdown)

    def spread(self, l, w):
        p, o = self.p, self.o
        own = self.full[w].at[l, p.z, p.y]
        if w in (QKV, UP):
            src = o.in_qkv if w == QKV else o.in_up
            for t in range(1, p.d.sp_n):
                j = p.slot(t)
                rcopy(src.at[l, j], own.at[p.s], o.s_send.at[l, w, j], o.s_recv.at[l, w, p.s], (p.r, j)).start()
            pltpu.make_async_copy(src.at[l, p.s], own.at[p.s], o.own_sem.at[l, w]).start()
        elif w == DOWN:
            pltpu.make_async_copy(o.in_down.at[l], own, o.own_sem.at[l, w]).start()
        else:
            goal, _, stays = p.moved()

            @pl.when(stays)
            def _():
                pltpu.make_async_copy(o.in_out.at[l], own, o.own_sem.at[l, w]).start()

            @pl.when(jnp.logical_not(stays))
            def _():
                there = self.full[w].at[l, goal[0] // p.d.y_n, goal[0] % p.d.y_n]
                rcopy(o.in_out.at[l], there, o.s_send.at[l, w, 0], o.s_recv.at[l, w, 0], goal).start()

    def lines(self, l, w):
        p, o = self.p, self.o
        own = self.full[w].at[l, p.z, p.y]
        if w in (QKV, UP):
            src = o.in_qkv if w == QKV else o.in_up
            pltpu.make_async_copy(src.at[l, p.s], own.at[p.s], o.own_sem.at[l, w]).wait()
            for t in range(1, p.d.sp_n):
                j = p.slot(t)
                rcopy(src.at[l, j], own.at[j], o.s_send.at[l, w, j], o.s_recv.at[l, w, j], (p.r, j)).wait_recv()
        elif w == DOWN:
            pltpu.make_async_copy(o.in_down.at[l], own, o.own_sem.at[l, w]).wait()
        else:
            goal, _, stays = p.moved()

            @pl.when(stays)
            def _():
                pltpu.make_async_copy(o.in_out.at[l], own, o.own_sem.at[l, w]).wait()

            @pl.when(jnp.logical_not(stays))
            def _():
                rcopy(o.in_out.at[l], own, o.s_send.at[l, w, 0], o.s_recv.at[l, w, 0], goal).wait_recv()

        for k in range(1, p.d.z_n):
            self.z_copy(l, w, p.z, k).start()
        for k in range(1, p.d.y_n):
            self.y_copy(l, w, p.z, p.y, k).start()

    def z_copy(self, l, w, z, k):
        p, o = self.p, self.o
        block = self.full[w].at[l, z, p.y]
        there = p.zpeer(k)
        return rcopy(block, block, o.z_send.at[l, w, there], o.z_recv.at[l, w, z], p.dev(there, p.y))

    def y_copy(self, l, w, z, y, k):
        p, o = self.p, self.o
        block = self.full[w].at[l, z, y]
        there = p.ypeer(k)
        return rcopy(block, block, o.y_send.at[l, w, z, there], o.y_recv.at[l, w, z, y], p.dev(p.z, there))

    def onward(self, l, w):
        p = self.p
        for k in range(1, p.d.z_n):
            z = p.zpeer(k)
            self.z_copy(l, w, z, k).wait_recv()
            for m in range(1, p.d.y_n):
                self.y_copy(l, w, z, p.y, m).start()

    def ready(self, l, w):
        p, o = self.p, self.o
        for m in range(1, p.d.y_n):
            for k in range(p.d.z_n):
                self.y_copy(l, w, p.zpeer(k), p.ypeer(m), m).wait_recv()
        pltpu.make_async_copy(self.full[w].at[l], o.w_save[w].at[l], o.w_sem.at[l, w]).start()

    def end(self):
        p, o = self.p, self.o
        for l in range(p.d.layers):
            for w in range(4):
                own = self.full[w].at[l, p.z, p.y]
                if w in (QKV, UP):
                    src = o.in_qkv if w == QKV else o.in_up
                    for t in range(1, p.d.sp_n):
                        j = p.slot(t)
                        rcopy(src.at[l, j], own.at[p.s], o.s_send.at[l, w, j], o.s_recv.at[l, w, p.s], (p.r, j)).wait_send()
                elif w == OUT:
                    goal, _, stays = p.moved()

                    @pl.when(jnp.logical_not(stays))
                    def _():
                        rcopy(o.in_out.at[l], own, o.s_send.at[l, w, 0], o.s_recv.at[l, w, 0], goal).wait_send()

                for k in range(1, p.d.z_n):
                    self.z_copy(l, w, p.z, k).wait_send()
                for k in range(p.d.z_n):
                    for m in range(1, p.d.y_n):
                        self.y_copy(l, w, p.zpeer(k), p.y, m).wait_send()
                pltpu.make_async_copy(self.full[w].at[l], o.w_save[w].at[l], o.w_sem.at[l, w]).wait()


class Refs:
    pass


def mean_of(v):
    return jnp.mean(v, axis=-1, keepdims=True)


def norm_rows(v, gain):
    center = v - mean_of(v)
    return center * lax.rsqrt(mean_of(center * center) + EPS) * gain


def row_loop(tok, body, step=32):
    @pl.loop(0, tok // step)
    def _(i):
        body(pl.ds(pl.multiple_of(i * step, step), step))


def attention_forward(d, o, l):
    tok = d.tok
    for i in range(d.sp_n):
        here = o.meta[0, i]
        pos = i * tok + lax.broadcasted_iota(jnp.int32, (tok, 1), 0)
        start = jnp.zeros((tok, 1), jnp.int32)
        for b in range(1, d.docs):
            start = jnp.where(pos >= o.meta[2, b], o.meta[2, b], start)
        blocks = range(max(0, i - d.back), i + 1)
        for h in range(d.heads):
            lanes = slice(h * HD, (h + 1) * HD)
            query = o.qkv[0, here, :, lanes]
            scores = []
            for b in blocks:
                keys = o.qkv[0, o.meta[0, b], :, d.dh + h * HD : d.dh + (h + 1) * HD]
                key_pos = b * tok + lax.broadcasted_iota(jnp.int32, (tok, tok), 1)
                query_pos = i * tok + lax.broadcasted_iota(jnp.int32, (tok, tok), 0)
                score = nt(query, keys) * HD ** (-0.5) + o.head_slope[h] * (key_pos - query_pos).astype(F32)
                allowed = key_pos >= start
                if b == i:
                    allowed = allowed & (key_pos <= query_pos)
                scores.append(jnp.where(allowed, score, MASKED))
            top = scores[0].max(axis=-1, keepdims=True)
            for score in scores[1:]:
                top = jnp.maximum(top, score.max(axis=-1, keepdims=True))
            expo = [jnp.exp(score - top) for score in scores]
            total = expo[0].sum(axis=-1, keepdims=True)
            for part in expo[1:]:
                total = total + part.sum(axis=-1, keepdims=True)
            inverse = 1.0 / total
            result = None
            for b, part in zip(blocks, expo):
                low = (part * inverse).astype(BF)
                o.probs[0, h, d.pairs.index((i, b))] = low
                values = o.qkv[0, o.meta[0, b], :, 2 * d.dh + h * HD : 2 * d.dh + (h + 1) * HD]
                term = nn(low, values)
                result = term if result is None else result + term
            o.sorted_att[i, :, lanes] = result.astype(BF)


def fwd_kernel(d, names, *refs):
    o = Refs()
    for name, ref in zip(names, refs):
        setattr(o, name, ref)
    o.w_save = (o.o_wqkv, o.o_wout, o.o_wup, o.o_wdown)
    p = Place(d)
    p.barrier()
    fetch = Fetch(p, o)
    gather = Gather(p, o.ag_send, o.ag_recv)
    scatter = Scatter(p, o.part, o.near, o.far, o.near_send, o.near_recv, o.far_send, o.far_recv)
    small = SmallSum(p, o.in_gains, o.sp_in, o.mid_a, o.z_in, o.mid_b, o.y_in, o.sp_sem, o.z_sem, o.y_sem)

    def save(name, l):
        ref, out = getattr(o, name), getattr(o, "o_" + name)
        held = 0 if name in ONCE else l
        return pltpu.make_async_copy(ref.at[held], out.at[l], o.save_sem.at[l, SAVED.index(name)])

    def free(l, *names):
        if l > 0:
            for name in names:
                save(name, l - 1).wait()

    small.start(0)
    for w in range(4):
        fetch.spread(0, w)
    fetch.lines(0, QKV)
    small.finish(0, o.mid_a)
    small.start(1)
    fetch.lines(0, OUT)
    fetch.lines(0, UP)
    fetch.lines(0, DOWN)
    small.finish(1, o.mid_b)
    small.start(2)
    small.finish(2, o.o_gains)

    for l in range(d.layers):
        gain_in = o.o_gains[2 * l : 2 * l + 1, :]
        gain_mid = o.o_gains[2 * l + 1 : 2 * l + 2, :]

        if l == 0:

            def first(rows):
                v = o.in_tokens[rows, :].astype(F32)
                o.stream[0, rows] = v
                o.xin[0, p.s, rows] = norm_rows(v, gain_in).astype(BF)

            row_loop(d.tok, first)
        xin = o.xin.at[l]
        gather.start(xin)
        save("stream", l).start()
        if l == 0:
            fetch.onward(0, QKV)
            for later in range(1, d.layers):
                for w in range(4):
                    fetch.spread(later, w)
        else:
            fetch.onward(l, UP)
        fetch.ready(l, QKV)
        free(l, "qkv")

        @pl.loop(0, d.sp_n)
        def _(t):
            slot = gather.take(xin, t)
            block = xin[slot]
            for n in range(3 * d.dh // d.chunk if d.dh % d.chunk == 0 else 3):
                size = 3 * d.dh // (3 * d.dh // d.chunk if d.dh % d.chunk == 0 else 3)
                cols = slice(n * size, (n + 1) * size)
                weight = o.wqkv[l, :, :, :, :, cols].reshape(d.width, size)
                o.qkv[0, slot, :, cols] = nn(block, weight).astype(BF)

        gather.end(xin)
        save("xin", l).start()
        save("qkv", l).start()
        if l == 0:
            fetch.onward(0, OUT)
        free(l, "probs", "att")
        attention_forward(d, o, l)
        save("probs", l).start()
        fetch.onward(l, UP if l == 0 else DOWN)
        fetch.ready(l, OUT)

        @pl.loop(0, d.sp_n)
        def _(t):
            slot = p.slot(t)
            block = o.sorted_att[o.meta[1, slot]]
            o.att[0, slot] = block
            for n in range(d.n_width):
                cols = slice(n * d.chunk, (n + 1) * d.chunk)
                weight = o.wout[l, :, :, :, cols].reshape(d.dh, d.chunk)
                o.part[slot, :, cols] = nn(block, weight).astype(BF)
            scatter.put(t)

        save("att", l).start()
        scatter.cross()
        if l + 1 < d.layers:
            for w in range(4):
                fetch.lines(l + 1, w)
        scatter.arrive()
        xmid = o.xmid.at[l]

        def middle(rows):
            v = o.stream[l, rows] + scatter.total(rows)
            o.mid[l, rows] = v
            xmid[p.s, rows] = norm_rows(v, gain_mid).astype(BF)

        row_loop(d.tok, middle)
        scatter.end()
        gather.start(xmid)
        save("mid", l).start()
        if l == 0:
            fetch.onward(0, DOWN)
        fetch.ready(l, UP)
        fetch.ready(l, DOWN)
        free(l, "hid", "slope")

        @pl.loop(0, d.sp_n)
        def _(t):
            slot = gather.take(xmid, t)
            block = xmid[slot]
            for n in range(d.n_hid):
                cols = slice(n * d.chunk, (n + 1) * d.chunk)
                weight = o.wup[l, :, :, :, :, cols].reshape(d.width, d.chunk)
                pre = nn(block, weight)
                phi = 0.5 * (1.0 + lax.erf(pre * (0.5**0.5)))
                o.hid[0, slot, :, cols] = (pre * phi).astype(BF)
                density = jnp.exp(-0.5 * pre * pre) * 0.3989422804014327
                o.slope[0, slot, :, cols] = (phi + pre * density).astype(BF)
            hidden = o.hid[0, slot]
            for n in range(d.n_width):
                cols = slice(n * d.chunk, (n + 1) * d.chunk)
                weight = o.wdown[l, :, :, :, cols].reshape(d.hid, d.chunk)
                o.part[slot, :, cols] = nn(hidden, weight).astype(BF)
            scatter.put(t)

        gather.end(xmid)
        save("xmid", l).start()
        save("hid", l).start()
        save("slope", l).start()
        scatter.cross()
        if l + 1 < d.layers:
            fetch.onward(l + 1, QKV)
            fetch.onward(l + 1, OUT)
        scatter.arrive()
        if l + 1 < d.layers:
            gain_next = o.o_gains[2 * l + 2 : 2 * l + 3, :]

            def last(rows):
                v = o.mid[l, rows] + scatter.total(rows)
                o.stream[l + 1, rows] = v
                o.xin[l + 1, p.s, rows] = norm_rows(v, gain_next).astype(BF)

        else:

            def last(rows):
                o.o_output[rows, :] = (o.mid[l, rows] + scatter.total(rows)).astype(BF)

        row_loop(d.tok, last)
        scatter.end()

    fetch.end()
    for l in range(d.layers):
        for name in SAVED:
            if l == d.layers - 1 or name not in ONCE:
                save(name, l).wait()


class Reduce:
    def __init__(self, p, o):
        self.p, self.o = p, o
        self.grad = (o.g_qkv, o.g_out, o.g_up, o.g_down)
        self.y_in = (o.y_qkv, o.y_out, o.y_up, o.y_down)
        self.z_in = (o.z_qkv, o.z_out, o.z_up, o.z_down)
        self.sp_in = (o.x_qkv, o.x_out, o.x_up, None)
        self.result = (o.o_qkv, o.o_out, o.o_up, o.o_down)

    def y_copy(self, l, w, k):
        p, o = self.p, self.o
        index = p.d.y_n - k - 1
        there = p.ypeer(k)
        return rcopy(
            self.grad[w].at[:, there], self.y_in[w].at[l, index], o.ry_send.at[l, w, k], o.ry_recv.at[l, w, index], p.dev(p.z, there)
        )

    def z_copy(self, l, w, k):
        p, o = self.p, self.o
        index = p.d.z_n - k - 1
        there = p.zpeer(k)
        return rcopy(
            self.grad[w].at[there, p.y], self.z_in[w].at[l, index], o.rz_send.at[l, w, k], o.rz_recv.at[l, w, index], p.dev(there, p.y)
        )

    def begin(self, l, w):
        for k in range(1, self.p.d.y_n):
            self.y_copy(l, w, k).start()

    def add_rows(self, w, body):
        shape = self.p.d.block_shape(w)
        if len(shape) == 3:
            for j in range(shape[0]):
                body((j,))
        else:
            rows = 32 if shape[0] % 32 == 0 else shape[0]
            for j in range(shape[0] // rows):
                body((slice(j * rows, (j + 1) * rows),))

    def across(self, l, w):
        p = self.p
        for k in range(1, p.d.y_n):
            self.y_copy(l, w, p.d.y_n - k).wait_recv()
        for k in range(1, p.d.z_n):
            z = p.zpeer(k)

            def add(index):
                value = self.grad[w][(z, p.y) + index].astype(F32)
                for m in range(p.d.y_n - 1):
                    value = value + self.y_in[w][(l, m, z) + index].astype(F32)
                self.grad[w][(z, p.y) + index] = value.astype(BF)

            self.add_rows(w, add)
            self.z_copy(l, w, k).start()

    def s_copy(self, l, w, j, source):
        p, o = self.p, self.o
        return rcopy(
            self.grad[w].at[p.z, p.y, j], self.sp_in[w].at[l, source], o.rs_send.at[l, w, j], o.rs_recv.at[l, w, source], (p.r, j)
        )

    def settle(self, l, w):
        p, o = self.p, self.o
        for k in range(1, p.d.z_n):
            self.z_copy(l, w, p.d.z_n - k).wait_recv()

        def add(index):
            value = self.grad[w][(p.z, p.y) + index].astype(F32)
            for m in range(p.d.y_n - 1):
                value = value + self.y_in[w][(l, m, p.z) + index].astype(F32)
            for m in range(p.d.z_n - 1):
                value = value + self.z_in[w][(l, m) + index].astype(F32)
            if w == DOWN:
                self.result[w][(l,) + index] = value
            else:
                self.grad[w][(p.z, p.y) + index] = value.astype(BF)

        self.add_rows(w, add)
        if w in (QKV, UP):
            for t in range(1, p.d.sp_n):
                self.s_copy(l, w, p.slot(t), p.s).start()
            self.result[w][l, p.s] = self.grad[w][p.z, p.y, p.s].astype(F32)
        elif w == OUT:
            _, source, stays = p.moved()

            @pl.when(stays)
            def _():
                self.result[w][l] = self.grad[w][p.z, p.y].astype(F32)

            @pl.when(jnp.logical_not(stays))
            def _():
                self.out_copy(l, source).start()

    def out_copy(self, l, device):
        p, o = self.p, self.o
        return rcopy(
            self.grad[OUT].at[p.z, p.y], self.sp_in[OUT].at[l], o.rs_send.at[l, OUT, 0], o.rs_recv.at[l, OUT, 0], device
        )

    def sent(self, l, w):
        p = self.p
        for k in range(1, p.d.y_n):
            self.y_copy(l, w, k).wait_send()
        for k in range(1, p.d.z_n):
            self.z_copy(l, w, k).wait_send()
        if w in (QKV, UP):
            for t in range(1, p.d.sp_n):
                self.s_copy(l, w, p.slot(t), p.s).wait_send()
        elif w == OUT:
            _, source, stays = p.moved()

            @pl.when(jnp.logical_not(stays))
            def _():
                self.out_copy(l, source).wait_send()

    def last(self, l, w):
        p = self.p
        if w in (QKV, UP):
            for t in range(1, p.d.sp_n):
                j = p.slot(t)
                self.s_copy(l, w, j, j).wait_recv()
                self.result[w][l, j] = self.sp_in[w][l, j].astype(F32)
        elif w == OUT:
            _, source, stays = p.moved()

            @pl.when(jnp.logical_not(stays))
            def _():
                self.out_copy(l, source).wait_recv()
                self.result[w][l] = self.sp_in[w][l].astype(F32)


def norm_back(v, d_out, gain):
    center = v - mean_of(v)
    inverse = lax.rsqrt(mean_of(center * center) + EPS)
    unit = center * inverse
    gain_term = jnp.sum(d_out * unit, axis=0, keepdims=True)
    e = d_out * gain
    back = (e - mean_of(e) - unit * mean_of(e * unit)) * inverse
    return back, gain_term


def attention_backward(d, o):
    tok = d.tok
    for i in range(d.sp_n):
        here = o.meta[0, i]
        blocks = range(max(0, i - d.back), i + 1)
        for h in range(d.heads):
            lanes = slice(h * HD, (h + 1) * HD)
            key_lanes = slice(d.dh + h * HD, d.dh + (h + 1) * HD)
            value_lanes = slice(2 * d.dh + h * HD, 2 * d.dh + (h + 1) * HD)
            query = o.qkv[here, :, lanes]
            grad = o.d_att[here, :, lanes]
            d_probs, inner = [], None
            for b in blocks:
                low = o.probs[h, d.pairs.index((i, b))].astype(F32)
                term = nt(grad, o.qkv[o.meta[0, b], :, value_lanes])
                d_probs.append(term)
                weighted = jnp.sum(low * term, axis=-1, keepdims=True)
                inner = weighted if inner is None else inner + weighted
            d_query = None
            for b, term in zip(blocks, d_probs):
                low = o.probs[h, d.pairs.index((i, b))]
                d_score = (low.astype(F32) * (term - inner)).astype(BF)
                step = nn(d_score, o.qkv[o.meta[0, b], :, key_lanes])
                d_query = step if d_query is None else d_query + step
                d_key, d_value = tn(d_score, query), tn(low, grad)
                if b == i:
                    o.d_keys[b, :, lanes] = d_key
                    o.d_values[b, :, lanes] = d_value
                else:
                    o.d_keys[b, :, lanes] += d_key
                    o.d_values[b, :, lanes] += d_value
            o.sorted_dqkv[i, :, lanes] = (d_query * HD ** (-0.5)).astype(BF)
    for b in range(d.sp_n):
        o.sorted_dqkv[b, :, d.dh : 2 * d.dh] = (o.d_keys[b] * HD ** (-0.5)).astype(BF)
        o.sorted_dqkv[b, :, 2 * d.dh :] = o.d_values[b].astype(BF)


def bwd_kernel(d, names, *refs):
    o = Refs()
    for name, ref in zip(names, refs):
        setattr(o, name, ref)
    p = Place(d)
    gather = Gather(p, o.ag_send, o.ag_recv)
    scatter = Scatter(p, o.part, o.near, o.far, o.near_send, o.near_recv, o.far_send, o.far_recv)
    small = SmallSum(p, o.gain_sum, o.sp_in, o.mid_a, o.z_in, o.mid_b, o.y_in, o.sp_sem, o.z_sem, o.y_sem)
    reduce = Reduce(p, o)
    loads = WEIGHTS + SAVED

    def load(name, l):
        return pltpu.make_async_copy(getattr(o, "i_" + name).at[l], getattr(o, name), o.load_sem.at[loads.index(name)])

    def refill(l, *which):
        if l > 0:
            for name in which:
                load(name, l - 1).start()

    top = d.layers - 1
    for name in ("wdown", "slope", "wup", "hid", "xmid", "mid", "wout", "qkv", "probs", "att", "wqkv", "xin", "stream"):
        load(name, top).start()
    p.barrier()
    o.gain_sum[...] = jnp.zeros_like(o.gain_sum)

    def begin(rows):
        v = o.in_cotangent[rows, :].astype(F32)
        o.o_grad[rows, :] = v
        o.gl[p.s, rows] = v.astype(BF)

    row_loop(d.tok, begin)
    gather.start(o.gl)
    tokens = d.sp_n * d.tok
    per_width = d.chunk // (d.sp_n * d.rows)
    per_hid = d.chunk // d.hid_own

    for l in reversed(range(d.layers)):
        gain_in = o.in_gains[2 * l : 2 * l + 1, :]
        gain_mid = o.in_gains[2 * l + 1 : 2 * l + 2, :]

        def hid_rows(n):
            step = per_hid
            first = n * step
            flat = [(k // d.y_n, k % d.y_n) for k in range(first, first + step)]
            return flat

        load("wdown", l).wait()
        load("slope", l).wait()
        load("wup", l).wait()

        @pl.loop(0, d.sp_n)
        def _(t):
            slot = gather.take(o.gl, t)
            block = o.gl[slot]
            wdown = o.wdown
            for n in range(d.n_hid):
                cols = slice(n * d.chunk, (n + 1) * d.chunk)
                zs = slice(n * d.z_n // d.n_hid, (n + 1) * d.z_n // d.n_hid)
                weight = wdown[zs].reshape(d.chunk, d.width)
                d_hidden = nt(block, weight)
                o.slope[slot, :, cols] = (d_hidden * o.slope[slot, :, cols].astype(F32)).astype(BF)
            d_pre = o.slope[slot]
            for n in range(d.n_width):
                cols = slice(n * d.chunk, (n + 1) * d.chunk)
                zs = slice(n * d.z_n // d.n_width, (n + 1) * d.z_n // d.n_width)
                weight = o.wup[zs].reshape(d.chunk, d.hid)
                o.part[slot, :, cols] = nt(d_pre, weight).astype(BF)
            scatter.put(t)

        gather.end(o.gl)
        refill(l, "wdown", "wup")
        scatter.cross()
        load("hid", l).wait()
        if l < top:
            reduce.sent(l + 1, DOWN)
        grad_low = o.gl[...].reshape(tokens, d.width)
        for n in range(d.n_hid):
            left = o.hid[:, :, n * d.chunk : (n + 1) * d.chunk].reshape(tokens, d.chunk)
            zs = slice(n * d.z_n // d.n_hid, (n + 1) * d.z_n // d.n_hid)
            value = tn(left, o.gl[...].reshape(tokens, d.width)).astype(BF)
            o.g_down[zs] = value.reshape((d.z_n // d.n_hid, d.y_n, d.hid_own, d.width))
        reduce.begin(l, DOWN)
        refill(l, "hid")
        load("mid", l).wait()
        scatter.arrive()

        def middle(rows):
            back, gain_term = norm_back(o.mid[rows, :], scatter.total(rows), gain_mid)
            o.gain_sum[2 * l + 1 : 2 * l + 2, :] += gain_term
            value = o.o_grad[rows, :] + back
            o.o_grad[rows, :] = value
            o.ml[p.s, rows] = value.astype(BF)

        row_loop(d.tok, middle)
        scatter.end()
        gather.start(o.ml)
        refill(l, "mid")
        load("xmid", l).wait()
        if l < top:
            reduce.sent(l + 1, UP)
        for n in range(d.n_width):
            left = o.xmid[:, :, n * d.chunk : (n + 1) * d.chunk].reshape(tokens, d.chunk)
            zs = slice(n * d.z_n // d.n_width, (n + 1) * d.z_n // d.n_width)
            value = tn(left, o.slope[...].reshape(tokens, d.hid)).astype(BF)
            o.g_up[zs] = value.reshape((d.z_n // d.n_width, d.y_n, d.sp_n, d.rows, d.hid))
        reduce.begin(l, UP)
        reduce.across(l, DOWN)
        refill(l, "xmid", "slope")
        load("wout", l).wait()

        @pl.loop(0, d.sp_n)
        def _(t):
            slot = gather.take(o.ml, t)
            weight = o.wout[...].reshape(d.dh, d.width)
            o.d_att[slot] = nt(o.ml[slot], weight).astype(BF)

        gather.end(o.ml)
        refill(l, "wout")
        load("qkv", l).wait()
        load("probs", l).wait()
        attention_backward(d, o)
        refill(l, "qkv", "probs")
        reduce.settle(l, DOWN)
        reduce.across(l, UP)
        load("wqkv", l).wait()

        @pl.loop(0, d.sp_n)
        def _(t):
            slot = p.slot(t)
            block = o.sorted_dqkv[o.meta[1, slot]]
            o.d_qkv[slot] = block
            for n in range(d.n_width):
                cols = slice(n * d.chunk, (n + 1) * d.chunk)
                zs = slice(n * d.z_n // d.n_width, (n + 1) * d.z_n // d.n_width)
                weight = o.wqkv[zs].reshape(d.chunk, 3 * d.dh)
                o.part[slot, :, cols] = nt(block, weight).astype(BF)
            scatter.put(t)

        scatter.cross()
        refill(l, "wqkv")
        load("att", l).wait()
        if l < top:
            reduce.sent(l + 1, OUT)
        value = tn(o.att[...].reshape(tokens, d.dh), o.ml[...].reshape(tokens, d.width)).astype(BF)
        o.g_out[...] = value.reshape((d.z_n, d.y_n, d.rows, d.width))
        reduce.begin(l, OUT)
        refill(l, "att")
        load("xin", l).wait()
        if l < top:
            reduce.sent(l + 1, QKV)
        for n in range(d.n_width):
            left = o.xin[:, :, n * d.chunk : (n + 1) * d.chunk].reshape(tokens, d.chunk)
            zs = slice(n * d.z_n // d.n_width, (n + 1) * d.z_n // d.n_width)
            value = tn(left, o.d_qkv[...].reshape(tokens, 3 * d.dh)).astype(BF)
            o.g_qkv[zs] = value.reshape((d.z_n // d.n_width, d.y_n, d.sp_n, d.rows, 3 * d.dh))
        reduce.begin(l, QKV)
        refill(l, "xin")
        load("stream", l).wait()
        scatter.arrive()

        def lower(rows):
            back, gain_term = norm_back(o.stream[rows, :], scatter.total(rows), gain_in)
            o.gain_sum[2 * l : 2 * l + 1, :] += gain_term
            value = o.o_grad[rows, :] + back
            o.o_grad[rows, :] = value
            if l > 0:
                o.gl[p.s, rows] = value.astype(BF)

        row_loop(d.tok, lower)
        scatter.end()
        if l > 0:
            gather.start(o.gl)
        else:
            small.start(0)
        refill(l, "stream")
        reduce.settle(l, UP)
        reduce.across(l, OUT)
        reduce.across(l, QKV)
        if l == 0:
            small.finish(0, o.mid_a)
            small.start(1)
        reduce.settle(l, OUT)
        reduce.settle(l, QKV)

    small.finish(1, o.mid_b)
    small.start(2)
    small.finish(2, o.o_gains)
    for l in reversed(range(d.layers)):
        for w in (DOWN, UP, OUT, QKV):
            reduce.last(l, w)
    for w in (DOWN, UP, OUT, QKV):
        reduce.sent(0, w)


ANY = pl.BlockSpec(memory_space=pl.ANY)
VM = pl.BlockSpec(memory_space=pltpu.VMEM)
SM = pl.BlockSpec(memory_space=pltpu.SMEM)


def call(kernel, d, inputs, outputs, scratch, identity):
    names = [i[0] for i in inputs] + [i[0] for i in outputs] + [i[0] for i in scratch]
    results = pl.pallas_call(
        functools.partial(kernel, d, names),
        out_shape=[jax.ShapeDtypeStruct(i[2], i[3]) for i in outputs],
        in_specs=[i[1] for i in inputs],
        out_specs=[i[1] for i in outputs],
        scratch_shapes=[i[1] for i in scratch],
        compiler_params=pltpu.CompilerParams(
            collective_id=identity, has_side_effects=True, vmem_limit_bytes=61 * 1024 * 1024
        ),
        name=kernel.__name__,
    )(*[i[2] for i in inputs])
    return dict(zip([i[0] for i in outputs], results))


def shards(dp_n, sp_n, tokens, cotangent, w_qkv, w_out, w_up, w_down, gains, piece_order, doc_lengths):
    _, tok, width = tokens.shape
    layers, _, rows, _ = w_qkv.shape
    ff = w_up.shape[-1]
    d = Dims(dp_n, sp_n, layers, tok, width, ff, doc_lengths.shape[1])
    r, s = lax.axis_index("dp"), lax.axis_index("sp")

    order = piece_order[0]
    ids = jnp.arange(sp_n, dtype=jnp.int32)
    inverse = jnp.sum(jnp.where(order[None, :] == ids[:, None], ids[None, :], 0), axis=1).astype(jnp.int32)
    starts = (jnp.cumsum(doc_lengths[0]) - doc_lengths[0]).astype(jnp.int32)
    meta = jnp.zeros((3, max(sp_n, d.docs)), jnp.int32)
    meta = meta.at[0, :sp_n].set(inverse).at[1, :sp_n].set(order).at[2, : d.docs].set(starts)
    head_ids = (s * d.heads + jnp.arange(d.heads, dtype=jnp.int32)).astype(F32)
    head_slope = jnp.exp2(-8.0 * (head_ids + 1.0) / HEADS)
    own = gains.shape[-1]
    padded = jnp.zeros((8, width), F32)
    padded = lax.dynamic_update_slice(
        padded, gains.reshape(2 * layers, own).astype(F32), (0, (r * sp_n + s) * own)
    )
    in_qkv = w_qkv.reshape(layers, 3, rows, sp_n, d.dh).transpose(0, 3, 2, 1, 4).reshape(layers, sp_n, rows, 3 * d.dh)
    in_up = (
        w_up.reshape(layers, rows, dp_n, sp_n, d.hid_own).transpose(0, 3, 1, 2, 4).reshape(layers, sp_n, rows, d.hid)
    )

    saved, weights = saved_shapes(d), weight_shapes(d)
    dma = pltpu.SemaphoreType.DMA
    fwd = call(
        fwd_kernel,
        d,
        [
            ("meta", SM, meta),
            ("head_slope", SM, head_slope),
            ("in_tokens", VM, tokens[0]),
            ("in_gains", VM, padded),
            ("in_qkv", ANY, in_qkv),
            ("in_out", ANY, w_out),
            ("in_up", ANY, in_up),
            ("in_down", ANY, w_down),
        ],
        [("o_output", VM, (tok, width), BF), ("o_gains", VM, (8, width), F32)]
        + [("o_" + n, ANY, (layers,) + weights[n][0], BF) for n in WEIGHTS]
        + [("o_" + n, ANY, (layers,) + saved[n][0], saved[n][1]) for n in SAVED],
        [(n, pltpu.VMEM((layers,) + weights[n][0], BF)) for n in WEIGHTS]
        + [(n, pltpu.VMEM((1 if n in ONCE else layers,) + saved[n][0], saved[n][1])) for n in SAVED]
        + [("sorted_att", pltpu.VMEM(saved["att"][0], BF))]
        + small_scratch(d)
        + comm_scratch(d)
        + [
            ("s_send", dma((layers, 4, sp_n))),
            ("s_recv", dma((layers, 4, sp_n))),
            ("own_sem", dma((layers, 4))),
            ("z_send", dma((layers, 4, d.z_n))),
            ("z_recv", dma((layers, 4, d.z_n))),
            ("y_send", dma((layers, 4, d.z_n, d.y_n))),
            ("y_recv", dma((layers, 4, d.z_n, d.y_n))),
            ("w_sem", dma((layers, 4))),
            ("save_sem", dma((layers, len(SAVED)))),
        ],
        0,
    )
    kinds = ("qkv", "out", "up", "down")
    blocks = [d.block_shape(w) for w in range(4)]
    bwd = call(
        bwd_kernel,
        d,
        [("meta", SM, meta), ("in_cotangent", VM, cotangent[0]), ("in_gains", VM, fwd["o_gains"])]
        + [("i_" + n, ANY, fwd["o_" + n]) for n in WEIGHTS + SAVED],
        [("o_grad", VM, (tok, width), F32), ("o_gains", VM, (8, width), F32)]
        + [("o_" + k, VM, (layers,) + b, F32) for k, b in zip(kinds, blocks)],
        [(n, pltpu.VMEM(weights[n][0], BF)) for n in WEIGHTS]
        + [(n, pltpu.VMEM(saved[n][0], saved[n][1])) for n in SAVED]
        + [
            ("gl", pltpu.VMEM((sp_n, tok, width), BF)),
            ("ml", pltpu.VMEM((sp_n, tok, width), BF)),
            ("d_att", pltpu.VMEM((sp_n, tok, d.dh), BF)),
            ("sorted_dqkv", pltpu.VMEM((sp_n, tok, 3 * d.dh), BF)),
            ("d_qkv", pltpu.VMEM((sp_n, tok, 3 * d.dh), BF)),
            ("d_keys", pltpu.VMEM((sp_n, tok, d.dh), F32)),
            ("d_values", pltpu.VMEM((sp_n, tok, d.dh), F32)),
            ("gain_sum", pltpu.VMEM((8, width), F32)),
        ]
        + [("g_" + k, pltpu.VMEM((d.z_n, d.y_n) + b, BF)) for k, b in zip(kinds, blocks)]
        + [("y_" + k, pltpu.VMEM((layers, max(1, d.y_n - 1), d.z_n) + b, BF)) for k, b in zip(kinds, blocks)]
        + [("z_" + k, pltpu.VMEM((layers, max(1, d.z_n - 1)) + b, BF)) for k, b in zip(kinds, blocks)]
        + [("x_" + k, pltpu.VMEM((layers,) + b, BF)) for k, b in zip(kinds[:3], blocks)]
        + small_scratch(d)
        + comm_scratch(d)
        + [
            ("load_sem", dma((len(WEIGHTS + SAVED),))),
            ("ry_send", dma((layers, 4, d.y_n))),
            ("ry_recv", dma((layers, 4, d.y_n))),
            ("rz_send", dma((layers, 4, d.z_n))),
            ("rz_recv", dma((layers, 4, d.z_n))),
            ("rs_send", dma((layers, 4, sp_n))),
            ("rs_recv", dma((layers, 4, sp_n))),
        ],
        1,
    )
    grad_qkv = bwd["o_qkv"].reshape(layers, sp_n, rows, 3, d.dh).transpose(0, 3, 2, 1, 4).reshape(w_qkv.shape)
    grad_up = (
        bwd["o_up"].reshape(layers, sp_n, rows, dp_n, d.hid_own).transpose(0, 2, 3, 1, 4).reshape(w_up.shape)
    )
    grad_gains = lax.dynamic_slice(bwd["o_gains"], (0, (r * sp_n + s) * own), (2 * layers, own))
    return (
        fwd["o_output"][None],
        bwd["o_grad"][None],
        grad_qkv,
        bwd["o_out"],
        grad_up,
        bwd["o_down"],
        grad_gains.reshape(gains.shape),
    )


def solution(mesh):
    return jax.shard_map(
        functools.partial(shards, mesh.shape["dp"], mesh.shape["sp"]),
        mesh=mesh,
        in_specs=(
            P("dp", "sp", None),
            P("dp", "sp", None),
            P(None, None, ("dp", "sp"), None),
            P(None, ("dp", "sp"), None),
            P(None, ("dp", "sp"), None),
            P(None, ("dp", "sp"), None),
            P(None, None, ("dp", "sp")),
            P("dp", None),
            P("dp", None),
        ),
        out_specs=(
            P("dp", "sp", None),
            P("dp", "sp", None),
            P(None, None, ("dp", "sp"), None),
            P(None, ("dp", "sp"), None),
            P(None, ("dp", "sp"), None),
            P(None, ("dp", "sp"), None),
            P(None, None, ("dp", "sp")),
        ),
        check_vma=False,
    )
```

```python
import functools

import jax
import jax.numpy as jnp
from jax import lax
from jax.experimental import pallas as pl
from jax.experimental.pallas import tpu as pltpu
from jax.sharding import PartitionSpec as P

HEADS = 8
HD = 128
EPS = 1e-05
MASKED = -1e30
MESH = pl.DeviceIdType.MESH
BF = jnp.bfloat16
F32 = jnp.float32
QKV, OUT, UP, DOWN = range(4)
Q0, Q1, O0, U0, U1, D0, D1 = range(7)


def nn(a, b):
    return lax.dot_general(a, b, (((1,), (0,)), ((), ())), preferred_element_type=F32)


def nt(a, b):
    return lax.dot_general(a, b, (((1,), (1,)), ((), ())), preferred_element_type=F32)


def tn(a, b):
    return lax.dot_general(a, b, (((0,), (0,)), ((), ())), preferred_element_type=F32)


FORWARD_PLAN = {
    "a": (("w", 0, 0), ("z", 0, 0), ("y", 0, 0), ("s", 1, 0), ("w", 0, 3), ("w", 0, 1), ("w", 0, 2), ("y", 0, 5),),
    "b": (("z", 0, 2), ("y", 0, 1), ("y", 0, 2), ("i", 0, 0),),
    "c": (("s", 1, 1), ("z", 0, 1), ("s", 1, 2), ("1", 0, 0), ("o", 0, 0), ("z", 0, 3),),
    "d0": (("i", 0, 1), ("z", 0, 4), ("3", 0, 0), ("i", 0, 2),),
    "e0": (("w", 1, 2), ("z", 0, 5), ("y", 1, 3), ("o", 0, 1), ("1", 0, 1),),
    "f0": (("3", 0, 1), ("1", 0, 2), ("i", 0, 4), ("i", 0, 3), ("s", 1, 3), ("w", 1, 1), ("w", 1, 0),),
    "g0": (("y", 0, 3), ("o", 0, 4), ("1", 0, 3), ("z", 1, 1),),
    "h0": (("3", 0, 3), ("1", 0, 5), ("o", 0, 3), ("w", 1, 3), ("y", 0, 4), ("i", 0, 5), ("1", 0, 4), ("o", 0, 2), ("o", 0, 5), ("i", 1, 1),),
    "i0": (("3", 0, 2),),
    "j0": (("3", 0, 5), ("z", 1, 0), ("y", 1, 5), ("3", 0, 4), ("y", 1, 0), ("y", 1, 2), ("z", 1, 2), ("1", 1, 1), ("y", 1, 4),),
    "k0": (("1", 1, 0), ("z", 1, 5), ("z", 1, 3),),
    "l0": (("o", 1, 0), ("i", 1, 0), ("3", 1, 0), ("z", 1, 4),),
    "m0": (("1", 1, 4),),
    "d1": (("3", 1, 1), ("y", 1, 1), ("o", 1, 1), ("1", 1, 5),),
    "e1": (("i", 1, 2), ("i", 1, 4), ("1", 1, 2),),
    "f1": (("i", 1, 5), ("3", 1, 4),),
    "g1": (("o", 1, 2), ("o", 1, 4), ("i", 1, 3),),
    "h1": (("1", 1, 3),),
    "i1": (("3", 1, 2), ("o", 1, 5), ("3", 1, 5), ("o", 1, 3),),
    "j1": (("3", 1, 3),),
}
BACKWARD_PLAN = {
    "D1": ((1, 5), (1, 6),),
    "G1": ((1, 3), (1, 4),),
    "H1": ((1, 5),),
    "K1": ((1, 5),),
    "L1": ((1, 3),),
    "M1": ((1, 0),),
    "N1": ((1, 6), (1, 1),),
    "B0": ((1, 3), (1, 6), (1, 3), (1, 2), (1, 4), (1, 0), (1, 5),),
    "C0": ((1, 6),),
    "D0": ((0, 6), (1, 0),),
    "E0": ((1, 1), (1, 4), (1, 4),),
    "F0": ((0, 5), (1, 2), (1, 1),),
    "G0": ((1, 1), (1, 2),),
    "H0": ((0, 4), (0, 6),),
    "I0": ((1, 2), (0, 5),),
    "J0": ((1, 0), (0, 6),),
    "K0": ((0, 4),),
    "L0": ((0, 5), (0, 6), (0, 3),),
    "M0": ((0, 0), (0, 2), (0, 1), (0, 4), (0, 3),),
    "N0": ((0, 0), (0, 1), (0, 5), (0, 1), (0, 3),),
    "O0": ((0, 2),),
    "P0": ((0, 3), (0, 4), (0, 1), (0, 2),),
    "Q0": ((0, 0), (0, 2), (0, 0),),
}


class Dims:
    def __init__(self, dp_n, sp_n, layers, tok, width, ff, docs):
        self.dp_n, self.sp_n, self.layers, self.tok, self.width = dp_n, sp_n, layers, tok, width
        self.z_n = 4 if dp_n % 4 == 0 else 1
        self.y_n = dp_n // self.z_n
        self.x_n = sp_n // 2
        self.rows = width // (dp_n * sp_n)
        self.heads = HEADS // sp_n
        self.dh = width // sp_n
        self.hid = ff // sp_n
        self.hid_own = ff // (dp_n * sp_n)
        self.docs = docs
        self.whole_lanes = self.hid_own % 128 == 0
        self.chunk = min(256, tok)
        self.half = tok // 2
        self.n_width = width // self.chunk
        self.n_hid = self.hid // self.chunk
        self.back = self.x_n
        half, part = sp_n // 2, self.hid_own // 2
        self.pieces = (
            (QKV, 0, sp_n, False),
            (OUT, 0, self.rows, False),
            (UP, 0, half, False),
            (UP, half, sp_n, False),
            (DOWN, 0, part, False),
            (DOWN, part, self.hid_own, True),
        )
        self.terms = (
            (QKV, 0, half),
            (QKV, half, sp_n),
            (OUT, 0, self.rows),
            (UP, 0, half),
            (UP, half, sp_n),
            (DOWN, 0, part),
            (DOWN, part, self.hid_own),
        )
        self.z_first = [(Q1,)] + [(D1,)] * (layers - 1)
        self.pairs = [(i, b) for i in range(sp_n) for b in range(max(0, i - self.back), i + 1)]

    def block_shape(self, which):
        return {
            QKV: (self.sp_n, self.rows, 3 * self.dh),
            OUT: (self.rows, self.width),
            UP: (self.sp_n, self.rows, self.hid),
            DOWN: (self.hid_own, self.width),
        }[which]


class Place:
    def __init__(self, d):
        self.d = d
        self.r = lax.axis_index("dp")
        self.s = lax.axis_index("sp")
        self.z, self.y = self.r // d.y_n, self.r % d.y_n
        self.x, self.c = self.s // 2, self.s % 2
        self.partner = self.x * 2 + (self.c + 1) % 2

    def slot(self, step):
        return ((self.x + step // 2) % self.d.x_n) * 2 + (self.c + step % 2) % 2

    def pieces(self, step):
        if isinstance(step, int) and step < 2:
            return (self.slot(step), 0), (self.slot(step), 1)
        first = step // 2 * 2
        return (self.slot(first), step % 2), (self.slot(first + 1), step % 2)

    def zpeer(self, dz):
        return (self.z + dz) % self.d.z_n

    def ypeer(self, dy):
        return (self.y + dy) % self.d.y_n

    def line(self):
        high = self.z // 2
        inside = ((self.z + 1) // 2) % 2
        first = inside * 3 * high + (1 - inside) * (1 + high)
        return inside == 1, (self.z, first, 2 - high, 3 - 3 * high)

    def dev(self, z, y):
        return (z * self.d.y_n + y, self.s)

    def moved(self):
        d = self.d
        flat = self.r * d.sp_n + self.s
        goal = (flat % d.dp_n, flat // d.dp_n)
        mine = self.s * d.dp_n + self.r
        source = (mine // d.sp_n, mine % d.sp_n)
        stays = flat == mine
        return goal, source, stays

    def barrier(self):
        d = self.d
        sem = pltpu.get_barrier_semaphore()
        peers = [(self.r, self.slot(t)) for t in range(1, d.sp_n)]
        peers += [self.dev(self.zpeer(k), self.y) for k in range(1, d.z_n)]
        peers += [self.dev(self.z, self.ypeer(k)) for k in range(1, d.y_n)]
        for peer in peers:
            pl.semaphore_signal(sem, inc=1, device_id=peer, device_id_type=MESH)
        goal, source, stays = self.moved()

        @pl.when(jnp.logical_not(stays))
        def _():
            pl.semaphore_signal(sem, inc=1, device_id=goal, device_id_type=MESH)
            pl.semaphore_signal(sem, inc=1, device_id=source, device_id_type=MESH)
            pl.semaphore_wait(sem, len(peers) + 2)

        @pl.when(stays)
        def _():
            pl.semaphore_wait(sem, len(peers))


def rcopy(src, dst, send, recv, device):
    return pltpu.make_async_remote_copy(
        src_ref=src, dst_ref=dst, send_sem=send, recv_sem=recv, device_id=device, device_id_type=MESH
    )


def pair(ref, pieces, *cols):
    return jnp.concatenate([ref[(slot, half) + (slice(None),) + cols] for slot, half in pieces], axis=0)


def put_pair(ref, pieces, cols, value):
    rows = value.shape[0] // 2
    for k, (slot, half) in enumerate(pieces):
        ref[slot, half, :, cols] = value[k * rows : (k + 1) * rows].astype(ref.dtype)


class Gather:
    def __init__(self, p, send, recv):
        self.p, self.send, self.recv = p, send, recv

    def copy(self, buf, slot, half, way, goal):
        block = buf.at[slot, half]
        return rcopy(block, block, self.send.at[way, goal, half], self.recv.at[slot, half], (self.p.r, goal))

    def start(self, buf, half):
        p = self.p
        for dx in range(1, p.d.x_n):
            self.copy(buf, p.s, half, 0, p.slot(2 * dx)).start()
        self.copy(buf, p.s, half, 0, p.partner).start()

    def onward(self, buf, slot, half):
        block = buf.at[slot, half]
        p = self.p
        return rcopy(block, block, self.send.at[1, slot, half], self.recv.at[slot, half], (p.r, p.partner))

    def arrived(self, buf, slot, half):
        self.copy(buf, slot, half, 0, self.p.partner).wait_recv()

    def near(self, buf):
        for half in range(2):
            self.arrived(buf, self.p.partner, half)

    def far(self, buf, step):
        first, second = self.p.pieces(step)
        self.arrived(buf, *first)
        self.onward(buf, *first).start()
        self.arrived(buf, *second)

    def end(self, buf):
        p = self.p
        for half in range(2):
            for dx in range(1, p.d.x_n):
                self.copy(buf, p.s, half, 0, p.slot(2 * dx)).wait_send()
                self.onward(buf, p.slot(2 * dx), half).wait_send()
            self.copy(buf, p.s, half, 0, p.partner).wait_send()


class Scatter:
    def __init__(self, p, part, near, far, near_send, near_recv, far_send, far_recv):
        self.p, self.part, self.near, self.far = p, part, near, far
        self.near_send, self.near_recv, self.far_send, self.far_recv = near_send, near_recv, far_send, far_recv

    def near_copy(self, x, half):
        p = self.p
        return rcopy(
            self.part.at[x * 2 + (p.c + 1) % 2, half],
            self.near.at[x, half],
            self.near_send.at[x, half],
            self.near_recv.at[x, half],
            (p.r, p.partner),
        )

    def far_copy(self, x, half, source):
        p = self.p
        goal = x * 2 + p.c
        return rcopy(
            self.part.at[goal, half],
            self.far.at[source, half],
            self.far_send.at[x, half],
            self.far_recv.at[source, half],
            (p.r, goal),
        )

    def put(self, step):
        if isinstance(step, int):
            if step == 1:
                for half in range(2):
                    self.near_copy(self.p.x, half).start()
        else:
            self.near_copy(self.p.slot(step // 2 * 2) // 2, step % 2).start()

    def cross(self, step):
        p = self.p
        slot, half = p.slot(step // 2 * 2), step % 2
        x = slot // 2
        self.near_copy(x, half).wait_recv()
        size = min(64, p.d.half)

        @pl.loop(0, p.d.half // size)
        def _(i):
            rows = pl.ds(pl.multiple_of(i * size, size), size)
            both = self.part[slot, half, rows].astype(F32) + self.near[x, half, rows].astype(F32)
            self.part[slot, half, rows] = both.astype(BF)

        self.far_copy(x, half, p.x).start()

    def arrive(self, half):
        p = self.p
        self.near_copy(p.x, half).wait_recv()
        for dx in range(1, p.d.x_n):
            x = (p.x + dx) % p.d.x_n
            self.far_copy(x, half, x).wait_recv()

    def total(self, half, rows):
        p = self.p
        value = self.part[p.s, half, rows].astype(F32) + self.near[p.x, half, rows].astype(F32)
        for dx in range(1, p.d.x_n):
            value = value + self.far[(p.x + dx) % p.d.x_n, half, rows].astype(F32)
        return value

    def end(self):
        p = self.p
        for half in range(2):
            for dx in range(p.d.x_n):
                x = (p.x + dx) % p.d.x_n
                self.near_copy(x, half).wait_send()
                if dx:
                    self.far_copy(x, half, p.x).wait_send()


class SmallSum:
    def __init__(self, p, first, sp_in, mid_a, z_in, mid_b, y_in, sp_sem, z_sem, y_sem):
        self.p = p
        self.bufs = ((first, sp_in, sp_sem), (mid_a, z_in, z_sem), (mid_b, y_in, y_sem))

    def plan(self, stage):
        p = self.p
        if stage == 0:
            return p.s, [(p.slot(t), (p.r, p.slot(t))) for t in range(1, p.d.sp_n)]
        if stage == 1:
            return p.z, [(p.zpeer(k), p.dev(p.zpeer(k), p.y)) for k in range(1, p.d.z_n)]
        return p.y, [(p.ypeer(k), p.dev(p.z, p.ypeer(k))) for k in range(1, p.d.y_n)]

    def start(self, stage):
        src, dst, sem = self.bufs[stage]
        own, peers = self.plan(stage)
        for index, device in peers:
            rcopy(src, dst.at[own], sem.at[0, index], sem.at[1, own], device).start()

    def finish(self, stage, result):
        src, dst, sem = self.bufs[stage]
        own, peers = self.plan(stage)
        value = src[...]
        for index, device in peers:
            rcopy(src, dst.at[index], sem.at[0, index], sem.at[1, index], device).wait_recv()
            value = value + dst[index]
        result[...] = value
        for index, device in peers:
            rcopy(src, dst.at[own], sem.at[0, index], sem.at[1, own], device).wait_send()


def small_scratch(d):
    return [
        ("sp_in", pltpu.VMEM((d.sp_n, 8, d.width), F32)),
        ("mid_a", pltpu.VMEM((8, d.width), F32)),
        ("z_in", pltpu.VMEM((d.z_n, 8, d.width), F32)),
        ("mid_b", pltpu.VMEM((8, d.width), F32)),
        ("y_in", pltpu.VMEM((d.y_n, 8, d.width), F32)),
        ("sp_sem", pltpu.SemaphoreType.DMA((2, d.sp_n))),
        ("z_sem", pltpu.SemaphoreType.DMA((2, d.z_n))),
        ("y_sem", pltpu.SemaphoreType.DMA((2, d.y_n))),
    ]


def comm_scratch(d):
    return [
        ("part", pltpu.VMEM((d.sp_n, 2, d.half, d.width), BF)),
        ("near", pltpu.VMEM((d.x_n, 2, d.half, d.width), BF)),
        ("far", pltpu.VMEM((d.x_n, 2, d.half, d.width), BF)),
        ("ag_send", pltpu.SemaphoreType.DMA((2, d.sp_n, 2))),
        ("ag_recv", pltpu.SemaphoreType.DMA((d.sp_n, 2))),
        ("near_send", pltpu.SemaphoreType.DMA((d.x_n, 2))),
        ("near_recv", pltpu.SemaphoreType.DMA((d.x_n, 2))),
        ("far_send", pltpu.SemaphoreType.DMA((d.x_n, 2))),
        ("far_recv", pltpu.SemaphoreType.DMA((d.x_n, 2))),
    ]


def term_scratch(d, l, term):
    w, first, last = d.terms[term]
    block = (last - first,) + d.block_shape(w)[1:]
    z_first = term in d.z_first[l]
    y_shape = (max(1, d.y_n - 1), 1 if z_first else d.z_n) + block
    z_shape = (5, d.y_n if z_first else 1) + block
    return [
        ("y_in_%d_%d" % (l, term), pltpu.VMEM(y_shape, BF)),
        ("z_in_%d_%d" % (l, term), pltpu.VMEM(z_shape, BF)),
    ]


SAVED = ("xin", "qkv", "att", "probs", "xmid", "hid", "slope", "stream", "mid")
ONCE = ("qkv", "att", "probs", "hid", "slope")
WEIGHTS = ("wqkv", "wout", "wup", "wdown")


def saved_shapes(d):
    full = (d.sp_n, 2, d.half)
    return {
        "xin": (full + (d.width,), BF),
        "qkv": (full + (3 * d.dh,), BF),
        "att": (full + (d.dh,), BF),
        "probs": ((d.heads, len(d.pairs), d.tok, d.tok), BF),
        "xmid": (full + (d.width,), BF),
        "hid": (full + (d.hid,), BF),
        "slope": (full + (d.hid,), BF),
        "stream": ((2, d.half, d.width), F32),
        "mid": ((2, d.half, d.width), F32),
    }


def weight_shapes(d):
    return {name: ((d.z_n, d.y_n) + d.block_shape(i), BF) for i, name in enumerate(WEIGHTS)}


class Fetch:
    def __init__(self, p, o):
        self.p, self.o = p, o
        self.full = (o.wqkv, o.wout, o.wup, o.wdown)

    def spread(self, l, w):
        p, o = self.p, self.o
        own = self.full[w].at[l, p.z, p.y]
        if w in (QKV, UP):
            src = o.in_qkv if w == QKV else o.in_up
            for t in range(1, p.d.sp_n):
                j = p.slot(t)
                rcopy(src.at[l, j], own.at[p.s], o.s_send.at[l, w, j], o.s_recv.at[l, w, p.s], (p.r, j)).start()
            pltpu.make_async_copy(src.at[l, p.s], own.at[p.s], o.own_sem.at[l, w]).start()
        elif w == DOWN:
            pltpu.make_async_copy(o.in_down.at[l], own, o.own_sem.at[l, w]).start()
        else:
            goal, _, stays = p.moved()

            @pl.when(stays)
            def _():
                pltpu.make_async_copy(o.in_out.at[l], own, o.own_sem.at[l, w]).start()

            @pl.when(jnp.logical_not(stays))
            def _():
                there = self.full[w].at[l, goal[0] // p.d.y_n, goal[0] % p.d.y_n]
                rcopy(o.in_out.at[l], there, o.s_send.at[l, w, 0], o.s_recv.at[l, w, 0], goal).start()

    def own(self, l, w):
        p, o = self.p, self.o
        own = self.full[w].at[l, p.z, p.y]
        if w in (QKV, UP):
            src = o.in_qkv if w == QKV else o.in_up
            pltpu.make_async_copy(src.at[l, p.s], own.at[p.s], o.own_sem.at[l, w]).wait()
            for t in range(1, p.d.sp_n):
                j = p.slot(t)
                rcopy(src.at[l, j], own.at[j], o.s_send.at[l, w, j], o.s_recv.at[l, w, j], (p.r, j)).wait_recv()
        elif w == DOWN:
            pltpu.make_async_copy(o.in_down.at[l], own, o.own_sem.at[l, w]).wait()
        else:
            goal, _, stays = p.moved()

            @pl.when(stays)
            def _():
                pltpu.make_async_copy(o.in_out.at[l], own, o.own_sem.at[l, w]).wait()

            @pl.when(jnp.logical_not(stays))
            def _():
                rcopy(o.in_out.at[l], own, o.s_send.at[l, w, 0], o.s_recv.at[l, w, 0], goal).wait_recv()

    def block(self, l, piece, z, y):
        w, first, last, _ = self.p.d.pieces[piece]
        return self.full[w].at[l, z, y, first:last]

    def columns(self, piece):
        p = self.p
        if self.p.d.pieces[piece][3]:
            return [p.y] + [p.ypeer(m) for m in range(1, p.d.y_n)]
        return [p.y]

    def copy(self, l, piece, z, y, way, device):
        o = self.o
        block = self.block(l, piece, z, y)
        return rcopy(block, block, o.b_send.at[l, piece, z, y, way], o.b_recv.at[l, piece, z, y], device)

    def arrived(self, l, piece, z, y):
        self.copy(l, piece, z, y, 0, (self.p.r, self.p.s)).wait_recv()

    def along_z(self, l, piece, role, y, act):
        p = self.p
        if p.d.z_n == 1 or role == 3:
            return
        inside, at = p.line()
        z = at[role]

        @pl.when(inside)
        def _():
            for way, goal in enumerate(((at[1], at[2]), (at[2], at[3]), (at[1],))[role]):
                act(self.copy(l, piece, z, y, way, p.dev(goal, p.y)))

        if role == 0:

            @pl.when(jnp.logical_not(inside))
            def _():
                act(self.copy(l, piece, z, y, 0, p.dev(at[1], p.y)))

    def along_y(self, l, piece, role, act):
        p = self.p
        z = p.line()[1][role]
        for m in range(1, p.d.y_n):
            act(self.copy(l, piece, z, p.y, 1 + m, p.dev(p.z, p.ypeer(m))))

    def start_z(self, l, *pieces):
        for piece in pieces:
            self.along_z(l, piece, 0, self.p.y, lambda c: c.start())

    def start_y(self, l, *pieces):
        for piece in pieces:
            self.along_y(l, piece, 0, lambda c: c.start())

    def inner(self, l, *pieces):
        if self.p.d.z_n > 1:

            @pl.when(self.p.line()[0])
            def _():
                for piece in pieces:
                    self.relay(l, piece, 2)

    def outer(self, l, *pieces):
        if self.p.d.z_n > 1:

            @pl.when(jnp.logical_not(self.p.line()[0]))
            def _():
                for piece in pieces:
                    self.relay(l, piece, 2)

    def relay(self, l, piece, *roles):
        p = self.p
        cross_first = p.d.pieces[piece][3]
        at = p.line()[1]
        for role in roles:
            if role == 1 and cross_first:
                for y in self.columns(piece)[1:]:
                    self.arrived(l, piece, p.z, y)
                    self.along_z(l, piece, 0, y, lambda c: c.start())
            if p.d.z_n == 1:
                continue
            for y in self.columns(piece):
                self.arrived(l, piece, at[role], y)
                self.along_z(l, piece, role, y, lambda c: c.start())
            if not cross_first:
                self.along_y(l, piece, role, lambda c: c.start())

    def ready(self, l, *pieces):
        p = self.p
        for piece in pieces:
            if not p.d.pieces[piece][3]:
                for role in range(4 if p.d.z_n > 1 else 1):
                    for m in range(1, p.d.y_n):
                        self.arrived(l, piece, p.line()[1][role], p.ypeer(m))

    def save(self, l, w):
        return pltpu.make_async_copy(self.full[w].at[l], self.o.w_save[w].at[l], self.o.w_sem.at[l, w])

    def end(self):
        p, o = self.p, self.o
        for l in range(p.d.layers):
            for w in range(4):
                own = self.full[w].at[l, p.z, p.y]
                if w in (QKV, UP):
                    src = o.in_qkv if w == QKV else o.in_up
                    for t in range(1, p.d.sp_n):
                        j = p.slot(t)
                        rcopy(src.at[l, j], own.at[p.s], o.s_send.at[l, w, j], o.s_recv.at[l, w, p.s], (p.r, j)).wait_send()
                elif w == OUT:
                    goal, _, stays = p.moved()

                    @pl.when(jnp.logical_not(stays))
                    def _():
                        rcopy(o.in_out.at[l], own, o.s_send.at[l, w, 0], o.s_recv.at[l, w, 0], goal).wait_send()

                self.save(l, w).wait()
            for piece in range(len(p.d.pieces)):
                for role in range(4 if p.d.z_n > 1 else 1):
                    for y in self.columns(piece):
                        self.along_z(l, piece, role, y, lambda c: c.wait_send())
                    if role == 0 or not p.d.pieces[piece][3]:
                        self.along_y(l, piece, role, lambda c: c.wait_send())


class Refs:
    pass


def mean_of(v):
    return jnp.mean(v, axis=-1, keepdims=True)


def norm_rows(v, gain):
    center = v - mean_of(v)
    return center * lax.rsqrt(mean_of(center * center) + EPS) * gain


def row_loop(tok, body, step=32):
    step = min(step, tok)

    @pl.loop(0, tok // step)
    def _(i):
        body(pl.ds(pl.multiple_of(i * step, step), step))


def lay_out(d, o):
    for i in range(d.sp_n):
        where = jnp.int32(0)
        for j in range(1, d.sp_n):
            where = jnp.where(o.in_order[0, j] == i, j, where)
        o.meta[0, i] = where
        o.meta[1, i] = o.in_order[0, i]
    start = jnp.int32(0)
    for b in range(d.docs):
        o.meta[2, b] = start
        start = start + o.in_lengths[0, b]


def up_columns(d, j, k):
    first = (k * d.sp_n + j) * d.hid_own
    return slice(first, first + d.hid_own), slice(k * d.hid_own, (k + 1) * d.hid_own)


def attention_forward(d, o, l):
    tok = d.tok
    slopes = []
    for h in range(d.heads):
        head = (lax.axis_index("sp") * d.heads + (h + 1)).astype(F32)
        slopes.append(jnp.exp2(jnp.full((1, 1), -8.0 / HEADS, F32) * head))
    for i in range(d.sp_n):
        here = o.meta[0, i]
        pos = i * tok + lax.broadcasted_iota(jnp.int32, (tok, 1), 0)
        start = jnp.zeros((tok, 1), jnp.int32)
        for b in range(1, d.docs):
            start = jnp.where(pos >= o.meta[2, b], o.meta[2, b], start)
        blocks = range(max(0, i - d.back), i + 1)
        for h in range(d.heads):
            lanes = slice(h * HD, (h + 1) * HD)
            query = o.qkv[0, here, :, :, lanes].reshape(tok, HD)
            scores = []
            for b in blocks:
                keys = o.qkv[0, o.meta[0, b], :, :, d.dh + h * HD : d.dh + (h + 1) * HD].reshape(tok, HD)
                key_pos = b * tok + lax.broadcasted_iota(jnp.int32, (tok, tok), 1)
                query_pos = i * tok + lax.broadcasted_iota(jnp.int32, (tok, tok), 0)
                score = nt(query, keys) * HD ** (-0.5) + slopes[h] * (key_pos - query_pos).astype(F32)
                allowed = key_pos >= start
                if b == i:
                    allowed = allowed & (key_pos <= query_pos)
                scores.append(jnp.where(allowed, score, MASKED))
            top = scores[0].max(axis=-1, keepdims=True)
            for score in scores[1:]:
                top = jnp.maximum(top, score.max(axis=-1, keepdims=True))
            expo = [jnp.exp(score - top) for score in scores]
            total = expo[0].sum(axis=-1, keepdims=True)
            for part in expo[1:]:
                total = total + part.sum(axis=-1, keepdims=True)
            inverse = 1.0 / total
            result = None
            for b, part in zip(blocks, expo):
                low = (part * inverse).astype(BF)
                o.probs[0, h, d.pairs.index((i, b))] = low
                values = o.qkv[0, o.meta[0, b], :, :, 2 * d.dh + h * HD : 2 * d.dh + (h + 1) * HD].reshape(tok, HD)
                term = nn(low, values)
                result = term if result is None else result + term
            o.sorted_att[i, :, :, lanes] = result.astype(BF).reshape(2, d.half, HD)


def fwd_kernel(d, names, *refs):
    o = Refs()
    for name, ref in zip(names, refs):
        setattr(o, name, ref)
    o.w_save = (o.o_wqkv, o.o_wout, o.o_wup, o.o_wdown)
    p = Place(d)
    fetch = Fetch(p, o)
    gather = Gather(p, o.ag_send, o.ag_recv)
    scatter = Scatter(p, o.part, o.near, o.far, o.near_send, o.near_recv, o.far_send, o.far_recv)
    small = SmallSum(p, o.in_gains, o.sp_in, o.mid_a, o.z_in, o.mid_b, o.y_in, o.sp_sem, o.z_sem, o.y_sem)

    def save(name, l):
        ref, out = getattr(o, name), getattr(o, "o_" + name)
        held = 0 if name in ONCE else l
        return pltpu.make_async_copy(ref.at[held], out.at[l], o.save_sem.at[l, SAVED.index(name)])

    def free(l, *names):
        if l > 0:
            for name in names:
                save(name, l - 1).wait()

    def run(slot):
        for op, l, piece in FORWARD_PLAN.get(slot, ()):
            if op == "s":
                fetch.spread(l, piece)
            elif op == "w":
                fetch.own(l, piece)
            elif op == "z":
                fetch.start_z(l, piece)
            elif op == "y":
                fetch.start_y(l, piece)
            elif op == "i":
                fetch.inner(l, piece)
            elif op == "o":
                fetch.outer(l, piece)
            else:
                fetch.relay(l, piece, int(op))

    def place(l):
        if d.whole_lanes:
            for j in range(d.sp_n):
                for i in range(3):
                    o.in_qkv[l, j, :, i * d.dh : (i + 1) * d.dh] = o.raw_qkv[l, i, :, j * d.dh : (j + 1) * d.dh]
                for k in range(d.dp_n):
                    whole, kept = up_columns(d, j, k)
                    o.in_up[l, j, :, kept] = o.raw_up[l, :, whole]

    place(0)
    p.barrier()
    for w in (QKV, OUT):
        fetch.spread(0, w)
    small.start(0)
    for l in range(1, d.layers):
        place(l)
    lay_out(d, o)
    for w in (UP, DOWN):
        fetch.spread(0, w)
    run("a")
    small.finish(0, o.mid_a)
    small.start(1)
    run("b")
    small.finish(1, o.mid_b)
    small.start(2)
    run("c")
    small.finish(2, o.o_gains)

    def norm_in(l, half, gain):
        def first(rows):
            v = o.in_tokens[half, rows].astype(F32)
            o.stream[0, half, rows] = v
            o.xin[0, p.s, half, rows] = norm_rows(v, gain).astype(BF)

        row_loop(d.half, first)

    for half in range(2):
        norm_in(0, half, o.o_gains[0:1, :])
        gather.start(o.xin.at[0], half)

    for l in range(d.layers):
        gain_mid = o.o_gains[2 * l + 1 : 2 * l + 2, :]
        xin, xmid = o.xin.at[l], o.xmid.at[l]
        save("stream", l).start()
        run("d%d" % l)
        fetch.ready(l, 0)
        fetch.save(l, QKV).start()
        free(l, "qkv")
        third = 3 * d.dh // 3

        def project(pieces):
            block = pair(xin, pieces)
            for n in range(3):
                cols = slice(n * third, (n + 1) * third)
                weight = o.wqkv[l, :, :, :, :, cols].reshape(d.width, third)
                put_pair(o.qkv.at[0], pieces, cols, nn(block, weight))

        project(p.pieces(0))
        gather.near(xin)
        project(p.pieces(1))
        run("e%d" % l)

        @pl.loop(2, d.sp_n)
        def _(t):
            gather.far(xin, t)
            project(p.pieces(t))

        gather.end(xin)
        save("xin", l).start()
        save("qkv", l).start()
        run("f%d" % l)
        free(l, "probs", "att")
        attention_forward(d, o, l)
        save("probs", l).start()
        run("g%d" % l)
        fetch.ready(l, 1)
        fetch.save(l, OUT).start()

        def out_part(pieces):
            blocks = []
            for slot, half in pieces:
                block = o.sorted_att[o.meta[1, slot], half]
                o.att[0, slot, half] = block
                blocks.append(block)
            block = jnp.concatenate(blocks, axis=0)
            for n in range(d.n_width):
                cols = slice(n * d.chunk, (n + 1) * d.chunk)
                weight = o.wout[l, :, :, :, cols].reshape(d.dh, d.chunk)
                put_pair(o.part, pieces, cols, nn(block, weight))

        @pl.loop(2, d.sp_n)
        def _(t):
            out_part(p.pieces(t))
            scatter.put(t)

            @pl.when(t > 2)
            def _():
                scatter.cross(t - 1)

        out_part(p.pieces(1))
        scatter.put(1)
        scatter.cross(d.sp_n - 1)
        out_part(p.pieces(0))
        save("att", l).start()
        run("h%d" % l)

        def middle(half, rows):
            v = o.stream[l, half, rows] + scatter.total(half, rows)
            o.mid[l, half, rows] = v
            xmid[p.s, half, rows] = norm_rows(v, gain_mid).astype(BF)

        for half in range(2):
            scatter.arrive(half)
            row_loop(d.half, functools.partial(middle, half))
            gather.start(xmid, half)
            if half == 0:
                run("i%d" % l)
        scatter.end()
        save("mid", l).start()
        run("j%d" % l)
        fetch.ready(l, 2, 3)
        fetch.save(l, UP).start()
        free(l, "hid", "slope")

        def up(pieces):
            block = pair(xmid, pieces)
            for n in range(d.n_hid):
                cols = slice(n * d.chunk, (n + 1) * d.chunk)
                weight = o.wup[l, :, :, :, :, cols].reshape(d.width, d.chunk)
                pre = nn(block, weight)
                phi = 0.5 * (1.0 + lax.erf(pre * (0.5**0.5)))
                put_pair(o.hid.at[0], pieces, cols, pre * phi)
                density = jnp.exp(-0.5 * pre * pre) * 0.3989422804014327
                put_pair(o.slope.at[0], pieces, cols, phi + pre * density)

        def down(pieces):
            hidden = pair(o.hid.at[0], pieces)
            for n in range(d.n_width):
                cols = slice(n * d.chunk, (n + 1) * d.chunk)
                weight = o.wdown[l, :, :, :, cols].reshape(d.hid, d.chunk)
                put_pair(o.part, pieces, cols, nn(hidden, weight))

        up(p.pieces(0))
        gather.near(xmid)
        up(p.pieces(1))
        run("k%d" % l)
        fetch.ready(l, 4, 5)
        fetch.save(l, DOWN).start()

        @pl.loop(2, d.sp_n)
        def _(t):
            gather.far(xmid, t)
            up(p.pieces(t))

            @pl.when(t > 2)
            def _():
                scatter.cross(t - 1)

            down(p.pieces(t))
            scatter.put(t)

        down(p.pieces(1))
        scatter.put(1)
        scatter.cross(d.sp_n - 1)
        down(p.pieces(0))
        gather.end(xmid)
        save("xmid", l).start()
        save("hid", l).start()
        save("slope", l).start()
        run("l%d" % l)

        def last(half, rows):
            v = o.mid[l, half, rows] + scatter.total(half, rows)
            if l + 1 < d.layers:
                o.stream[l + 1, half, rows] = v
                o.xin[l + 1, p.s, half, rows] = norm_rows(v, o.o_gains[2 * l + 2 : 2 * l + 3, :]).astype(BF)
            else:
                o.o_output[half, rows] = v.astype(BF)

        for half in range(2):
            scatter.arrive(half)
            row_loop(d.half, functools.partial(last, half))
            if l + 1 < d.layers:
                gather.start(o.xin.at[l + 1], half)
                if half == 0:
                    run("m%d" % l)
        scatter.end()

    fetch.end()
    for l in range(d.layers):
        for name in SAVED:
            if l == d.layers - 1 or name not in ONCE:
                save(name, l).wait()


class Reduce:
    def __init__(self, p, o):
        self.p, self.o = p, o
        self.grad = (o.g_qkv, o.g_out, o.g_up, o.g_down)
        self.sp_in = (o.x_qkv, o.x_out, o.x_up, None)
        self.result = (o.o_qkv, o.o_out, o.o_up, o.o_down)
        self.done = {}

    def z_first(self, l, term):
        return term in self.p.d.z_first[l]

    def ins(self, l, term):
        o = self.o
        return getattr(o, "y_in_%d_%d" % (l, term)), getattr(o, "z_in_%d_%d" % (l, term))

    def columns(self, l, term):
        p = self.p
        if self.z_first(l, term):
            return [(y, y) for y in [p.y] + [p.ypeer(m) for m in range(1, p.d.y_n)]]
        return [(p.y, 0)]

    def step(self, l, *terms):
        for term in terms:
            stages = (self.y_send, self.y_sum, self.inner, self.finish_z)
            if self.z_first(l, term):
                stages = (self.z_send, self.inner, self.z_sum, self.finish_y)
            count = self.done.get((l, term), 0)
            self.done[l, term] = count + 1
            stages[count](l, term)

    def groups(self, term):
        w, first, last = self.p.d.terms[term]
        if w in (QKV, UP):
            return [((j,), (j - first,)) for j in range(first, last)]
        rows = min(32, last - first)
        return [
            ((slice(j, j + rows),), (slice(j - first, j - first + rows),)) for j in range(first, last, rows)
        ]

    def y_copy(self, l, term, k):
        p, o = self.p, self.o
        w, first, last = p.d.terms[term]
        index = p.d.y_n - k - 1
        there = p.ypeer(k)
        into = self.ins(l, term)[0].at[index]
        if self.z_first(l, term):
            src, into = self.grad[w].at[p.z, there, first:last], into.at[0]
        else:
            src = self.grad[w].at[:, there, first:last]
        return rcopy(src, into, o.ry_send.at[l, term, k], o.ry_recv.at[l, term, index], p.dev(p.z, there))

    def y_send(self, l, term):
        for k in range(1, self.p.d.y_n):
            self.y_copy(l, term, k).start()

    def y_wait(self, l, term):
        for k in range(1, self.p.d.y_n):
            self.y_copy(l, term, self.p.d.y_n - k).wait_recv()

    def y_sum(self, l, term):
        p = self.p
        w = p.d.terms[term][0]
        y_in, _ = self.ins(l, term)
        self.y_wait(l, term)
        for z in range(p.d.z_n):
            for index, here in self.groups(term):
                value = self.grad[w][(z, p.y) + index].astype(F32)
                for m in range(p.d.y_n - 1):
                    value = value + y_in[(m, z) + here].astype(F32)
                self.grad[w][(z, p.y) + index] = value.astype(BF)
        self.z_send(l, term)

    def z_copy(self, l, term, column, z, goal, place, way):
        p, o = self.p, self.o
        w, first, last = p.d.terms[term]
        y, slot = column
        return rcopy(
            self.grad[w].at[z, y, first:last],
            self.ins(l, term)[1].at[place, slot],
            o.rz_send.at[l, term, slot, way],
            o.rz_recv.at[l, term, slot, place],
            p.dev(goal, p.y),
        )

    def z_goals(self, inside):
        at = self.p.line()[1]
        if inside:
            return ((at[3], at[2], 3), (at[2], at[2], 1), (at[1], at[1], 0))
        return ((at[1], at[1], 0), (at[2], at[1], 2), (at[3], at[2], 4))

    def both(self, inner, outer):
        inside, _ = self.p.line()
        pl.when(inside)(inner)
        pl.when(jnp.logical_not(inside))(outer)

    def z_send(self, l, term):
        if self.p.d.z_n == 1:
            return

        def send(inside, ways):
            for column in self.columns(l, term):
                for way in ways:
                    self.z_copy(l, term, column, *self.z_goals(inside)[way], way).start()

        self.both(lambda: send(True, (0,)), lambda: send(False, (0, 1, 2)))

    def z_wait(self, l, term, column, place):
        self.z_copy(l, term, column, self.p.z, self.p.z, place, 0).wait_recv()

    def inner(self, l, term):
        p = self.p
        if p.d.z_n == 1:
            return
        w = p.d.terms[term][0]
        _, z_in = self.ins(l, term)

        def relay():
            for way, places in ((1, (2,)), (2, (3, 4))):
                z, goal, place = self.z_goals(True)[way]
                for column in self.columns(l, term):
                    y, slot = column
                    for source in places:
                        self.z_wait(l, term, column, source)
                    for index, here in self.groups(term):
                        value = self.grad[w][(z, y) + index].astype(F32)
                        for source in places:
                            value = value + z_in[(source, slot) + here].astype(F32)
                        self.grad[w][(z, y) + index] = value.astype(BF)
                    self.z_copy(l, term, column, z, goal, place, way).start()

        pl.when(p.line()[0])(relay)

    def z_total(self, l, term, column, store):
        p = self.p
        w = p.d.terms[term][0]
        _, z_in = self.ins(l, term)
        y, slot = column

        def total(places):
            for source in places:
                self.z_wait(l, term, column, source)
            for index, here in self.groups(term):
                value = self.grad[w][(p.z, y) + index].astype(F32)
                for source in places:
                    value = value + z_in[(source, slot) + here].astype(F32)
                store(y, index, here, value)

        if p.d.z_n == 1:
            total(())
        else:
            self.both(lambda: total((0, 1)), lambda: total((0,)))

    def z_sum(self, l, term):
        w = self.p.d.terms[term][0]

        def store(y, index, here, value):
            self.grad[w][(self.p.z, y) + index] = value.astype(BF)

        for column in self.columns(l, term):
            self.z_total(l, term, column, store)
        self.y_send(l, term)

    def finish_z(self, l, term):
        def store(y, index, here, value):
            self.settle(l, term, index, value)

        self.z_total(l, term, self.columns(l, term)[0], store)
        self.pass_on(l, term)

    def finish_y(self, l, term):
        p = self.p
        w = p.d.terms[term][0]
        y_in, _ = self.ins(l, term)
        self.y_wait(l, term)
        for index, here in self.groups(term):
            value = self.grad[w][(p.z, p.y) + index].astype(F32)
            for m in range(p.d.y_n - 1):
                value = value + y_in[(m, 0) + here].astype(F32)
            self.settle(l, term, index, value)
        self.pass_on(l, term)

    def settle(self, l, term, index, value):
        w = self.p.d.terms[term][0]
        if w == DOWN:
            self.result[w][(l,) + index] = value
        else:
            self.grad[w][(self.p.z, self.p.y) + index] = value.astype(BF)

    def s_copy(self, l, w, j, source):
        p, o = self.p, self.o
        return rcopy(
            self.grad[w].at[p.z, p.y, j], self.sp_in[w].at[l, source], o.rs_send.at[l, w, j], o.rs_recv.at[l, w, source], (p.r, j)
        )

    def out_copy(self, l, device):
        p, o = self.p, self.o
        return rcopy(
            self.grad[OUT].at[p.z, p.y], self.sp_in[OUT].at[l], o.rs_send.at[l, OUT, 0], o.rs_recv.at[l, OUT, 0], device
        )

    def keep(self, l, w, j, ref):
        d, result = self.p.d, self.result[w]
        if not d.whole_lanes:
            result[l, j] = ref[...].astype(F32)
        elif w == QKV:
            for i in range(3):
                result[l, i, :, j * d.dh : (j + 1) * d.dh] = ref[:, i * d.dh : (i + 1) * d.dh].astype(F32)
        else:
            for k in range(d.dp_n):
                whole, kept = up_columns(d, j, k)
                result[l, :, whole] = ref[:, kept].astype(F32)

    def pass_on(self, l, term):
        p = self.p
        w, first, last = p.d.terms[term]
        if w in (QKV, UP):
            for j in range(first, last):

                @pl.when(p.s == j)
                def _():
                    self.keep(l, w, j, self.grad[w].at[p.z, p.y, j])

                @pl.when(p.s != j)
                def _():
                    self.s_copy(l, w, j, p.s).start()

        elif w == OUT:
            _, source, stays = p.moved()

            @pl.when(stays)
            def _():
                self.result[w][l] = self.grad[w][p.z, p.y].astype(F32)

            @pl.when(jnp.logical_not(stays))
            def _():
                self.out_copy(l, source).start()

    def sent(self, l, w):
        p = self.p
        for term, (kind, first, last) in enumerate(p.d.terms):
            if kind != w:
                continue
            for k in range(1, p.d.y_n):
                self.y_copy(l, term, k).wait_send()
            if p.d.z_n > 1:

                def wait(inside):
                    for column in self.columns(l, term):
                        for way in range(3):
                            self.z_copy(l, term, column, *self.z_goals(inside)[way], way).wait_send()

                self.both(lambda: wait(True), lambda: wait(False))
        if w in (QKV, UP):
            for t in range(1, p.d.sp_n):
                self.s_copy(l, w, p.slot(t), p.s).wait_send()
        elif w == OUT:
            _, source, stays = p.moved()

            @pl.when(jnp.logical_not(stays))
            def _():
                self.out_copy(l, source).wait_send()

    def last(self, l, w):
        p = self.p
        if w in (QKV, UP):
            for j in range(p.d.sp_n):

                @pl.when(p.s != j)
                def _():
                    self.s_copy(l, w, j, j).wait_recv()
                    self.keep(l, w, j, self.sp_in[w].at[l, j])
        elif w == OUT:
            _, source, stays = p.moved()

            @pl.when(jnp.logical_not(stays))
            def _():
                self.out_copy(l, source).wait_recv()
                self.result[w][l] = self.sp_in[w][l].astype(F32)


def norm_back(v, d_out, gain):
    center = v - mean_of(v)
    inverse = lax.rsqrt(mean_of(center * center) + EPS)
    unit = center * inverse
    gain_term = jnp.sum(d_out * unit, axis=0, keepdims=True)
    e = d_out * gain
    back = (e - mean_of(e) - unit * mean_of(e * unit)) * inverse
    return back, gain_term


def attention_backward(d, o):
    tok = d.tok
    for i in range(d.sp_n):
        here = o.meta[0, i]
        blocks = range(max(0, i - d.back), i + 1)
        for h in range(d.heads):
            lanes = slice(h * HD, (h + 1) * HD)
            key_lanes = slice(d.dh + h * HD, d.dh + (h + 1) * HD)
            value_lanes = slice(2 * d.dh + h * HD, 2 * d.dh + (h + 1) * HD)
            query = o.qkv[here, :, :, lanes].reshape(tok, HD)
            grad = o.d_att[here, :, :, lanes].reshape(tok, HD)
            d_probs, inner = [], None
            for b in blocks:
                low = o.probs[h, d.pairs.index((i, b))].astype(F32)
                term = nt(grad, o.qkv[o.meta[0, b], :, :, value_lanes].reshape(tok, HD))
                d_probs.append(term)
                weighted = jnp.sum(low * term, axis=-1, keepdims=True)
                inner = weighted if inner is None else inner + weighted
            d_query = None
            for b, term in zip(blocks, d_probs):
                low = o.probs[h, d.pairs.index((i, b))]
                d_score = (low.astype(F32) * (term - inner)).astype(BF)
                step = nn(d_score, o.qkv[o.meta[0, b], :, :, key_lanes].reshape(tok, HD))
                d_query = step if d_query is None else d_query + step
                d_key, d_value = tn(d_score, query), tn(low, grad)
                if b == i:
                    o.d_keys[b, :, lanes] = d_key
                    o.d_values[b, :, lanes] = d_value
                else:
                    o.d_keys[b, :, lanes] += d_key
                    o.d_values[b, :, lanes] += d_value
            o.sorted_dqkv[i, :, :, lanes] = (d_query * HD ** (-0.5)).astype(BF).reshape(2, d.half, HD)
    for b in range(d.sp_n):
        shape = (2, d.half, d.dh)
        o.sorted_dqkv[b, :, :, d.dh : 2 * d.dh] = (o.d_keys[b] * HD ** (-0.5)).astype(BF).reshape(shape)
        o.sorted_dqkv[b, :, :, 2 * d.dh :] = o.d_values[b].astype(BF).reshape(shape)


def bwd_kernel(d, names, *refs):
    o = Refs()
    for name, ref in zip(names, refs):
        setattr(o, name, ref)
    p = Place(d)
    gather = Gather(p, o.ag_send, o.ag_recv)
    scatter = Scatter(p, o.part, o.near, o.far, o.near_send, o.near_recv, o.far_send, o.far_recv)
    small = SmallSum(p, o.gain_sum, o.sp_in, o.mid_a, o.z_in, o.mid_b, o.y_in, o.sp_sem, o.z_sem, o.y_sem)
    reduce = Reduce(p, o)
    loads = WEIGHTS + SAVED

    def load(name, l):
        ref = o.mid if name == "stream" else getattr(o, name)
        return pltpu.make_async_copy(getattr(o, "i_" + name).at[l], ref, o.load_sem.at[loads.index(name)])

    def refill(l, *which):
        if l > 0:
            for name in which:
                load(name, l - 1).start()

    def run(slot):
        for layer, term in BACKWARD_PLAN.get(slot, ()):
            reduce.step(layer, term)

    top = d.layers - 1
    for name in ("wdown", "slope", "wup", "hid", "xmid", "mid", "wout", "qkv", "probs", "att", "wqkv", "xin"):
        load(name, top).start()
    p.barrier()
    lay_out(d, o)
    o.gain_sum[...] = jnp.zeros_like(o.gain_sum)

    for half in range(2):

        def begin(rows):
            v = o.in_cotangent[half, rows].astype(F32)
            o.o_grad[half, rows] = v
            o.gl[p.s, half, rows] = v.astype(BF)

        row_loop(d.half, begin)
        gather.start(o.gl, half)
    tokens = d.sp_n * d.tok

    def rows_of(ref, n, count):
        part = ref[n * d.z_n // count : (n + 1) * d.z_n // count]
        return part.reshape(d.chunk, part.shape[-1])

    def weight_grad(out, left_ref, right_ref, count, width):
        for n in range(count):
            left = left_ref[:, :, :, n * d.chunk : (n + 1) * d.chunk].reshape(tokens, d.chunk)
            value = tn(left, right_ref[...].reshape(tokens, width)).astype(BF)
            zs = slice(n * d.z_n // count, (n + 1) * d.z_n // count)
            out[zs] = value.reshape((d.z_n // count,) + out.shape[1:])

    for l in reversed(range(d.layers)):
        gain_in = o.in_gains[2 * l : 2 * l + 1, :]
        gain_mid = o.in_gains[2 * l + 1 : 2 * l + 2, :]
        run("A%d" % l)
        load("wdown", l).wait()
        load("slope", l).wait()
        load("wup", l).wait()

        def pre_grad(pieces):
            block = pair(o.gl, pieces)
            for n in range(d.n_hid):
                cols = slice(n * d.chunk, (n + 1) * d.chunk)
                d_hidden = nt(block, rows_of(o.wdown, n, d.n_hid))
                put_pair(o.slope, pieces, cols, d_hidden * pair(o.slope, pieces, cols).astype(F32))

        def mid_grad(pieces):
            d_pre = pair(o.slope, pieces)
            for n in range(d.n_width):
                cols = slice(n * d.chunk, (n + 1) * d.chunk)
                put_pair(o.part, pieces, cols, nt(d_pre, rows_of(o.wup, n, d.n_width)))

        pre_grad(p.pieces(0))
        gather.near(o.gl)
        pre_grad(p.pieces(1))
        run("B%d" % l)

        @pl.loop(2, d.sp_n)
        def _(t):
            gather.far(o.gl, t)
            pre_grad(p.pieces(t))

            @pl.when(t > 2)
            def _():
                scatter.cross(t - 1)

            mid_grad(p.pieces(t))
            scatter.put(t)

        mid_grad(p.pieces(1))
        scatter.put(1)
        scatter.cross(d.sp_n - 1)
        mid_grad(p.pieces(0))
        gather.end(o.gl)
        refill(l, "wdown", "wup")
        load("hid", l).wait()
        run("C%d" % l)
        if l < top:
            reduce.sent(l + 1, DOWN)
        weight_grad(o.g_down, o.hid, o.gl, d.n_hid, d.width)
        run("D%d" % l)
        refill(l, "hid")
        load("mid", l).wait()

        def middle(half, rows):
            back, gain_term = norm_back(o.mid[half, rows], scatter.total(half, rows), gain_mid)
            o.gain_sum[2 * l + 1 : 2 * l + 2, :] += gain_term
            value = o.o_grad[half, rows] + back
            o.o_grad[half, rows] = value
            o.ml[p.s, half, rows] = value.astype(BF)

        for half in range(2):
            scatter.arrive(half)
            row_loop(d.half, functools.partial(middle, half))
            gather.start(o.ml, half)
            if half == 0:
                run("E%d" % l)
        scatter.end()
        load("stream", l).start()
        load("xmid", l).wait()
        run("F%d" % l)
        if l < top:
            reduce.sent(l + 1, UP)
        weight_grad(o.g_up, o.xmid, o.slope, d.n_width, d.hid)
        run("G%d" % l)
        refill(l, "xmid", "slope")
        load("wout", l).wait()

        def att_grad(pieces):
            weight = o.wout[...].reshape(d.dh, d.width)
            put_pair(o.d_att, pieces, slice(None), nt(pair(o.ml, pieces), weight))

        att_grad(p.pieces(0))
        gather.near(o.ml)
        att_grad(p.pieces(1))
        run("H%d" % l)

        @pl.loop(2, d.sp_n)
        def _(t):
            gather.far(o.ml, t)
            att_grad(p.pieces(t))

        gather.end(o.ml)
        refill(l, "wout")
        run("I%d" % l)
        load("qkv", l).wait()
        load("probs", l).wait()
        attention_backward(d, o)
        refill(l, "qkv", "probs")
        run("J%d" % l)
        load("wqkv", l).wait()

        def in_grad(pieces):
            blocks = []
            for slot, half in pieces:
                block = o.sorted_dqkv[o.meta[1, slot], half]
                o.d_qkv[slot, half] = block
                blocks.append(block)
            block = jnp.concatenate(blocks, axis=0)
            for n in range(d.n_width):
                cols = slice(n * d.chunk, (n + 1) * d.chunk)
                put_pair(o.part, pieces, cols, nt(block, rows_of(o.wqkv, n, d.n_width)))

        @pl.loop(2, d.sp_n)
        def _(t):
            in_grad(p.pieces(t))
            scatter.put(t)

            @pl.when(t > 2)
            def _():
                scatter.cross(t - 1)

        in_grad(p.pieces(1))
        scatter.put(1)
        scatter.cross(d.sp_n - 1)
        in_grad(p.pieces(0))
        run("K%d" % l)
        refill(l, "wqkv")
        load("att", l).wait()
        if l < top:
            reduce.sent(l + 1, OUT)
        value = tn(o.att[...].reshape(tokens, d.dh), o.ml[...].reshape(tokens, d.width)).astype(BF)
        o.g_out[...] = value.reshape((d.z_n, d.y_n, d.rows, d.width))
        run("L%d" % l)
        refill(l, "att")
        load("xin", l).wait()
        if l < top:
            reduce.sent(l + 1, QKV)
        weight_grad(o.g_qkv, o.xin, o.d_qkv, d.n_width, 3 * d.dh)
        run("M%d" % l)
        refill(l, "xin")
        load("stream", l).wait()

        def lower(half, rows):
            back, gain_term = norm_back(o.mid[half, rows], scatter.total(half, rows), gain_in)
            o.gain_sum[2 * l : 2 * l + 1, :] += gain_term
            value = o.o_grad[half, rows] + back
            o.o_grad[half, rows] = value
            if l > 0:
                o.gl[p.s, half, rows] = value.astype(BF)

        for half in range(2):
            scatter.arrive(half)
            row_loop(d.half, functools.partial(lower, half))
            if l > 0:
                gather.start(o.gl, half)
            if half == 0:
                run("N%d" % l)
        scatter.end()
        if l == 0:
            small.start(0)
        refill(l, "mid")

    run("O0")
    small.finish(0, o.mid_a)
    small.start(1)
    run("P0")
    small.finish(1, o.mid_b)
    small.start(2)
    run("Q0")
    small.finish(2, o.o_gains)
    for l in reversed(range(d.layers)):
        for w in (DOWN, UP, OUT, QKV):
            reduce.last(l, w)
    for w in (DOWN, UP, OUT, QKV):
        reduce.sent(0, w)


ANY = pl.BlockSpec(memory_space=pl.ANY)
VM = pl.BlockSpec(memory_space=pltpu.VMEM)
SM = pl.BlockSpec(memory_space=pltpu.SMEM)


def call(kernel, d, inputs, outputs, scratch, identity):
    names = [i[0] for i in inputs] + [i[0] for i in outputs] + [i[0] for i in scratch]
    results = pl.pallas_call(
        functools.partial(kernel, d, names),
        out_shape=[jax.ShapeDtypeStruct(i[2], i[3]) for i in outputs],
        in_specs=[i[1] for i in inputs],
        out_specs=[i[1] for i in outputs],
        scratch_shapes=[i[1] for i in scratch],
        compiler_params=pltpu.CompilerParams(
            collective_id=identity, has_side_effects=True, vmem_limit_bytes=62 * 1024 * 1024
        ),
        name=kernel.__name__,
    )(*[i[2] for i in inputs])
    return dict(zip([i[0] for i in outputs], results))


def shards(dp_n, sp_n, tokens, cotangent, w_qkv, w_out, w_up, w_down, gains, piece_order, doc_lengths):
    _, tok, width = tokens.shape
    layers, _, rows, _ = w_qkv.shape
    ff = w_up.shape[-1]
    d = Dims(dp_n, sp_n, layers, tok, width, ff, doc_lengths.shape[1])
    r, s = lax.axis_index("dp"), lax.axis_index("sp")

    own = gains.shape[-1]
    padded = jnp.zeros((8, width), F32)
    padded = lax.dynamic_update_slice(
        padded, gains.reshape(2 * layers, own).astype(F32), (0, (r * sp_n + s) * own)
    )
    lay_scratch = []
    if d.whole_lanes:
        lay_scratch = [
            ("in_qkv", pltpu.VMEM((layers, sp_n, rows, 3 * d.dh), BF)),
            ("in_up", pltpu.VMEM((layers, sp_n, rows, d.hid), BF)),
        ]
        given = [("raw_qkv", VM, w_qkv), ("raw_up", VM, w_up)]
    else:
        in_qkv = w_qkv.reshape(layers, 3, rows, sp_n, d.dh).transpose(0, 3, 2, 1, 4)
        in_up = w_up.reshape(layers, rows, dp_n, sp_n, d.hid_own).transpose(0, 3, 1, 2, 4)
        given = [
            ("in_qkv", ANY, in_qkv.reshape(layers, sp_n, rows, 3 * d.dh)),
            ("in_up", ANY, in_up.reshape(layers, sp_n, rows, d.hid)),
        ]

    saved, weights = saved_shapes(d), weight_shapes(d)
    dma = pltpu.SemaphoreType.DMA
    fwd = call(
        fwd_kernel,
        d,
        [
            ("in_order", SM, piece_order),
            ("in_lengths", SM, doc_lengths),
            ("in_tokens", VM, tokens.reshape(2, d.half, width)),
            ("in_gains", VM, padded),
            ("in_out", ANY, w_out),
            ("in_down", ANY, w_down),
        ]
        + given,
        [("o_output", VM, (2, d.half, width), BF), ("o_gains", VM, (8, width), F32)]
        + [("o_" + n, ANY, (layers,) + weights[n][0], BF) for n in WEIGHTS]
        + [("o_" + n, ANY, (layers,) + saved[n][0], saved[n][1]) for n in SAVED],
        [(n, pltpu.VMEM((layers,) + weights[n][0], BF)) for n in WEIGHTS]
        + [(n, pltpu.VMEM((1 if n in ONCE else layers,) + saved[n][0], saved[n][1])) for n in SAVED]
        + [
            ("sorted_att", pltpu.VMEM(saved["att"][0], BF)),
            ("meta", pltpu.SMEM((3, max(sp_n, d.docs)), jnp.int32)),
        ]
        + lay_scratch
        + small_scratch(d)
        + comm_scratch(d)
        + [
            ("s_send", dma((layers, 4, sp_n))),
            ("s_recv", dma((layers, 4, sp_n))),
            ("own_sem", dma((layers, 4))),
            ("b_send", dma((layers, len(d.pieces), d.z_n, d.y_n, 1 + d.y_n))),
            ("b_recv", dma((layers, len(d.pieces), d.z_n, d.y_n))),
            ("w_sem", dma((layers, 4))),
            ("save_sem", dma((layers, len(SAVED)))),
        ],
        0,
    )
    kinds = ("qkv", "out", "up", "down")
    blocks = [d.block_shape(w) for w in range(4)]
    results = [(layers,) + b for b in blocks]
    if d.whole_lanes:
        results[QKV], results[UP] = w_qkv.shape, w_up.shape
    bwd = call(
        bwd_kernel,
        d,
        [("in_order", SM, piece_order), ("in_lengths", SM, doc_lengths), ("in_cotangent", VM, cotangent.reshape(2, d.half, width)), ("in_gains", VM, fwd["o_gains"])]
        + [("i_" + n, ANY, fwd["o_" + n]) for n in WEIGHTS + SAVED],
        [("o_grad", VM, (2, d.half, width), F32), ("o_gains", VM, (8, width), F32)]
        + [("o_" + k, VM, shape, F32) for k, shape in zip(kinds, results)],
        [(n, pltpu.VMEM(weights[n][0], BF)) for n in WEIGHTS]
        + [(n, pltpu.VMEM(saved[n][0], saved[n][1])) for n in SAVED if n != "stream"]
        + [
            ("gl", pltpu.VMEM((sp_n, 2, d.half, width), BF)),
            ("ml", pltpu.VMEM((sp_n, 2, d.half, width), BF)),
            ("d_att", pltpu.VMEM((sp_n, 2, d.half, d.dh), BF)),
            ("sorted_dqkv", pltpu.VMEM((sp_n, 2, d.half, 3 * d.dh), BF)),
            ("d_qkv", pltpu.VMEM((sp_n, 2, d.half, 3 * d.dh), BF)),
            ("d_keys", pltpu.VMEM((sp_n, tok, d.dh), F32)),
            ("d_values", pltpu.VMEM((sp_n, tok, d.dh), F32)),
            ("gain_sum", pltpu.VMEM((8, width), F32)),
            ("meta", pltpu.SMEM((3, max(sp_n, d.docs)), jnp.int32)),
        ]
        + [("g_" + k, pltpu.VMEM((d.z_n, d.y_n) + b, BF)) for k, b in zip(kinds, blocks)]
        + [i for l in range(layers) for t in range(len(d.terms)) for i in term_scratch(d, l, t)]
        + [("x_" + k, pltpu.VMEM((layers,) + b, BF)) for k, b in zip(kinds[:3], blocks)]
        + small_scratch(d)
        + comm_scratch(d)
        + [
            ("load_sem", dma((len(WEIGHTS + SAVED),))),
            ("ry_send", dma((layers, len(d.terms), d.y_n))),
            ("ry_recv", dma((layers, len(d.terms), d.y_n))),
            ("rz_send", dma((layers, len(d.terms), d.y_n, 3))),
            ("rz_recv", dma((layers, len(d.terms), d.y_n, 5))),
            ("rs_send", dma((layers, 4, sp_n))),
            ("rs_recv", dma((layers, 4, sp_n))),
        ],
        1,
    )
    grad_qkv, grad_up = bwd["o_qkv"], bwd["o_up"]
    if not d.whole_lanes:
        grad_qkv = grad_qkv.reshape(layers, sp_n, rows, 3, d.dh).transpose(0, 3, 2, 1, 4).reshape(w_qkv.shape)
        grad_up = grad_up.reshape(layers, sp_n, rows, dp_n, d.hid_own).transpose(0, 2, 3, 1, 4).reshape(w_up.shape)
    grad_gains = lax.dynamic_slice(bwd["o_gains"], (0, (r * sp_n + s) * own), (2 * layers, own))
    return (
        fwd["o_output"].reshape(tokens.shape),
        bwd["o_grad"].reshape(tokens.shape),
        grad_qkv,
        bwd["o_out"],
        grad_up,
        bwd["o_down"],
        grad_gains.reshape(gains.shape),
    )


def solution(mesh):
    return jax.shard_map(
        functools.partial(shards, mesh.shape["dp"], mesh.shape["sp"]),
        mesh=mesh,
        in_specs=(
            P("dp", "sp", None),
            P("dp", "sp", None),
            P(None, None, ("dp", "sp"), None),
            P(None, ("dp", "sp"), None),
            P(None, ("dp", "sp"), None),
            P(None, ("dp", "sp"), None),
            P(None, None, ("dp", "sp")),
            P("dp", None),
            P("dp", None),
        ),
        out_specs=(
            P("dp", "sp", None),
            P("dp", "sp", None),
            P(None, None, ("dp", "sp"), None),
            P(None, ("dp", "sp"), None),
            P(None, ("dp", "sp"), None),
            P(None, ("dp", "sp"), None),
            P(None, None, ("dp", "sp")),
        ),
        check_vma=False,
    )
```

```python
import functools

import jax
import jax.numpy as jnp
from jax import lax
from jax.experimental import pallas as pl
from jax.experimental.pallas import tpu as pltpu
from jax.sharding import PartitionSpec as P

HEADS = 8
HD = 128
EPS = 1e-05
MASKED = -1e30
MESH = pl.DeviceIdType.MESH
BF = jnp.bfloat16
F32 = jnp.float32
AXES = ("dp", "sp")
QKV, OUT, UP, DOWN = range(4)
Q0, Q1, O0, U0, U1, D0, D1 = range(7)
SPREAD, OWN, START_Z, START_Y, RELAY_1, INNER, OUTER, RELAY_3, LATE_START, LATE_ON, LATE_END = range(11)


def nn(a, b):
    return lax.dot_general(a, b, (((1,), (0,)), ((), ())), preferred_element_type=F32)


def nt(a, b):
    return lax.dot_general(a, b, (((1,), (1,)), ((), ())), preferred_element_type=F32)


def tn(a, b):
    return lax.dot_general(a, b, (((0,), (0,)), ((), ())), preferred_element_type=F32)


FORWARD_PLAN = {
    0: ((OWN, 0, 3), (START_Z, 0, 4), (SPREAD, 1, 3), (OWN, 0, 0), (LATE_START, 0, 1), (START_Y, 0, 0), (START_Z, 0, 0), (OWN, 0, 1), (START_Z, 0, 1),),
    1: ((RELAY_1, 0, 0), (OWN, 0, 2), (OUTER, 0, 0), (INNER, 0, 0), (START_Y, 0, 5),),
    2: ((START_Z, 0, 3), (LATE_START, 0, 0), (RELAY_3, 0, 0), (RELAY_1, 0, 1), (START_Y, 0, 2), (SPREAD, 1, 0),),
    3: ((START_Z, 0, 2), (START_Y, 0, 1), (INNER, 0, 1), (INNER, 0, 4), (OWN, 1, 3), (INNER, 0, 3), (OUTER, 0, 1),),
    4: ((RELAY_3, 0, 1), (SPREAD, 1, 1), (RELAY_1, 0, 2), (START_Y, 0, 3),),
    5: ((START_Z, 0, 5), (SPREAD, 1, 2), (LATE_ON, 0, 0), (RELAY_1, 0, 4),),
    6: ((OWN, 1, 2), (START_Y, 1, 4), (START_Y, 1, 5), (OUTER, 0, 4), (OWN, 1, 1), (START_Z, 1, 1), (INNER, 0, 2), (RELAY_1, 0, 3),),
    7: ((RELAY_3, 0, 2), (RELAY_1, 0, 5), (INNER, 0, 5), (OUTER, 0, 3),),
    8: ((OUTER, 0, 2), (RELAY_3, 0, 3), (RELAY_3, 0, 4), (START_Y, 0, 4), (OWN, 1, 0), (START_Y, 1, 0),),
    9: ((START_Y, 1, 3), (START_Z, 1, 0), (RELAY_1, 1, 0),),
    10: ((RELAY_3, 0, 5), (START_Z, 1, 4), (OUTER, 0, 5), (START_Z, 1, 5),),
    11: ((INNER, 1, 0), (RELAY_3, 1, 0), (START_Z, 1, 2), (OUTER, 1, 0),),
    12: ((INNER, 1, 4), (RELAY_1, 1, 1), (START_Z, 1, 3), (OUTER, 1, 4), (START_Y, 1, 1), (LATE_ON, 0, 1), (RELAY_1, 1, 4), (RELAY_1, 1, 5),),
    14: ((INNER, 1, 2), (RELAY_1, 1, 2),),
    15: ((OUTER, 1, 1), (INNER, 1, 1), (LATE_END, 0, 0), (RELAY_3, 1, 1), (RELAY_1, 1, 3),),
    16: ((RELAY_3, 1, 4), (INNER, 1, 5), (INNER, 1, 3),),
    17: ((OUTER, 1, 2), (START_Y, 1, 2), (OUTER, 1, 5), (RELAY_3, 1, 2), (OUTER, 1, 3),),
    18: ((RELAY_3, 1, 5), (RELAY_3, 1, 3),),
}
BACKWARD_PLAN = {
    3: ((1, D1), (1, D0),),
    6: ((1, U0), (1, U1),),
    7: ((1, D0),),
    10: ((1, D0),),
    11: ((1, U0),),
    12: ((1, Q0),),
    13: ((1, D1), (1, Q1),),
    15: ((1, U0), (1, D1), (1, U0), (1, O0), (1, U1), (1, Q0), (1, D0),),
    16: ((1, D1),),
    17: ((0, D1),),
    18: ((1, Q1), (1, U1), (1, U1), (1, Q0),),
    19: ((0, D0), (1, O0), (1, Q1),),
    20: ((1, Q1), (1, O0),),
    21: ((0, U1), (0, D1),),
    22: ((1, O0), (0, D0),),
    23: ((1, Q0), (0, D1),),
    24: ((0, U1),),
    25: ((0, D0), (0, D1), (0, U0),),
    26: ((0, Q1), (0, O0), (0, U1), (0, U0),),
    27: ((0, Q0), (0, Q1), (0, D0), (0, Q1), (0, Q0), (0, U0),),
    28: ((0, O0),),
    29: ((0, U0), (0, U1), (0, Q1), (0, O0),),
    30: ((0, Q0), (0, O0), (0, Q0),),
}


class Dims:
    def __init__(self, dp_n, sp_n, layers, tok, width, ff, docs):
        self.dp_n, self.sp_n, self.layers, self.tok, self.width = dp_n, sp_n, layers, tok, width
        self.z_n = 4 if dp_n % 4 == 0 else 1
        self.y_n = dp_n // self.z_n
        self.x_n = sp_n // 2
        self.rows = width // (dp_n * sp_n)
        self.heads = HEADS // sp_n
        self.dh = width // sp_n
        self.hid = ff // sp_n
        self.hid_own = ff // (dp_n * sp_n)
        self.docs = docs
        self.whole_lanes = self.hid_own % 128 == 0
        self.chunk = min(256, tok)
        self.half = tok // 2
        self.n_width = width // self.chunk
        self.n_hid = self.hid // self.chunk
        self.back = self.x_n
        half, part = sp_n // 2, self.hid_own // 2
        self.pieces = (
            (QKV, 0, sp_n, False),
            (OUT, 0, self.rows, False),
            (UP, 0, half, False),
            (UP, half, sp_n, False),
            (DOWN, 0, part, False),
            (DOWN, part, self.hid_own, True),
        )
        self.terms = (
            (QKV, 0, half),
            (QKV, half, sp_n),
            (OUT, 0, self.rows),
            (UP, 0, half),
            (UP, half, sp_n),
            (DOWN, 0, part),
            (DOWN, part, self.hid_own),
        )
        self.z_first = [(Q1,)] + [(D1,)] * (layers - 1)
        self.pairs = [(i, b) for i in range(sp_n) for b in range(max(0, i - self.back), i + 1)]

    def block_shape(self, which):
        return {
            QKV: (self.sp_n, self.rows, 3 * self.dh),
            OUT: (self.rows, self.width),
            UP: (self.sp_n, self.rows, self.hid),
            DOWN: (self.hid_own, self.width),
        }[which]


class Place:
    def __init__(self, d):
        self.d = d
        self.r = lax.axis_index("dp")
        self.s = lax.axis_index("sp")
        self.z, self.y = self.r // d.y_n, self.r % d.y_n
        self.x, self.c = self.s // 2, self.s % 2
        self.partner = self.x * 2 + (self.c + 1) % 2

    def slot(self, step):
        return ((self.x + step // 2) % self.d.x_n) * 2 + (self.c + step % 2) % 2

    def pieces(self, step):
        if isinstance(step, int) and step < 2:
            return (self.slot(step), 0), (self.slot(step), 1)
        first = step // 2 * 2
        return (self.slot(first), step % 2), (self.slot(first + 1), step % 2)

    def zpeer(self, dz):
        return (self.z + dz) % self.d.z_n

    def ypeer(self, dy):
        return (self.y + dy) % self.d.y_n

    def line(self):
        high = self.z // 2
        inside = ((self.z + 1) // 2) % 2
        first = inside * 3 * high + (1 - inside) * (1 + high)
        return inside == 1, (self.z, first, 2 - high, 3 - 3 * high)

    def dev(self, z, y):
        return (z * self.d.y_n + y, self.s)

    def moved(self):
        d = self.d
        flat = self.r * d.sp_n + self.s
        goal = (flat % d.dp_n, flat // d.dp_n)
        mine = self.s * d.dp_n + self.r
        source = (mine // d.sp_n, mine % d.sp_n)
        stays = flat == mine
        return goal, source, stays

    def barrier(self):
        d = self.d
        sem = pltpu.get_barrier_semaphore()
        peers = [(self.r, self.slot(t)) for t in range(1, d.sp_n)]
        peers += [self.dev(self.zpeer(k), self.y) for k in range(1, d.z_n)]
        peers += [self.dev(self.z, self.ypeer(k)) for k in range(1, d.y_n)]
        for peer in peers:
            pl.semaphore_signal(sem, inc=1, device_id=peer, device_id_type=MESH)
        goal, source, stays = self.moved()

        @pl.when(jnp.logical_not(stays))
        def _():
            pl.semaphore_signal(sem, inc=1, device_id=goal, device_id_type=MESH)
            pl.semaphore_signal(sem, inc=1, device_id=source, device_id_type=MESH)
            pl.semaphore_wait(sem, len(peers) + 2)

        @pl.when(stays)
        def _():
            pl.semaphore_wait(sem, len(peers))


def rcopy(src, dst, send, recv, device):
    return pltpu.make_async_remote_copy(
        src_ref=src, dst_ref=dst, send_sem=send, recv_sem=recv, device_id=device, device_id_type=MESH
    )


def pair(ref, pieces, *cols):
    return jnp.concatenate([ref[(slot, half) + (slice(None),) + cols] for slot, half in pieces], axis=0)


def put_pair(ref, pieces, cols, value):
    rows = value.shape[0] // 2
    for k, (slot, half) in enumerate(pieces):
        ref[slot, half, :, cols] = value[k * rows : (k + 1) * rows].astype(ref.dtype)


class Gather:
    def __init__(self, p, send, recv):
        self.p, self.send, self.recv = p, send, recv

    def copy(self, buf, slot, half, way, goal):
        block = buf.at[slot, half]
        return rcopy(block, block, self.send.at[way, goal, half], self.recv.at[slot, half], (self.p.r, goal))

    def start(self, buf, half):
        p = self.p
        for dx in range(1, p.d.x_n):
            self.copy(buf, p.s, half, 0, p.slot(2 * dx)).start()
        self.copy(buf, p.s, half, 0, p.partner).start()

    def onward(self, buf, slot, half):
        block = buf.at[slot, half]
        p = self.p
        return rcopy(block, block, self.send.at[1, slot, half], self.recv.at[slot, half], (p.r, p.partner))

    def arrived(self, buf, slot, half):
        self.copy(buf, slot, half, 0, self.p.partner).wait_recv()

    def near(self, buf):
        for half in range(2):
            self.arrived(buf, self.p.partner, half)

    def through(self, buf, step):
        first, _ = self.p.pieces(step)
        self.arrived(buf, *first)
        self.onward(buf, *first).start()

    def rest(self, buf):
        self.near(buf)
        for step in range(2, self.p.d.sp_n):
            self.arrived(buf, *self.p.pieces(step)[1])

    def far(self, buf, step):
        first, second = self.p.pieces(step)
        self.arrived(buf, *first)
        self.onward(buf, *first).start()
        self.arrived(buf, *second)

    def end(self, buf):
        p = self.p
        for half in range(2):
            for dx in range(1, p.d.x_n):
                self.copy(buf, p.s, half, 0, p.slot(2 * dx)).wait_send()
                self.onward(buf, p.slot(2 * dx), half).wait_send()
            self.copy(buf, p.s, half, 0, p.partner).wait_send()


class Scatter:
    def __init__(self, p, part, near, far, near_send, near_recv, far_send, far_recv):
        self.p, self.part, self.near, self.far = p, part, near, far
        self.near_send, self.near_recv, self.far_send, self.far_recv = near_send, near_recv, far_send, far_recv

    def near_copy(self, x, half):
        p = self.p
        return rcopy(
            self.part.at[x * 2 + (p.c + 1) % 2, half],
            self.near.at[x, half],
            self.near_send.at[x, half],
            self.near_recv.at[x, half],
            (p.r, p.partner),
        )

    def far_copy(self, x, half, source):
        p = self.p
        goal = x * 2 + p.c
        return rcopy(
            self.part.at[goal, half],
            self.far.at[source, half],
            self.far_send.at[x, half],
            self.far_recv.at[source, half],
            (p.r, goal),
        )

    def put(self, step):
        if isinstance(step, int):
            if step == 1:
                for half in range(2):
                    self.near_copy(self.p.x, half).start()
        else:
            self.near_copy(self.p.slot(step // 2 * 2) // 2, step % 2).start()

    def cross(self, step):
        p = self.p
        slot, half = p.slot(step // 2 * 2), step % 2
        x = slot // 2
        self.near_copy(x, half).wait_recv()
        size = min(64, p.d.half)

        @pl.loop(0, p.d.half // size)
        def _(i):
            rows = pl.ds(pl.multiple_of(i * size, size), size)
            both = self.part[slot, half, rows].astype(F32) + self.near[x, half, rows].astype(F32)
            self.part[slot, half, rows] = both.astype(BF)

        self.far_copy(x, half, p.x).start()

    def arrive(self, half):
        p = self.p
        self.near_copy(p.x, half).wait_recv()
        for dx in range(1, p.d.x_n):
            x = (p.x + dx) % p.d.x_n
            self.far_copy(x, half, x).wait_recv()

    def total(self, half, rows):
        p = self.p
        value = self.part[p.s, half, rows].astype(F32) + self.near[p.x, half, rows].astype(F32)
        for dx in range(1, p.d.x_n):
            value = value + self.far[(p.x + dx) % p.d.x_n, half, rows].astype(F32)
        return value

    def end(self):
        p = self.p
        for half in range(2):
            for dx in range(p.d.x_n):
                x = (p.x + dx) % p.d.x_n
                self.near_copy(x, half).wait_send()
                if dx:
                    self.far_copy(x, half, p.x).wait_send()


class SmallSum:
    def __init__(self, p, first, sp_in, mid_a, z_in, mid_b, y_in, sp_sem, z_sem, y_sem):
        self.p = p
        self.bufs = ((first, sp_in, sp_sem), (mid_a, z_in, z_sem), (mid_b, y_in, y_sem))

    def plan(self, stage):
        p = self.p
        if stage == 0:
            return p.s, [(p.slot(t), (p.r, p.slot(t))) for t in range(1, p.d.sp_n)]
        if stage == 1:
            return p.z, [(p.zpeer(k), p.dev(p.zpeer(k), p.y)) for k in range(1, p.d.z_n)]
        return p.y, [(p.ypeer(k), p.dev(p.z, p.ypeer(k))) for k in range(1, p.d.y_n)]

    def start(self, stage):
        src, dst, sem = self.bufs[stage]
        own, peers = self.plan(stage)
        for index, device in peers:
            rcopy(src, dst.at[own], sem.at[0, index], sem.at[1, own], device).start()

    def finish(self, stage, result):
        src, dst, sem = self.bufs[stage]
        own, peers = self.plan(stage)
        value = src[...]
        for index, device in peers:
            rcopy(src, dst.at[index], sem.at[0, index], sem.at[1, index], device).wait_recv()
            value = value + dst[index]
        result[...] = value
        for index, device in peers:
            rcopy(src, dst.at[own], sem.at[0, index], sem.at[1, own], device).wait_send()


def small_scratch(d):
    return [
        ("sp_in", pltpu.VMEM((d.sp_n, 8, d.width), F32)),
        ("mid_a", pltpu.VMEM((8, d.width), F32)),
        ("z_in", pltpu.VMEM((d.z_n, 8, d.width), F32)),
        ("mid_b", pltpu.VMEM((8, d.width), F32)),
        ("y_in", pltpu.VMEM((d.y_n, 8, d.width), F32)),
        ("sp_sem", pltpu.SemaphoreType.DMA((2, d.sp_n))),
        ("z_sem", pltpu.SemaphoreType.DMA((2, d.z_n))),
        ("y_sem", pltpu.SemaphoreType.DMA((2, d.y_n))),
    ]


def comm_scratch(d):
    return [
        ("part", pltpu.VMEM((d.sp_n, 2, d.half, d.width), BF)),
        ("near", pltpu.VMEM((d.x_n, 2, d.half, d.width), BF)),
        ("far", pltpu.VMEM((d.x_n, 2, d.half, d.width), BF)),
        ("ag_send", pltpu.SemaphoreType.DMA((2, d.sp_n, 2))),
        ("ag_recv", pltpu.SemaphoreType.DMA((d.sp_n, 2))),
        ("near_send", pltpu.SemaphoreType.DMA((d.x_n, 2))),
        ("near_recv", pltpu.SemaphoreType.DMA((d.x_n, 2))),
        ("far_send", pltpu.SemaphoreType.DMA((d.x_n, 2))),
        ("far_recv", pltpu.SemaphoreType.DMA((d.x_n, 2))),
    ]


def term_scratch(d, l, term):
    w, first, last = d.terms[term]
    block = (last - first,) + d.block_shape(w)[1:]
    z_first = term in d.z_first[l]
    y_shape = (max(1, d.y_n - 1), 1 if z_first else d.z_n) + block
    z_shape = (5, d.y_n if z_first else 1) + block
    return [
        ("y_in_%d_%d" % (l, term), pltpu.VMEM(y_shape, BF)),
        ("z_in_%d_%d" % (l, term), pltpu.VMEM(z_shape, BF)),
    ]


SAVED = ("xin", "qkv", "att", "probs", "xmid", "hid", "slope", "stream", "mid")
ONCE = ("qkv", "att", "probs", "hid", "slope")
WEIGHTS = ("wqkv", "wout", "wup", "wdown")


def saved_shapes(d):
    full = (d.sp_n, 2, d.half)
    return {
        "xin": (full + (d.width,), BF),
        "qkv": (full + (3 * d.dh,), BF),
        "att": (full + (d.dh,), BF),
        "probs": ((d.heads, len(d.pairs), d.tok, d.tok), BF),
        "xmid": (full + (d.width,), BF),
        "hid": (full + (d.hid,), BF),
        "slope": (full + (d.hid,), BF),
        "stream": ((2, d.half, d.width), F32),
        "mid": ((2, d.half, d.width), F32),
    }


def weight_shapes(d):
    return {name: ((d.z_n, d.y_n) + d.block_shape(i), BF) for i, name in enumerate(WEIGHTS)}


class Fetch:
    def __init__(self, p, o):
        self.p, self.o = p, o
        self.full = (o.wqkv, o.wout, o.wup, o.wdown)

    def spread(self, l, w):
        p, o = self.p, self.o
        own = self.full[w].at[l, p.z, p.y]
        if w in (QKV, UP):
            src = o.in_qkv if w == QKV else o.in_up
            for t in range(1, p.d.sp_n):
                j = p.slot(t)
                rcopy(src.at[l, j], own.at[p.s], o.s_send.at[l, w, j], o.s_recv.at[l, w, p.s], (p.r, j)).start()
            pltpu.make_async_copy(src.at[l, p.s], own.at[p.s], o.own_sem.at[l, w]).start()
        elif w == DOWN:
            pltpu.make_async_copy(o.in_down.at[l], own, o.own_sem.at[l, w]).start()
        else:
            goal, _, stays = p.moved()

            @pl.when(stays)
            def _():
                pltpu.make_async_copy(o.in_out.at[l], own, o.own_sem.at[l, w]).start()

            @pl.when(jnp.logical_not(stays))
            def _():
                there = self.full[w].at[l, goal[0] // p.d.y_n, goal[0] % p.d.y_n]
                rcopy(o.in_out.at[l], there, o.s_send.at[l, w, 0], o.s_recv.at[l, w, 0], goal).start()

    def own(self, l, w):
        p, o = self.p, self.o
        own = self.full[w].at[l, p.z, p.y]
        if w in (QKV, UP):
            src = o.in_qkv if w == QKV else o.in_up
            pltpu.make_async_copy(src.at[l, p.s], own.at[p.s], o.own_sem.at[l, w]).wait()
            for t in range(1, p.d.sp_n):
                j = p.slot(t)
                rcopy(src.at[l, j], own.at[j], o.s_send.at[l, w, j], o.s_recv.at[l, w, j], (p.r, j)).wait_recv()
        elif w == DOWN:
            pltpu.make_async_copy(o.in_down.at[l], own, o.own_sem.at[l, w]).wait()
        else:
            goal, _, stays = p.moved()

            @pl.when(stays)
            def _():
                pltpu.make_async_copy(o.in_out.at[l], own, o.own_sem.at[l, w]).wait()

            @pl.when(jnp.logical_not(stays))
            def _():
                rcopy(o.in_out.at[l], own, o.s_send.at[l, w, 0], o.s_recv.at[l, w, 0], goal).wait_recv()

    def block(self, l, piece, z, y):
        w, first, last, _ = self.p.d.pieces[piece]
        return self.full[w].at[l, z, y, first:last]

    def columns(self, piece):
        p = self.p
        if self.p.d.pieces[piece][3]:
            return [p.y] + [p.ypeer(m) for m in range(1, p.d.y_n)]
        return [p.y]

    def copy(self, l, piece, z, y, way, device):
        o = self.o
        block = self.block(l, piece, z, y)
        return rcopy(block, block, o.b_send.at[l, piece, z, y, way], o.b_recv.at[l, piece, z, y], device)

    def arrived(self, l, piece, z, y):
        self.copy(l, piece, z, y, 0, (self.p.r, self.p.s)).wait_recv()

    def along_z(self, l, piece, role, y, act):
        p = self.p
        if p.d.z_n == 1 or role == 3:
            return
        inside, at = p.line()
        z = at[role]

        @pl.when(inside)
        def _():
            for way, goal in enumerate(((at[1], at[2]), (at[2], at[3]), (at[1],))[role]):
                act(self.copy(l, piece, z, y, way, p.dev(goal, p.y)))

        if role == 0:

            @pl.when(jnp.logical_not(inside))
            def _():
                act(self.copy(l, piece, z, y, 0, p.dev(at[1], p.y)))

    def along_y(self, l, piece, role, act):
        p = self.p
        z = p.line()[1][role]
        for m in range(1, p.d.y_n):
            act(self.copy(l, piece, z, p.y, 1 + m, p.dev(p.z, p.ypeer(m))))

    def start_z(self, l, *pieces):
        for piece in pieces:
            self.along_z(l, piece, 0, self.p.y, lambda c: c.start())

    def start_y(self, l, *pieces):
        for piece in pieces:
            self.along_y(l, piece, 0, lambda c: c.start())

    def inner(self, l, *pieces):
        if self.p.d.z_n > 1:

            @pl.when(self.p.line()[0])
            def _():
                for piece in pieces:
                    self.relay(l, piece, 2)

    def outer(self, l, *pieces):
        if self.p.d.z_n > 1:

            @pl.when(jnp.logical_not(self.p.line()[0]))
            def _():
                for piece in pieces:
                    self.relay(l, piece, 2)

    def relay(self, l, piece, *roles):
        p = self.p
        cross_first = p.d.pieces[piece][3]
        at = p.line()[1]
        for role in roles:
            if role == 1 and cross_first:
                for y in self.columns(piece)[1:]:
                    self.arrived(l, piece, p.z, y)
                    self.along_z(l, piece, 0, y, lambda c: c.start())
            if p.d.z_n == 1:
                continue
            for y in self.columns(piece):
                self.arrived(l, piece, at[role], y)
                self.along_z(l, piece, role, y, lambda c: c.start())
            if not cross_first:
                self.along_y(l, piece, role, lambda c: c.start())

    def ready(self, l, *pieces):
        p = self.p
        for piece in pieces:
            if not p.d.pieces[piece][3]:
                for role in range(4 if p.d.z_n > 1 else 1):
                    for m in range(1, p.d.y_n):
                        self.arrived(l, piece, p.line()[1][role], p.ypeer(m))

    def save(self, l, w):
        return pltpu.make_async_copy(self.full[w].at[l], self.o.w_save[w].at[l], self.o.w_sem.at[l, w])

    def end(self):
        p, o = self.p, self.o
        for l in range(p.d.layers):
            for w in range(4):
                own = self.full[w].at[l, p.z, p.y]
                if w in (QKV, UP):
                    src = o.in_qkv if w == QKV else o.in_up
                    for t in range(1, p.d.sp_n):
                        j = p.slot(t)
                        rcopy(src.at[l, j], own.at[p.s], o.s_send.at[l, w, j], o.s_recv.at[l, w, p.s], (p.r, j)).wait_send()
                elif w == OUT:
                    goal, _, stays = p.moved()

                    @pl.when(jnp.logical_not(stays))
                    def _():
                        rcopy(o.in_out.at[l], own, o.s_send.at[l, w, 0], o.s_recv.at[l, w, 0], goal).wait_send()

                self.save(l, w).wait()
            for piece in range(len(p.d.pieces)):
                for role in range(4 if p.d.z_n > 1 else 1):
                    for y in self.columns(piece):
                        self.along_z(l, piece, role, y, lambda c: c.wait_send())
                    if role == 0 or not p.d.pieces[piece][3]:
                        self.along_y(l, piece, role, lambda c: c.wait_send())


class Refs:
    pass


def mean_of(v):
    return jnp.mean(v, axis=-1, keepdims=True)


def norm_rows(v, gain):
    center = v - mean_of(v)
    return center * lax.rsqrt(mean_of(center * center) + EPS) * gain


def row_loop(tok, body, step=32):
    step = min(step, tok)

    @pl.loop(0, tok // step, unroll=True)
    def _(i):
        body(pl.ds(pl.multiple_of(i * step, step), step))


def lay_out(d, o):
    for i in range(d.sp_n):
        where = jnp.int32(0)
        for j in range(1, d.sp_n):
            where = jnp.where(o.in_order[0, j] == i, j, where)
        o.meta[0, i] = where
        o.meta[1, i] = o.in_order[0, i]
    start = jnp.int32(0)
    for b in range(d.docs):
        o.meta[2, b] = start
        start = start + o.in_lengths[0, b]


def up_columns(d, j, k):
    first = (k * d.sp_n + j) * d.hid_own
    return slice(first, first + d.hid_own), slice(k * d.hid_own, (k + 1) * d.hid_own)


def attention_forward(d, o, l):
    tok = d.tok
    slopes = []
    for h in range(d.heads):
        head = (lax.axis_index("sp") * d.heads + (h + 1)).astype(F32)
        slopes.append(jnp.exp2(jnp.full((1, 1), -8.0 / HEADS, F32) * head))
    for i in range(d.sp_n):
        here = o.meta[0, i]
        pos = i * tok + lax.broadcasted_iota(jnp.int32, (tok, 1), 0)
        start = jnp.zeros((tok, 1), jnp.int32)
        for b in range(1, d.docs):
            start = jnp.where(pos >= o.meta[2, b], o.meta[2, b], start)
        blocks = range(max(0, i - d.back), i + 1)
        for h in range(d.heads):
            lanes = slice(h * HD, (h + 1) * HD)
            query = o.qkv[0, here, :, :, lanes].reshape(tok, HD)
            scores = []
            for b in blocks:
                keys = o.qkv[0, o.meta[0, b], :, :, d.dh + h * HD : d.dh + (h + 1) * HD].reshape(tok, HD)
                key_pos = b * tok + lax.broadcasted_iota(jnp.int32, (tok, tok), 1)
                query_pos = i * tok + lax.broadcasted_iota(jnp.int32, (tok, tok), 0)
                score = nt(query, keys) * HD ** (-0.5) + slopes[h] * (key_pos - query_pos).astype(F32)
                allowed = key_pos >= start
                if b == i:
                    allowed = allowed & (key_pos <= query_pos)
                scores.append(jnp.where(allowed, score, MASKED))
            top = scores[0].max(axis=-1, keepdims=True)
            for score in scores[1:]:
                top = jnp.maximum(top, score.max(axis=-1, keepdims=True))
            expo = [jnp.exp(score - top) for score in scores]
            total = expo[0].sum(axis=-1, keepdims=True)
            for part in expo[1:]:
                total = total + part.sum(axis=-1, keepdims=True)
            inverse = 1.0 / total
            result = None
            for b, part in zip(blocks, expo):
                low = (part * inverse).astype(BF)
                o.probs[0, h, d.pairs.index((i, b))] = low
                values = o.qkv[0, o.meta[0, b], :, :, 2 * d.dh + h * HD : 2 * d.dh + (h + 1) * HD].reshape(tok, HD)
                term = nn(low, values)
                result = term if result is None else result + term
            o.sorted_att[i, :, :, lanes] = result.astype(BF).reshape(2, d.half, HD)


def fwd_kernel(d, names, *refs):
    o = Refs()
    for name, ref in zip(names, refs):
        setattr(o, name, ref)
    o.w_save = (o.o_wqkv, o.o_wout, o.o_wup, o.o_wdown)
    p = Place(d)
    fetch = Fetch(p, o)
    gather = Gather(p, o.ag_send, o.ag_recv)
    scatter = Scatter(p, o.part, o.near, o.far, o.near_send, o.near_recv, o.far_send, o.far_recv)
    small = SmallSum(p, o.in_gains, o.sp_in, o.mid_a, o.z_in, o.mid_b, o.y_in, o.sp_sem, o.z_sem, o.y_sem)

    def save(name, l):
        ref, out = getattr(o, name), getattr(o, "o_" + name)
        held = 0 if name in ONCE else l
        return pltpu.make_async_copy(ref.at[held], out.at[l], o.save_sem.at[l, SAVED.index(name)])

    def free(l, *names):
        if l > 0:
            for name in names:
                save(name, l - 1).wait()

    late = Gather(p, o.late_send, o.late_recv)
    keep_gl = pltpu.make_async_copy(o.gl, o.o_gl, o.late_sem.at[0])

    def run(slot):
        for op, l, piece in FORWARD_PLAN.get(slot, ()):
            if op == LATE_START:
                o.gl[p.s, piece] = o.in_cotangent[piece]
                late.start(o.gl, piece)
            elif op == LATE_ON:
                for step in range(2 + piece, d.sp_n, 2):
                    late.through(o.gl, step)
            elif op == LATE_END:
                late.rest(o.gl)
                keep_gl.start()
            elif op == RELAY_1:
                fetch.relay(l, piece, 1)
            elif op == RELAY_3:
                fetch.relay(l, piece, 3)
            else:
                act = {
                    SPREAD: fetch.spread,
                    OWN: fetch.own,
                    START_Z: fetch.start_z,
                    START_Y: fetch.start_y,
                    INNER: fetch.inner,
                    OUTER: fetch.outer,
                }[op]
                act(l, piece)

    def place(l):
        if d.whole_lanes:
            for j in range(d.sp_n):
                for i in range(3):
                    o.in_qkv[l, j, :, i * d.dh : (i + 1) * d.dh] = o.raw_qkv[l, i, :, j * d.dh : (j + 1) * d.dh]
                for k in range(d.dp_n):
                    whole, kept = up_columns(d, j, k)
                    o.in_up[l, j, :, kept] = o.raw_up[l, :, whole]

    place(0)
    p.barrier()
    for w in (QKV, OUT):
        fetch.spread(0, w)
    small.start(0)
    for l in range(1, d.layers):
        place(l)
    lay_out(d, o)
    for w in (UP, DOWN):
        fetch.spread(0, w)
    run(0)
    small.finish(0, o.mid_a)
    small.start(1)
    run(1)
    small.finish(1, o.mid_b)
    small.start(2)
    run(2)
    small.finish(2, o.o_gains)

    def norm_in(l, half, gain):
        def first(rows):
            v = o.in_tokens[half, rows].astype(F32)
            o.stream[0, half, rows] = v
            o.xin[0, p.s, half, rows] = norm_rows(v, gain).astype(BF)

        row_loop(d.half, first)

    for half in range(2):
        norm_in(0, half, o.o_gains[0:1, :])
        gather.start(o.xin.at[0], half)

    for l in range(d.layers):
        gain_mid = o.o_gains[2 * l + 1 : 2 * l + 2, :]
        xin, xmid = o.xin.at[l], o.xmid.at[l]
        save("stream", l).start()
        run(3 + 10 * l)
        fetch.ready(l, 0)
        fetch.save(l, QKV).start()
        free(l, "qkv")
        third = 3 * d.dh // 3

        def project(pieces):
            block = pair(xin, pieces)
            for n in range(3):
                cols = slice(n * third, (n + 1) * third)
                weight = o.wqkv[l, :, :, :, :, cols].reshape(d.width, third)
                put_pair(o.qkv.at[0], pieces, cols, nn(block, weight))

        project(p.pieces(0))
        gather.near(xin)
        project(p.pieces(1))
        run(4 + 10 * l)

        @pl.loop(2, d.sp_n)
        def _(t):
            gather.far(xin, t)
            project(p.pieces(t))

        gather.end(xin)
        save("xin", l).start()
        save("qkv", l).start()
        run(5 + 10 * l)
        free(l, "probs", "att")
        attention_forward(d, o, l)
        save("probs", l).start()
        run(6 + 10 * l)
        fetch.ready(l, 1)
        fetch.save(l, OUT).start()

        def out_part(pieces):
            blocks = []
            for slot, half in pieces:
                block = o.sorted_att[o.meta[1, slot], half]
                o.att[0, slot, half] = block
                blocks.append(block)
            block = jnp.concatenate(blocks, axis=0)
            for n in range(d.n_width):
                cols = slice(n * d.chunk, (n + 1) * d.chunk)
                weight = o.wout[l, :, :, :, cols].reshape(d.dh, d.chunk)
                put_pair(o.part, pieces, cols, nn(block, weight))

        @pl.loop(2, d.sp_n)
        def _(t):
            out_part(p.pieces(t))
            scatter.put(t)

            @pl.when(t > 2)
            def _():
                scatter.cross(t - 1)

        out_part(p.pieces(1))
        scatter.put(1)
        scatter.cross(d.sp_n - 1)
        out_part(p.pieces(0))
        save("att", l).start()
        run(7 + 10 * l)

        def middle(half, rows):
            v = o.stream[l, half, rows] + scatter.total(half, rows)
            o.mid[l, half, rows] = v
            xmid[p.s, half, rows] = norm_rows(v, gain_mid).astype(BF)

        for half in range(2):
            scatter.arrive(half)
            row_loop(d.half, functools.partial(middle, half))
            gather.start(xmid, half)
            if half == 0:
                run(8 + 10 * l)
        scatter.end()
        save("mid", l).start()
        run(9 + 10 * l)
        fetch.ready(l, 2, 3)
        fetch.save(l, UP).start()
        free(l, "hid", "slope")

        def up(pieces):
            block = pair(xmid, pieces)
            for n in range(d.n_hid):
                cols = slice(n * d.chunk, (n + 1) * d.chunk)
                weight = o.wup[l, :, :, :, :, cols].reshape(d.width, d.chunk)
                pre = nn(block, weight)
                phi = 0.5 * (1.0 + lax.erf(pre * (0.5**0.5)))
                put_pair(o.hid.at[0], pieces, cols, pre * phi)
                density = jnp.exp(-0.5 * pre * pre) * 0.3989422804014327
                put_pair(o.slope.at[0], pieces, cols, phi + pre * density)

        def down(pieces):
            hidden = pair(o.hid.at[0], pieces)
            for n in range(d.n_width):
                cols = slice(n * d.chunk, (n + 1) * d.chunk)
                weight = o.wdown[l, :, :, :, cols].reshape(d.hid, d.chunk)
                put_pair(o.part, pieces, cols, nn(hidden, weight))

        up(p.pieces(0))
        gather.near(xmid)
        up(p.pieces(1))
        run(10 + 10 * l)
        if l == 0:

            @pl.loop(2, d.sp_n)
            def _(t):
                gather.far(xmid, t)
                up(p.pieces(t))

        fetch.ready(l, 4, 5)
        fetch.save(l, DOWN).start()

        @pl.loop(2, d.sp_n)
        def _(t):
            if l > 0:
                gather.far(xmid, t)
                up(p.pieces(t))

                @pl.when(t > 2)
                def _():
                    scatter.cross(t - 1)

            down(p.pieces(t))
            scatter.put(t)
            if l == 0:

                @pl.when(t > 2)
                def _():
                    scatter.cross(t - 1)

        down(p.pieces(1))
        scatter.put(1)
        scatter.cross(d.sp_n - 1)
        down(p.pieces(0))
        gather.end(xmid)
        save("xmid", l).start()
        save("hid", l).start()
        save("slope", l).start()
        run(11 + 10 * l)

        def last(half, rows):
            v = o.mid[l, half, rows] + scatter.total(half, rows)
            if l + 1 < d.layers:
                o.stream[l + 1, half, rows] = v
                o.xin[l + 1, p.s, half, rows] = norm_rows(v, o.o_gains[2 * l + 2 : 2 * l + 3, :]).astype(BF)
            else:
                o.o_output[half, rows] = v.astype(BF)

        for half in range(2):
            scatter.arrive(half)
            row_loop(d.half, functools.partial(last, half))
            if l + 1 < d.layers:
                gather.start(o.xin.at[l + 1], half)
                if half == 0:
                    run(12 + 10 * l)
        scatter.end()

    fetch.end()
    late.end(o.gl)
    keep_gl.wait()
    for l in range(d.layers):
        for name in SAVED:
            if l == d.layers - 1 or name not in ONCE:
                save(name, l).wait()


class Reduce:
    def __init__(self, p, o):
        self.p, self.o = p, o
        self.grad = (o.g_qkv, o.g_out, o.g_up, o.g_down)
        self.sp_in = (o.x_qkv, o.x_out, o.x_up, None)
        self.result = (o.o_qkv, o.o_out, o.o_up, o.o_down)
        self.done = {}

    def z_first(self, l, term):
        return term in self.p.d.z_first[l]

    def ins(self, l, term):
        o = self.o
        return getattr(o, "y_in_%d_%d" % (l, term)), getattr(o, "z_in_%d_%d" % (l, term))

    def columns(self, l, term):
        p = self.p
        if self.z_first(l, term):
            return [(y, y) for y in [p.y] + [p.ypeer(m) for m in range(1, p.d.y_n)]]
        return [(p.y, 0)]

    def step(self, l, *terms):
        for term in terms:
            stages = (self.y_send, self.y_sum, self.inner, self.finish_z)
            if self.z_first(l, term):
                stages = (self.z_send, self.inner, self.z_sum, self.finish_y)
            count = self.done.get((l, term), 0)
            self.done[l, term] = count + 1
            stages[count](l, term)

    def groups(self, term):
        w, first, last = self.p.d.terms[term]
        if w in (QKV, UP):
            return [((j,), (j - first,)) for j in range(first, last)]
        rows = min(32, last - first)
        return [
            ((slice(j, j + rows),), (slice(j - first, j - first + rows),)) for j in range(first, last, rows)
        ]

    def y_copy(self, l, term, k):
        p, o = self.p, self.o
        w, first, last = p.d.terms[term]
        index = p.d.y_n - k - 1
        there = p.ypeer(k)
        into = self.ins(l, term)[0].at[index]
        if self.z_first(l, term):
            src, into = self.grad[w].at[p.z, there, first:last], into.at[0]
        else:
            src = self.grad[w].at[:, there, first:last]
        return rcopy(src, into, o.ry_send.at[l, term, k], o.ry_recv.at[l, term, index], p.dev(p.z, there))

    def y_send(self, l, term):
        for k in range(1, self.p.d.y_n):
            self.y_copy(l, term, k).start()

    def y_wait(self, l, term):
        for k in range(1, self.p.d.y_n):
            self.y_copy(l, term, self.p.d.y_n - k).wait_recv()

    def y_sum(self, l, term):
        p = self.p
        w = p.d.terms[term][0]
        y_in, _ = self.ins(l, term)
        self.y_wait(l, term)
        for z in range(p.d.z_n):
            for index, here in self.groups(term):
                value = self.grad[w][(z, p.y) + index].astype(F32)
                for m in range(p.d.y_n - 1):
                    value = value + y_in[(m, z) + here].astype(F32)
                self.grad[w][(z, p.y) + index] = value.astype(BF)
        self.z_send(l, term)

    def z_copy(self, l, term, column, z, goal, place, way):
        p, o = self.p, self.o
        w, first, last = p.d.terms[term]
        y, slot = column
        return rcopy(
            self.grad[w].at[z, y, first:last],
            self.ins(l, term)[1].at[place, slot],
            o.rz_send.at[l, term, slot, way],
            o.rz_recv.at[l, term, slot, place],
            p.dev(goal, p.y),
        )

    def z_goals(self, inside):
        at = self.p.line()[1]
        if inside:
            return ((at[3], at[2], 3), (at[2], at[2], 1), (at[1], at[1], 0))
        return ((at[1], at[1], 0), (at[2], at[1], 2), (at[3], at[2], 4))

    def both(self, inner, outer):
        inside, _ = self.p.line()
        pl.when(inside)(inner)
        pl.when(jnp.logical_not(inside))(outer)

    def z_send(self, l, term):
        if self.p.d.z_n == 1:
            return

        def send(inside, ways):
            for column in self.columns(l, term):
                for way in ways:
                    self.z_copy(l, term, column, *self.z_goals(inside)[way], way).start()

        self.both(lambda: send(True, (0,)), lambda: send(False, (0, 1, 2)))

    def z_wait(self, l, term, column, place):
        self.z_copy(l, term, column, self.p.z, self.p.z, place, 0).wait_recv()

    def inner(self, l, term):
        p = self.p
        if p.d.z_n == 1:
            return
        w = p.d.terms[term][0]
        _, z_in = self.ins(l, term)

        def relay():
            for way, places in ((1, (2,)), (2, (3, 4))):
                z, goal, place = self.z_goals(True)[way]
                for column in self.columns(l, term):
                    y, slot = column
                    for source in places:
                        self.z_wait(l, term, column, source)
                    for index, here in self.groups(term):
                        value = self.grad[w][(z, y) + index].astype(F32)
                        for source in places:
                            value = value + z_in[(source, slot) + here].astype(F32)
                        self.grad[w][(z, y) + index] = value.astype(BF)
                    self.z_copy(l, term, column, z, goal, place, way).start()

        pl.when(p.line()[0])(relay)

    def z_total(self, l, term, column, store):
        p = self.p
        w = p.d.terms[term][0]
        _, z_in = self.ins(l, term)
        y, slot = column

        def total(places):
            for source in places:
                self.z_wait(l, term, column, source)
            for index, here in self.groups(term):
                value = self.grad[w][(p.z, y) + index].astype(F32)
                for source in places:
                    value = value + z_in[(source, slot) + here].astype(F32)
                store(y, index, here, value)

        if p.d.z_n == 1:
            total(())
        else:
            self.both(lambda: total((0, 1)), lambda: total((0,)))

    def z_sum(self, l, term):
        w = self.p.d.terms[term][0]

        def store(y, index, here, value):
            self.grad[w][(self.p.z, y) + index] = value.astype(BF)

        for column in self.columns(l, term):
            self.z_total(l, term, column, store)
        self.y_send(l, term)

    def finish_z(self, l, term):
        def store(y, index, here, value):
            self.settle(l, term, index, value)

        self.z_total(l, term, self.columns(l, term)[0], store)
        self.pass_on(l, term)

    def finish_y(self, l, term):
        p = self.p
        w = p.d.terms[term][0]
        y_in, _ = self.ins(l, term)
        self.y_wait(l, term)
        for index, here in self.groups(term):
            value = self.grad[w][(p.z, p.y) + index].astype(F32)
            for m in range(p.d.y_n - 1):
                value = value + y_in[(m, 0) + here].astype(F32)
            self.settle(l, term, index, value)
        self.pass_on(l, term)

    def settle(self, l, term, index, value):
        w = self.p.d.terms[term][0]
        if w == DOWN:
            self.result[w][(l,) + index] = value.astype(BF)
        else:
            self.grad[w][(self.p.z, self.p.y) + index] = value.astype(BF)

    def s_copy(self, l, w, j, source):
        p, o = self.p, self.o
        return rcopy(
            self.grad[w].at[p.z, p.y, j], self.sp_in[w].at[l, source], o.rs_send.at[l, w, j], o.rs_recv.at[l, w, source], (p.r, j)
        )

    def out_copy(self, l, device):
        p, o = self.p, self.o
        return rcopy(
            self.grad[OUT].at[p.z, p.y], self.sp_in[OUT].at[l], o.rs_send.at[l, OUT, 0], o.rs_recv.at[l, OUT, 0], device
        )

    def keep(self, l, w, j, ref):
        d, result = self.p.d, self.result[w]
        if not d.whole_lanes:
            result[l, j] = ref[...]
        elif w == QKV:
            for i in range(3):
                result[l, i, :, j * d.dh : (j + 1) * d.dh] = ref[:, i * d.dh : (i + 1) * d.dh]
        else:
            for k in range(d.dp_n):
                whole, kept = up_columns(d, j, k)
                result[l, :, whole] = ref[:, kept]

    def pass_on(self, l, term):
        p = self.p
        w, first, last = p.d.terms[term]
        if w in (QKV, UP):
            for j in range(first, last):

                @pl.when(p.s == j)
                def _():
                    self.keep(l, w, j, self.grad[w].at[p.z, p.y, j])

                @pl.when(p.s != j)
                def _():
                    self.s_copy(l, w, j, p.s).start()

        elif w == OUT:
            _, source, stays = p.moved()

            @pl.when(stays)
            def _():
                self.result[w][l] = self.grad[w][p.z, p.y]

            @pl.when(jnp.logical_not(stays))
            def _():
                self.out_copy(l, source).start()

    def sent(self, l, w):
        p = self.p
        for term, (kind, first, last) in enumerate(p.d.terms):
            if kind != w:
                continue
            for k in range(1, p.d.y_n):
                self.y_copy(l, term, k).wait_send()
            if p.d.z_n > 1:

                def wait(inside):
                    for column in self.columns(l, term):
                        for way in range(3):
                            self.z_copy(l, term, column, *self.z_goals(inside)[way], way).wait_send()

                self.both(lambda: wait(True), lambda: wait(False))
        if w in (QKV, UP):
            for t in range(1, p.d.sp_n):
                self.s_copy(l, w, p.slot(t), p.s).wait_send()
        elif w == OUT:
            _, source, stays = p.moved()

            @pl.when(jnp.logical_not(stays))
            def _():
                self.out_copy(l, source).wait_send()

    def last(self, l, w):
        p = self.p
        if w in (QKV, UP):
            for j in range(p.d.sp_n):

                @pl.when(p.s != j)
                def _():
                    self.s_copy(l, w, j, j).wait_recv()
                    self.keep(l, w, j, self.sp_in[w].at[l, j])
        elif w == OUT:
            _, source, stays = p.moved()

            @pl.when(jnp.logical_not(stays))
            def _():
                self.out_copy(l, source).wait_recv()
                self.result[w][l] = self.sp_in[w][l]


def norm_back(v, d_out, gain):
    center = v - mean_of(v)
    inverse = lax.rsqrt(mean_of(center * center) + EPS)
    unit = center * inverse
    gain_term = jnp.sum(d_out * unit, axis=0, keepdims=True)
    e = d_out * gain
    back = (e - mean_of(e) - unit * mean_of(e * unit)) * inverse
    return back, gain_term


def attention_backward(d, o):
    tok = d.tok
    for i in range(d.sp_n):
        here = o.meta[0, i]
        blocks = range(max(0, i - d.back), i + 1)
        for h in range(d.heads):
            lanes = slice(h * HD, (h + 1) * HD)
            key_lanes = slice(d.dh + h * HD, d.dh + (h + 1) * HD)
            value_lanes = slice(2 * d.dh + h * HD, 2 * d.dh + (h + 1) * HD)
            query = o.qkv[here, :, :, lanes].reshape(tok, HD)
            grad = o.d_att[here, :, :, lanes].reshape(tok, HD)
            d_probs, inner = [], None
            for b in blocks:
                low = o.probs[h, d.pairs.index((i, b))].astype(F32)
                term = nt(grad, o.qkv[o.meta[0, b], :, :, value_lanes].reshape(tok, HD))
                d_probs.append(term)
                weighted = jnp.sum(low * term, axis=-1, keepdims=True)
                inner = weighted if inner is None else inner + weighted
            d_query = None
            for b, term in zip(blocks, d_probs):
                low = o.probs[h, d.pairs.index((i, b))]
                d_score = (low.astype(F32) * (term - inner)).astype(BF)
                step = nn(d_score, o.qkv[o.meta[0, b], :, :, key_lanes].reshape(tok, HD))
                d_query = step if d_query is None else d_query + step
                d_key, d_value = tn(d_score, query), tn(low, grad)
                if b == i:
                    o.d_keys[b, :, lanes] = d_key
                    o.d_values[b, :, lanes] = d_value
                else:
                    o.d_keys[b, :, lanes] += d_key
                    o.d_values[b, :, lanes] += d_value
            o.sorted_dqkv[i, :, :, lanes] = (d_query * HD ** (-0.5)).astype(BF).reshape(2, d.half, HD)
    for b in range(d.sp_n):
        shape = (2, d.half, d.dh)
        o.sorted_dqkv[b, :, :, d.dh : 2 * d.dh] = (o.d_keys[b] * HD ** (-0.5)).astype(BF).reshape(shape)
        o.sorted_dqkv[b, :, :, 2 * d.dh :] = o.d_values[b].astype(BF).reshape(shape)


def bwd_kernel(d, names, *refs):
    o = Refs()
    for name, ref in zip(names, refs):
        setattr(o, name, ref)
    p = Place(d)
    gather = Gather(p, o.ag_send, o.ag_recv)
    scatter = Scatter(p, o.part, o.near, o.far, o.near_send, o.near_recv, o.far_send, o.far_recv)
    small = SmallSum(p, o.gain_sum, o.sp_in, o.mid_a, o.z_in, o.mid_b, o.y_in, o.sp_sem, o.z_sem, o.y_sem)
    reduce = Reduce(p, o)
    loads = WEIGHTS + SAVED

    def load(name, l):
        ref = o.mid if name == "stream" else getattr(o, name)
        return pltpu.make_async_copy(getattr(o, "i_" + name).at[l], ref, o.load_sem.at[loads.index(name)])

    def refill(l, *which):
        if l > 0:
            for name in which:
                load(name, l - 1).start()

    def run(slot):
        for layer, term in BACKWARD_PLAN.get(slot, ()):
            reduce.step(layer, term)

    top = d.layers - 1
    first_grad = pltpu.make_async_copy(o.i_gl, o.gl, o.late_sem.at[0])
    first_grad.start()
    for name in ("wdown", "slope", "wup", "hid", "xmid", "mid", "wout", "qkv", "probs", "att", "wqkv", "xin"):
        load(name, top).start()
    p.barrier()
    lay_out(d, o)
    o.gain_sum[...] = jnp.zeros_like(o.gain_sum)

    first_grad.wait()
    for half in range(2):

        def begin(rows):
            o.o_grad[half, rows] = o.gl[p.s, half, rows].astype(F32)

        row_loop(d.half, begin)
    tokens = d.sp_n * d.tok

    def rows_of(ref, n, count):
        part = ref[n * d.z_n // count : (n + 1) * d.z_n // count]
        return part.reshape(d.chunk, part.shape[-1])

    def weight_grad(out, left_ref, right_ref, count, width):
        for n in range(count):
            left = left_ref[:, :, :, n * d.chunk : (n + 1) * d.chunk].reshape(tokens, d.chunk)
            value = tn(left, right_ref[...].reshape(tokens, width)).astype(BF)
            zs = slice(n * d.z_n // count, (n + 1) * d.z_n // count)
            out[zs] = value.reshape((d.z_n // count,) + out.shape[1:])

    for l in reversed(range(d.layers)):
        gain_in = o.in_gains[2 * l : 2 * l + 1, :]
        gain_mid = o.in_gains[2 * l + 1 : 2 * l + 2, :]
        run(0 + 14 * (top - l))
        load("wdown", l).wait()
        load("slope", l).wait()
        load("wup", l).wait()

        def pre_grad(pieces):
            block = pair(o.gl, pieces)
            for n in range(d.n_hid):
                cols = slice(n * d.chunk, (n + 1) * d.chunk)
                d_hidden = nt(block, rows_of(o.wdown, n, d.n_hid))
                put_pair(o.slope, pieces, cols, d_hidden * pair(o.slope, pieces, cols).astype(F32))

        def mid_grad(pieces):
            d_pre = pair(o.slope, pieces)
            for n in range(d.n_width):
                cols = slice(n * d.chunk, (n + 1) * d.chunk)
                put_pair(o.part, pieces, cols, nt(d_pre, rows_of(o.wup, n, d.n_width)))

        if l < top:
            pre_grad(p.pieces(0))
            gather.near(o.gl)
            pre_grad(p.pieces(1))
        run(1 + 14 * (top - l))

        @pl.loop(2, d.sp_n)
        def _(t):
            if l < top:
                gather.far(o.gl, t)
            pre_grad(p.pieces(t))

            @pl.when(t > 2)
            def _():
                scatter.cross(t - 1)

            mid_grad(p.pieces(t))
            scatter.put(t)

        if l == top:
            pre_grad(p.pieces(1))
        mid_grad(p.pieces(1))
        scatter.put(1)
        scatter.cross(d.sp_n - 1)
        if l == top:
            pre_grad(p.pieces(0))
        mid_grad(p.pieces(0))
        if l < top:
            gather.end(o.gl)
        refill(l, "wdown", "wup")
        load("hid", l).wait()
        run(2 + 14 * (top - l))
        if l < top:
            reduce.sent(l + 1, DOWN)
        weight_grad(o.g_down, o.hid, o.gl, d.n_hid, d.width)
        run(3 + 14 * (top - l))
        refill(l, "hid")
        load("mid", l).wait()

        def middle(half, rows):
            back, gain_term = norm_back(o.mid[half, rows], scatter.total(half, rows), gain_mid)
            o.gain_sum[2 * l + 1 : 2 * l + 2, :] += gain_term
            value = o.o_grad[half, rows] + back
            o.o_grad[half, rows] = value
            o.ml[p.s, half, rows] = value.astype(BF)

        for half in range(2):
            scatter.arrive(half)
            row_loop(d.half, functools.partial(middle, half))
            gather.start(o.ml, half)
            if half == 0:
                run(4 + 14 * (top - l))
        scatter.end()
        load("stream", l).start()
        load("xmid", l).wait()
        run(5 + 14 * (top - l))
        if l < top:
            reduce.sent(l + 1, UP)
        weight_grad(o.g_up, o.xmid, o.slope, d.n_width, d.hid)
        run(6 + 14 * (top - l))
        refill(l, "xmid", "slope")
        load("wout", l).wait()

        def att_grad(pieces):
            weight = o.wout[...].reshape(d.dh, d.width)
            put_pair(o.d_att, pieces, slice(None), nt(pair(o.ml, pieces), weight))

        att_grad(p.pieces(0))
        gather.near(o.ml)
        att_grad(p.pieces(1))
        run(7 + 14 * (top - l))

        @pl.loop(2, d.sp_n)
        def _(t):
            gather.far(o.ml, t)
            att_grad(p.pieces(t))

        gather.end(o.ml)
        refill(l, "wout")
        run(8 + 14 * (top - l))
        load("qkv", l).wait()
        load("probs", l).wait()
        attention_backward(d, o)
        refill(l, "qkv", "probs")
        run(9 + 14 * (top - l))
        load("wqkv", l).wait()

        def in_grad(pieces):
            blocks = []
            for slot, half in pieces:
                block = o.sorted_dqkv[o.meta[1, slot], half]
                o.d_qkv[slot, half] = block
                blocks.append(block)
            block = jnp.concatenate(blocks, axis=0)
            for n in range(d.n_width):
                cols = slice(n * d.chunk, (n + 1) * d.chunk)
                put_pair(o.part, pieces, cols, nt(block, rows_of(o.wqkv, n, d.n_width)))

        @pl.loop(2, d.sp_n)
        def _(t):
            in_grad(p.pieces(t))
            scatter.put(t)

            @pl.when(t > 2)
            def _():
                scatter.cross(t - 1)

        in_grad(p.pieces(1))
        scatter.put(1)
        scatter.cross(d.sp_n - 1)
        in_grad(p.pieces(0))
        run(10 + 14 * (top - l))
        refill(l, "wqkv")
        load("att", l).wait()
        if l < top:
            reduce.sent(l + 1, OUT)
        value = tn(o.att[...].reshape(tokens, d.dh), o.ml[...].reshape(tokens, d.width)).astype(BF)
        o.g_out[...] = value.reshape((d.z_n, d.y_n, d.rows, d.width))
        run(11 + 14 * (top - l))
        refill(l, "att")
        load("xin", l).wait()
        if l < top:
            reduce.sent(l + 1, QKV)
        weight_grad(o.g_qkv, o.xin, o.d_qkv, d.n_width, 3 * d.dh)
        run(12 + 14 * (top - l))
        refill(l, "xin")
        load("stream", l).wait()

        def lower(half, rows):
            back, gain_term = norm_back(o.mid[half, rows], scatter.total(half, rows), gain_in)
            o.gain_sum[2 * l : 2 * l + 1, :] += gain_term
            value = o.o_grad[half, rows] + back
            o.o_grad[half, rows] = value
            if l > 0:
                o.gl[p.s, half, rows] = value.astype(BF)

        for half in range(2):
            scatter.arrive(half)
            row_loop(d.half, functools.partial(lower, half))
            if l > 0:
                gather.start(o.gl, half)
            if half == 0:
                run(13 + 14 * (top - l))
        scatter.end()
        if l == 0:
            small.start(0)
        refill(l, "mid")

    run(28)
    small.finish(0, o.mid_a)
    small.start(1)
    run(29)
    small.finish(1, o.mid_b)
    small.start(2)
    run(30)
    small.finish(2, o.o_gains)
    for l in reversed(range(d.layers)):
        for w in (DOWN, UP, OUT, QKV):
            reduce.last(l, w)
    for w in (DOWN, UP, OUT, QKV):
        reduce.sent(0, w)


def finish_kernel(d, names, *refs):
    o = Refs()
    for name, ref in zip(names, refs):
        setattr(o, name, ref)
    for given, out in ((o.o_qkv, o.r_qkv), (o.o_out, o.r_out), (o.o_up, o.r_up), (o.o_down, o.r_down)):
        for l in range(d.layers):
            out[l] = given[l].astype(F32)
    o.r_grad[...] = o.o_grad[...]
    o.r_output[...] = o.o_output[...]
    own = o.r_gains.shape[1]
    flat = lax.axis_index(AXES[0]) * d.sp_n + lax.axis_index(AXES[1])
    mine = jnp.zeros(o.r_gains.shape, F32)
    for k in range(d.width // own):
        mine = jnp.where(flat == k, o.o_gains[: o.r_gains.shape[0], k * own : (k + 1) * own], mine)
    o.r_gains[...] = mine


ANY = pl.BlockSpec(memory_space=pl.ANY)
VM = pl.BlockSpec(memory_space=pltpu.VMEM)
SM = pl.BlockSpec(memory_space=pltpu.SMEM)


def call(kernel, d, inputs, outputs, scratch, identity):
    names = [i[0] for i in inputs] + [i[0] for i in outputs] + [i[0] for i in scratch]
    results = pl.pallas_call(
        functools.partial(kernel, d, names),
        out_shape=[jax.ShapeDtypeStruct(i[2], i[3]) for i in outputs],
        in_specs=[i[1] for i in inputs],
        out_specs=[i[1] for i in outputs],
        scratch_shapes=[i[1] for i in scratch],
        compiler_params=pltpu.CompilerParams(
            collective_id=identity, has_side_effects=identity is not None, vmem_limit_bytes=62 * 1024 * 1024
        ),
        name=kernel.__name__,
    )(*[i[2] for i in inputs])
    return dict(zip([i[0] for i in outputs], results))


def shards(dp_n, sp_n, tokens, cotangent, w_qkv, w_out, w_up, w_down, gains, piece_order, doc_lengths):
    _, tok, width = tokens.shape
    layers, _, rows, _ = w_qkv.shape
    ff = w_up.shape[-1]
    d = Dims(dp_n, sp_n, layers, tok, width, ff, doc_lengths.shape[1])
    r, s = lax.axis_index("dp"), lax.axis_index("sp")

    own = gains.shape[-1]
    padded = jnp.zeros((8, width), F32)
    padded = lax.dynamic_update_slice(
        padded, gains.reshape(2 * layers, own).astype(F32), (0, (r * sp_n + s) * own)
    )
    lay_scratch = []
    if d.whole_lanes:
        lay_scratch = [
            ("in_qkv", pltpu.VMEM((layers, sp_n, rows, 3 * d.dh), BF)),
            ("in_up", pltpu.VMEM((layers, sp_n, rows, d.hid), BF)),
        ]
        given = [("raw_qkv", VM, w_qkv), ("raw_up", VM, w_up)]
    else:
        in_qkv = w_qkv.reshape(layers, 3, rows, sp_n, d.dh).transpose(0, 3, 2, 1, 4)
        in_up = w_up.reshape(layers, rows, dp_n, sp_n, d.hid_own).transpose(0, 3, 1, 2, 4)
        given = [
            ("in_qkv", ANY, in_qkv.reshape(layers, sp_n, rows, 3 * d.dh)),
            ("in_up", ANY, in_up.reshape(layers, sp_n, rows, d.hid)),
        ]

    saved, weights = saved_shapes(d), weight_shapes(d)
    dma = pltpu.SemaphoreType.DMA
    fwd = call(
        fwd_kernel,
        d,
        [
            ("in_order", SM, piece_order),
            ("in_lengths", SM, doc_lengths),
            ("in_tokens", VM, tokens.reshape(2, d.half, width)),
            ("in_cotangent", VM, cotangent.reshape(2, d.half, width)),
            ("in_gains", VM, padded),
            ("in_out", ANY, w_out),
            ("in_down", ANY, w_down),
        ]
        + given,
        [("o_output", VM, (2, d.half, width), BF), ("o_gains", VM, (8, width), F32)]
        + [("o_" + n, ANY, (layers,) + weights[n][0], BF) for n in WEIGHTS]
        + [("o_" + n, ANY, (layers,) + saved[n][0], saved[n][1]) for n in SAVED]
        + [("o_gl", ANY, (sp_n, 2, d.half, width), BF)],
        [(n, pltpu.VMEM((layers,) + weights[n][0], BF)) for n in WEIGHTS]
        + [(n, pltpu.VMEM((1 if n in ONCE else layers,) + saved[n][0], saved[n][1])) for n in SAVED]
        + [
            ("sorted_att", pltpu.VMEM(saved["att"][0], BF)),
            ("meta", pltpu.SMEM((3, max(sp_n, d.docs)), jnp.int32)),
        ]
        + [
            ("gl", pltpu.VMEM((sp_n, 2, d.half, width), BF)),
            ("late_send", dma((2, sp_n, 2))),
            ("late_recv", dma((sp_n, 2))),
            ("late_sem", dma((1,))),
        ]
        + lay_scratch
        + small_scratch(d)
        + comm_scratch(d)
        + [
            ("s_send", dma((layers, 4, sp_n))),
            ("s_recv", dma((layers, 4, sp_n))),
            ("own_sem", dma((layers, 4))),
            ("b_send", dma((layers, len(d.pieces), d.z_n, d.y_n, 1 + d.y_n))),
            ("b_recv", dma((layers, len(d.pieces), d.z_n, d.y_n))),
            ("w_sem", dma((layers, 4))),
            ("save_sem", dma((layers, len(SAVED)))),
        ],
        0,
    )
    kinds = ("qkv", "out", "up", "down")
    blocks = [d.block_shape(w) for w in range(4)]
    results = [(layers,) + b for b in blocks]
    if d.whole_lanes:
        results[QKV], results[UP] = w_qkv.shape, w_up.shape
    bwd = call(
        bwd_kernel,
        d,
        [("in_order", SM, piece_order), ("in_lengths", SM, doc_lengths), ("i_gl", ANY, fwd["o_gl"]), ("in_gains", VM, fwd["o_gains"])]
        + [("i_" + n, ANY, fwd["o_" + n]) for n in WEIGHTS + SAVED],
        [("o_grad", VM, (2, d.half, width), F32), ("o_gains", VM, (8, width), F32)]
        + [("o_" + k, VM, shape, BF) for k, shape in zip(kinds, results)],
        [(n, pltpu.VMEM(weights[n][0], BF)) for n in WEIGHTS]
        + [(n, pltpu.VMEM(saved[n][0], saved[n][1])) for n in SAVED if n != "stream"]
        + [
            ("gl", pltpu.VMEM((sp_n, 2, d.half, width), BF)),
            ("ml", pltpu.VMEM((sp_n, 2, d.half, width), BF)),
            ("d_att", pltpu.VMEM((sp_n, 2, d.half, d.dh), BF)),
            ("sorted_dqkv", pltpu.VMEM((sp_n, 2, d.half, 3 * d.dh), BF)),
            ("d_qkv", pltpu.VMEM((sp_n, 2, d.half, 3 * d.dh), BF)),
            ("d_keys", pltpu.VMEM((sp_n, tok, d.dh), F32)),
            ("d_values", pltpu.VMEM((sp_n, tok, d.dh), F32)),
            ("gain_sum", pltpu.VMEM((8, width), F32)),
            ("meta", pltpu.SMEM((3, max(sp_n, d.docs)), jnp.int32)),
        ]
        + [("g_" + k, pltpu.VMEM((d.z_n, d.y_n) + b, BF)) for k, b in zip(kinds, blocks)]
        + [i for l in range(layers) for t in range(len(d.terms)) for i in term_scratch(d, l, t)]
        + [("x_" + k, pltpu.VMEM((layers,) + b, BF)) for k, b in zip(kinds[:3], blocks)]
        + small_scratch(d)
        + comm_scratch(d)
        + [
            ("late_sem", dma((1,))),
            ("load_sem", dma((len(WEIGHTS + SAVED),))),
            ("ry_send", dma((layers, len(d.terms), d.y_n))),
            ("ry_recv", dma((layers, len(d.terms), d.y_n))),
            ("rz_send", dma((layers, len(d.terms), d.y_n, 3))),
            ("rz_recv", dma((layers, len(d.terms), d.y_n, 5))),
            ("rs_send", dma((layers, 4, sp_n))),
            ("rs_recv", dma((layers, 4, sp_n))),
        ],
        1,
    )
    done = call(
        finish_kernel,
        d,
        [(n, VM, bwd[n]) for n in ["o_" + k for k in kinds] + ["o_grad", "o_gains"]]
        + [("o_output", VM, fwd["o_output"])],
        [("r_" + k, VM, bwd["o_" + k].shape, F32) for k in kinds]
        + [
            ("r_grad", VM, bwd["o_grad"].shape, F32),
            ("r_output", VM, fwd["o_output"].shape, BF),
            ("r_gains", VM, (2 * layers, own), F32),
        ],
        [],
        None,
    )
    grad_qkv, grad_out, grad_up, grad_down = (done["r_" + k] for k in kinds)
    if not d.whole_lanes:
        grad_qkv = grad_qkv.reshape(layers, sp_n, rows, 3, d.dh).transpose(0, 3, 2, 1, 4).reshape(w_qkv.shape)
        grad_up = grad_up.reshape(layers, sp_n, rows, dp_n, d.hid_own).transpose(0, 2, 3, 1, 4).reshape(w_up.shape)
    return (
        done["r_output"].reshape(tokens.shape),
        done["r_grad"].reshape(tokens.shape),
        grad_qkv,
        grad_out,
        grad_up,
        grad_down,
        done["r_gains"].reshape(gains.shape),
    )


def solution(mesh):
    return jax.shard_map(
        functools.partial(shards, mesh.shape["dp"], mesh.shape["sp"]),
        mesh=mesh,
        in_specs=(
            P("dp", "sp", None),
            P("dp", "sp", None),
            P(None, None, ("dp", "sp"), None),
            P(None, ("dp", "sp"), None),
            P(None, ("dp", "sp"), None),
            P(None, ("dp", "sp"), None),
            P(None, None, ("dp", "sp")),
            P("dp", None),
            P("dp", None),
        ),
        out_specs=(
            P("dp", "sp", None),
            P("dp", "sp", None),
            P(None, None, ("dp", "sp"), None),
            P(None, ("dp", "sp"), None),
            P(None, ("dp", "sp"), None),
            P(None, ("dp", "sp"), None),
            P(None, None, ("dp", "sp")),
        ),
        check_vma=False,
    )
```

```python
import functools

import jax
import jax.numpy as jnp
from jax import lax
from jax.experimental import pallas as pl
from jax.experimental.pallas import tpu as pltpu
from jax.sharding import PartitionSpec as P

HEADS = 8
HD = 128
EPS = 1e-05
MASKED = -1e30
MESH = pl.DeviceIdType.MESH
BF = jnp.bfloat16
F32 = jnp.float32
AXES = ("dp", "sp")
QKV, OUT, UP, DOWN = range(4)
Q0, Q1, O0, U0, U1, D0, D1 = range(7)
SPREAD, OWN, START_Z, START_Y, RELAY_1, INNER, OUTER, RELAY_3, LATE_START, LATE_ON, LATE_END = range(11)


def nn(a, b):
    return lax.dot_general(a, b, (((1,), (0,)), ((), ())), preferred_element_type=F32)


def nt(a, b):
    return lax.dot_general(a, b, (((1,), (1,)), ((), ())), preferred_element_type=F32)


def tn(a, b):
    return lax.dot_general(a, b, (((0,), (0,)), ((), ())), preferred_element_type=F32)


FORWARD_PLAN = {
    0: ((LATE_START, 0, 0), (SPREAD, 1, 3), (OWN, 0, 3), (LATE_START, 0, 1), (START_Z, 0, 4), (START_Y, 0, 5), (OWN, 0, 0), (START_Z, 0, 0), (SPREAD, 1, 2), (START_Y, 0, 0),),
    1: ((OWN, 0, 1), (INNER, 0, 0), (START_Z, 0, 1), (RELAY_1, 0, 0), (OWN, 0, 2), (INNER, 0, 1),),
    2: ((RELAY_1, 0, 4), (OUTER, 0, 1), (OUTER, 0, 0), (RELAY_3, 0, 0), (START_Y, 0, 2), (OWN, 1, 3), (START_Y, 0, 1), (START_Z, 0, 3),),
    3: ((SPREAD, 1, 0),),
    4: ((OWN, 1, 2), (INNER, 0, 4), (START_Y, 0, 3), (SPREAD, 1, 1), (RELAY_1, 0, 1), (OUTER, 0, 4), (START_Z, 0, 2),),
    5: ((RELAY_3, 0, 1), (RELAY_1, 0, 2), (START_Z, 0, 5), (INNER, 0, 3),),
    6: ((RELAY_1, 0, 3),),
    7: ((INNER, 0, 2), (RELAY_3, 0, 4), (OWN, 1, 0), (RELAY_3, 0, 2), (OWN, 1, 1), (RELAY_1, 0, 5), (OUTER, 0, 2),),
    8: ((INNER, 0, 5), (OUTER, 0, 3), (START_Z, 1, 0), (START_Y, 0, 4), (RELAY_3, 0, 3),),
    9: ((START_Z, 1, 4), (START_Z, 1, 1), (START_Y, 1, 1), (START_Y, 1, 5), (OUTER, 0, 5), (LATE_ON, 0, 1), (LATE_ON, 0, 0), (RELAY_1, 1, 0), (START_Y, 1, 2), (START_Y, 1, 3),),
    10: ((START_Z, 1, 2), (RELAY_3, 0, 5), (START_Y, 1, 0),),
    11: ((RELAY_1, 1, 1), (INNER, 1, 0), (RELAY_3, 1, 0), (START_Z, 1, 3), (START_Z, 1, 5), (OUTER, 1, 0), (LATE_END, 0, 0),),
    13: ((START_Y, 1, 4), (INNER, 1, 1), (RELAY_1, 1, 4), (RELAY_1, 1, 5),),
    14: ((RELAY_3, 1, 1), (INNER, 1, 2), (RELAY_1, 1, 2), (INNER, 1, 3),),
    15: ((OUTER, 1, 1),),
    16: ((OUTER, 1, 3), (INNER, 1, 4), (RELAY_1, 1, 3), (RELAY_3, 1, 4),),
    18: ((INNER, 1, 5), (RELAY_3, 1, 5), (OUTER, 1, 2), (RELAY_3, 1, 2),),
    19: ((RELAY_3, 1, 3), (OUTER, 1, 4),),
    20: ((OUTER, 1, 5),),
}
BACKWARD_PLAN = {
    3: ((1, D0), (1, D1),),
    6: ((1, U1),),
    7: ((1, D0),),
    8: ((1, U0),),
    10: ((1, D1),),
    11: ((1, U1),),
    12: ((1, Q0), (1, D1),),
    13: ((1, D0),),
    14: ((1, Q0),),
    15: ((1, Q1), (1, O0), (1, U1), (1, U0),),
    16: ((1, Q1), (1, D0), (1, D1),),
    18: ((0, D1), (1, Q0), (1, Q1), (1, O0),),
    20: ((0, D0), (1, O0), (1, O0), (0, D1), (1, U0),),
    21: ((1, Q1),),
    23: ((0, U1), (1, Q0), (0, D0),),
    24: ((0, D1),),
    26: ((0, O0), (0, Q1),),
    27: ((0, D0), (0, U0),),
    28: ((0, Q0), (0, Q1), (0, U1), (0, U1), (0, Q1), (0, D0),),
    29: ((1, U0), (0, U0), (0, O0), (0, U1),),
    30: ((0, Q0), (1, U1), (0, Q1), (0, U0), (0, U0), (0, O0),),
    31: ((0, D1),),
    32: ((0, Q0), (0, O0), (0, Q0),),
}


class Dims:
    def __init__(self, dp_n, sp_n, layers, tok, width, ff, docs):
        self.dp_n, self.sp_n, self.layers, self.tok, self.width = dp_n, sp_n, layers, tok, width
        self.z_n = 4 if dp_n % 4 == 0 else 1
        self.y_n = dp_n // self.z_n
        self.x_n = sp_n // 2
        self.rows = width // (dp_n * sp_n)
        self.heads = HEADS // sp_n
        self.dh = width // sp_n
        self.hid = ff // sp_n
        self.hid_own = ff // (dp_n * sp_n)
        self.docs = docs
        self.whole_lanes = self.hid_own % 128 == 0
        self.chunk = min(256, tok)
        self.half = tok // 2
        self.n_width = width // self.chunk
        self.n_hid = self.hid // self.chunk
        self.back = self.x_n
        half, part = sp_n // 2, self.hid_own // 2
        self.pieces = (
            (QKV, 0, sp_n, False),
            (OUT, 0, self.rows, False),
            (UP, 0, half, False),
            (UP, half, sp_n, False),
            (DOWN, 0, part, False),
            (DOWN, part, self.hid_own, True),
        )
        self.terms = (
            (QKV, 0, half),
            (QKV, half, sp_n),
            (OUT, 0, self.rows),
            (UP, 0, half),
            (UP, half, sp_n),
            (DOWN, 0, part),
            (DOWN, part, self.hid_own),
        )
        self.z_first = [(Q1,)] + [(D1,)] * (layers - 1)
        self.pairs = [(i, b) for i in range(sp_n) for b in range(max(0, i - self.back), i + 1)]

    def block_shape(self, which):
        return {
            QKV: (self.sp_n, self.rows, 3 * self.dh),
            OUT: (self.rows, self.width),
            UP: (self.sp_n, self.rows, self.hid),
            DOWN: (self.hid_own, self.width),
        }[which]


class Place:
    def __init__(self, d):
        self.d = d
        self.r = lax.axis_index(AXES[0])
        self.s = lax.axis_index(AXES[1])
        self.z, self.y = self.r // d.y_n, self.r % d.y_n
        self.x, self.c = self.s // 2, self.s % 2
        self.partner = self.x * 2 + (self.c + 1) % 2

    def slot(self, step):
        return ((self.x + step // 2) % self.d.x_n) * 2 + (self.c + step % 2) % 2

    def pieces(self, step):
        if isinstance(step, int) and step < 2:
            return (self.slot(step), 0), (self.slot(step), 1)
        first = step // 2 * 2
        return (self.slot(first), step % 2), (self.slot(first + 1), step % 2)

    def zpeer(self, dz):
        return (self.z + dz) % self.d.z_n

    def ypeer(self, dy):
        return (self.y + dy) % self.d.y_n

    def line(self):
        high = self.z // 2
        inside = ((self.z + 1) // 2) % 2
        first = inside * 3 * high + (1 - inside) * (1 + high)
        return inside == 1, (self.z, first, 2 - high, 3 - 3 * high)

    def dev(self, z, y):
        return (z * self.d.y_n + y, self.s)

    def moved(self):
        d = self.d
        flat = self.r * d.sp_n + self.s
        goal = (flat % d.dp_n, flat // d.dp_n)
        mine = self.s * d.dp_n + self.r
        source = (mine // d.sp_n, mine % d.sp_n)
        stays = flat == mine
        return goal, source, stays

    def barrier(self):
        d = self.d
        sem = pltpu.get_barrier_semaphore()
        peers = [(self.r, self.slot(t)) for t in range(1, d.sp_n)]
        peers += [self.dev(self.zpeer(k), self.y) for k in range(1, d.z_n)]
        peers += [self.dev(self.z, self.ypeer(k)) for k in range(1, d.y_n)]
        for peer in peers:
            pl.semaphore_signal(sem, inc=1, device_id=peer, device_id_type=MESH)
        goal, source, stays = self.moved()

        @pl.when(jnp.logical_not(stays))
        def _():
            pl.semaphore_signal(sem, inc=1, device_id=goal, device_id_type=MESH)
            pl.semaphore_signal(sem, inc=1, device_id=source, device_id_type=MESH)
            pl.semaphore_wait(sem, len(peers) + 2)

        @pl.when(stays)
        def _():
            pl.semaphore_wait(sem, len(peers))


def rcopy(src, dst, send, recv, device):
    return pltpu.make_async_remote_copy(
        src_ref=src, dst_ref=dst, send_sem=send, recv_sem=recv, device_id=device, device_id_type=MESH
    )


def pair(ref, pieces, *cols):
    return jnp.concatenate([ref[(slot, half) + (slice(None),) + cols] for slot, half in pieces], axis=0)


def put_pair(ref, pieces, cols, value):
    rows = value.shape[0] // 2
    for k, (slot, half) in enumerate(pieces):
        ref[slot, half, :, cols] = value[k * rows : (k + 1) * rows].astype(ref.dtype)


class Gather:
    def __init__(self, p, send, recv):
        self.p, self.send, self.recv = p, send, recv

    def copy(self, buf, slot, half, way, goal):
        block = buf.at[slot, half]
        return rcopy(block, block, self.send.at[way, goal, half], self.recv.at[slot, half], (self.p.r, goal))

    def start(self, buf, half):
        p = self.p
        for dx in range(1, p.d.x_n):
            self.copy(buf, p.s, half, 0, p.slot(2 * dx)).start()
        self.copy(buf, p.s, half, 0, p.partner).start()

    def onward(self, buf, slot, half):
        block = buf.at[slot, half]
        p = self.p
        return rcopy(block, block, self.send.at[1, slot, half], self.recv.at[slot, half], (p.r, p.partner))

    def arrived(self, buf, slot, half):
        self.copy(buf, slot, half, 0, self.p.partner).wait_recv()

    def near(self, buf):
        for half in range(2):
            self.arrived(buf, self.p.partner, half)

    def through(self, buf, step):
        first, _ = self.p.pieces(step)
        self.arrived(buf, *first)
        self.onward(buf, *first).start()

    def rest(self, buf):
        self.near(buf)
        for step in range(2, self.p.d.sp_n):
            self.arrived(buf, *self.p.pieces(step)[1])

    def far(self, buf, step):
        first, second = self.p.pieces(step)
        self.arrived(buf, *first)
        self.onward(buf, *first).start()
        self.arrived(buf, *second)

    def end(self, buf):
        p = self.p
        for half in range(2):
            for dx in range(1, p.d.x_n):
                self.copy(buf, p.s, half, 0, p.slot(2 * dx)).wait_send()
                self.onward(buf, p.slot(2 * dx), half).wait_send()
            self.copy(buf, p.s, half, 0, p.partner).wait_send()


class Scatter:
    def __init__(self, p, part, near, far, near_send, near_recv, far_send, far_recv):
        self.p, self.part, self.near, self.far = p, part, near, far
        self.near_send, self.near_recv, self.far_send, self.far_recv = near_send, near_recv, far_send, far_recv

    def near_copy(self, x, half):
        p = self.p
        return rcopy(
            self.part.at[x * 2 + (p.c + 1) % 2, half],
            self.near.at[x, half],
            self.near_send.at[x, half],
            self.near_recv.at[x, half],
            (p.r, p.partner),
        )

    def far_copy(self, x, half, source):
        p = self.p
        goal = x * 2 + p.c
        return rcopy(
            self.part.at[goal, half],
            self.far.at[source, half],
            self.far_send.at[x, half],
            self.far_recv.at[source, half],
            (p.r, goal),
        )

    def put(self, step):
        if isinstance(step, int):
            if step == 1:
                for half in range(2):
                    self.near_copy(self.p.x, half).start()
        else:
            self.near_copy(self.p.slot(step // 2 * 2) // 2, step % 2).start()

    def cross(self, step):
        p = self.p
        slot, half = p.slot(step // 2 * 2), step % 2
        x = slot // 2
        self.near_copy(x, half).wait_recv()
        size = min(64, p.d.half)

        @pl.loop(0, p.d.half // size)
        def _(i):
            rows = pl.ds(pl.multiple_of(i * size, size), size)
            both = self.part[slot, half, rows].astype(F32) + self.near[x, half, rows].astype(F32)
            self.part[slot, half, rows] = both.astype(BF)

        self.far_copy(x, half, p.x).start()

    def arrive(self, half):
        p = self.p
        self.near_copy(p.x, half).wait_recv()
        for dx in range(1, p.d.x_n):
            x = (p.x + dx) % p.d.x_n
            self.far_copy(x, half, x).wait_recv()

    def total(self, half, rows):
        p = self.p
        value = self.part[p.s, half, rows].astype(F32) + self.near[p.x, half, rows].astype(F32)
        for dx in range(1, p.d.x_n):
            value = value + self.far[(p.x + dx) % p.d.x_n, half, rows].astype(F32)
        return value

    def end(self):
        p = self.p
        for half in range(2):
            for dx in range(p.d.x_n):
                x = (p.x + dx) % p.d.x_n
                self.near_copy(x, half).wait_send()
                if dx:
                    self.far_copy(x, half, p.x).wait_send()


class SmallSum:
    def __init__(self, p, first, sp_in, mid_a, z_in, mid_b, y_in, sp_sem, z_sem, y_sem):
        self.p = p
        self.bufs = ((first, sp_in, sp_sem), (mid_a, z_in, z_sem), (mid_b, y_in, y_sem))

    def plan(self, stage):
        p = self.p
        if stage == 0:
            return p.s, [(p.slot(t), (p.r, p.slot(t))) for t in range(1, p.d.sp_n)]
        if stage == 1:
            return p.z, [(p.zpeer(k), p.dev(p.zpeer(k), p.y)) for k in range(1, p.d.z_n)]
        return p.y, [(p.ypeer(k), p.dev(p.z, p.ypeer(k))) for k in range(1, p.d.y_n)]

    def start(self, stage):
        src, dst, sem = self.bufs[stage]
        own, peers = self.plan(stage)
        for index, device in peers:
            rcopy(src, dst.at[own], sem.at[0, index], sem.at[1, own], device).start()

    def finish(self, stage, result):
        src, dst, sem = self.bufs[stage]
        own, peers = self.plan(stage)
        value = src[...]
        for index, device in peers:
            rcopy(src, dst.at[index], sem.at[0, index], sem.at[1, index], device).wait_recv()
            value = value + dst[index]
        result[...] = value
        for index, device in peers:
            rcopy(src, dst.at[own], sem.at[0, index], sem.at[1, own], device).wait_send()


def small_scratch(d):
    return [
        ("sp_in", pltpu.VMEM((d.sp_n, 8, d.width), F32)),
        ("mid_a", pltpu.VMEM((8, d.width), F32)),
        ("z_in", pltpu.VMEM((d.z_n, 8, d.width), F32)),
        ("mid_b", pltpu.VMEM((8, d.width), F32)),
        ("y_in", pltpu.VMEM((d.y_n, 8, d.width), F32)),
        ("sp_sem", pltpu.SemaphoreType.DMA((2, d.sp_n))),
        ("z_sem", pltpu.SemaphoreType.DMA((2, d.z_n))),
        ("y_sem", pltpu.SemaphoreType.DMA((2, d.y_n))),
    ]


def comm_scratch(d):
    return [
        ("part", pltpu.VMEM((d.sp_n, 2, d.half, d.width), BF)),
        ("near", pltpu.VMEM((d.x_n, 2, d.half, d.width), BF)),
        ("far", pltpu.VMEM((d.x_n, 2, d.half, d.width), BF)),
        ("ag_send", pltpu.SemaphoreType.DMA((2, d.sp_n, 2))),
        ("ag_recv", pltpu.SemaphoreType.DMA((d.sp_n, 2))),
        ("near_send", pltpu.SemaphoreType.DMA((d.x_n, 2))),
        ("near_recv", pltpu.SemaphoreType.DMA((d.x_n, 2))),
        ("far_send", pltpu.SemaphoreType.DMA((d.x_n, 2))),
        ("far_recv", pltpu.SemaphoreType.DMA((d.x_n, 2))),
    ]


def term_scratch(d, l, term):
    w, first, last = d.terms[term]
    block = (last - first,) + d.block_shape(w)[1:]
    z_first = term in d.z_first[l]
    y_shape = (max(1, d.y_n - 1), 1 if z_first else d.z_n) + block
    z_shape = (5, d.y_n if z_first else 1) + block
    return [
        ("y_in_%d_%d" % (l, term), pltpu.VMEM(y_shape, BF)),
        ("z_in_%d_%d" % (l, term), pltpu.VMEM(z_shape, BF)),
    ]


SAVED = XIN, PROJ, ATT, PROBS, XMID, HID, SLOPE, STREAM, MID = (
    "xin",
    "qkv",
    "att",
    "probs",
    "xmid",
    "hid",
    "slope",
    "stream",
    "mid",
)
ONCE = (PROJ, ATT, PROBS, HID, SLOPE)
WEIGHTS = W_QKV, W_OUT, W_UP, W_DOWN = ("wqkv", "wout", "wup", "wdown")


def saved_shapes(d):
    full = (d.sp_n, 2, d.half)
    return {
        XIN: (full + (d.width,), BF),
        PROJ: (full + (3 * d.dh,), BF),
        ATT: (full + (d.dh,), BF),
        PROBS: ((d.heads, len(d.pairs), d.tok, d.tok), BF),
        XMID: (full + (d.width,), BF),
        HID: (full + (d.hid,), BF),
        SLOPE: (full + (d.hid,), BF),
        STREAM: ((2, d.half, d.width), F32),
        MID: ((2, d.half, d.width), F32),
    }


def weight_shapes(d):
    return {name: ((d.z_n, d.y_n) + d.block_shape(i), BF) for i, name in enumerate(WEIGHTS)}


class Fetch:
    def __init__(self, p, o):
        self.p, self.o = p, o
        self.full = (o.wqkv, o.wout, o.wup, o.wdown)

    def spread(self, l, w):
        p, o = self.p, self.o
        own = self.full[w].at[l, p.z, p.y]
        if w in (QKV, UP):
            src = o.in_qkv if w == QKV else o.in_up
            for t in range(1, p.d.sp_n):
                j = p.slot(t)
                rcopy(src.at[l, j], own.at[p.s], o.s_send.at[l, w, j], o.s_recv.at[l, w, p.s], (p.r, j)).start()
            pltpu.make_async_copy(src.at[l, p.s], own.at[p.s], o.own_sem.at[l, w]).start()
        elif w == DOWN:
            pltpu.make_async_copy(o.in_down.at[l], own, o.own_sem.at[l, w]).start()
        else:
            goal, _, stays = p.moved()

            @pl.when(stays)
            def _():
                pltpu.make_async_copy(o.in_out.at[l], own, o.own_sem.at[l, w]).start()

            @pl.when(jnp.logical_not(stays))
            def _():
                there = self.full[w].at[l, goal[0] // p.d.y_n, goal[0] % p.d.y_n]
                rcopy(o.in_out.at[l], there, o.s_send.at[l, w, 0], o.s_recv.at[l, w, 0], goal).start()

    def own(self, l, w):
        p, o = self.p, self.o
        own = self.full[w].at[l, p.z, p.y]
        if w in (QKV, UP):
            src = o.in_qkv if w == QKV else o.in_up
            pltpu.make_async_copy(src.at[l, p.s], own.at[p.s], o.own_sem.at[l, w]).wait()
            for t in range(1, p.d.sp_n):
                j = p.slot(t)
                rcopy(src.at[l, j], own.at[j], o.s_send.at[l, w, j], o.s_recv.at[l, w, j], (p.r, j)).wait_recv()
        elif w == DOWN:
            pltpu.make_async_copy(o.in_down.at[l], own, o.own_sem.at[l, w]).wait()
        else:
            goal, _, stays = p.moved()

            @pl.when(stays)
            def _():
                pltpu.make_async_copy(o.in_out.at[l], own, o.own_sem.at[l, w]).wait()

            @pl.when(jnp.logical_not(stays))
            def _():
                rcopy(o.in_out.at[l], own, o.s_send.at[l, w, 0], o.s_recv.at[l, w, 0], goal).wait_recv()

    def block(self, l, piece, z, y):
        w, first, last, _ = self.p.d.pieces[piece]
        return self.full[w].at[l, z, y, first:last]

    def columns(self, piece):
        p = self.p
        if self.p.d.pieces[piece][3]:
            return [p.y] + [p.ypeer(m) for m in range(1, p.d.y_n)]
        return [p.y]

    def copy(self, l, piece, z, y, way, device):
        o = self.o
        block = self.block(l, piece, z, y)
        return rcopy(block, block, o.b_send.at[l, piece, z, y, way], o.b_recv.at[l, piece, z, y], device)

    def arrived(self, l, piece, z, y):
        self.copy(l, piece, z, y, 0, (self.p.r, self.p.s)).wait_recv()

    def along_z(self, l, piece, role, y, act):
        p = self.p
        if p.d.z_n == 1 or role == 3:
            return
        inside, at = p.line()
        z = at[role]

        @pl.when(inside)
        def _():
            for way, goal in enumerate(((at[1], at[2]), (at[2], at[3]), (at[1],))[role]):
                act(self.copy(l, piece, z, y, way, p.dev(goal, p.y)))

        if role == 0:

            @pl.when(jnp.logical_not(inside))
            def _():
                act(self.copy(l, piece, z, y, 0, p.dev(at[1], p.y)))

    def along_y(self, l, piece, role, act):
        p = self.p
        z = p.line()[1][role]
        for m in range(1, p.d.y_n):
            act(self.copy(l, piece, z, p.y, 1 + m, p.dev(p.z, p.ypeer(m))))

    def start_z(self, l, *pieces):
        for piece in pieces:
            self.along_z(l, piece, 0, self.p.y, lambda c: c.start())

    def start_y(self, l, *pieces):
        for piece in pieces:
            self.along_y(l, piece, 0, lambda c: c.start())

    def inner(self, l, *pieces):
        if self.p.d.z_n > 1:

            @pl.when(self.p.line()[0])
            def _():
                for piece in pieces:
                    self.relay(l, piece, 2)

    def outer(self, l, *pieces):
        if self.p.d.z_n > 1:

            @pl.when(jnp.logical_not(self.p.line()[0]))
            def _():
                for piece in pieces:
                    self.relay(l, piece, 2)

    def relay(self, l, piece, *roles):
        p = self.p
        cross_first = p.d.pieces[piece][3]
        at = p.line()[1]
        for role in roles:
            if role == 1 and cross_first:
                for y in self.columns(piece)[1:]:
                    self.arrived(l, piece, p.z, y)
                    self.along_z(l, piece, 0, y, lambda c: c.start())
            if p.d.z_n == 1:
                continue
            for y in self.columns(piece):
                self.arrived(l, piece, at[role], y)
                self.along_z(l, piece, role, y, lambda c: c.start())
            if not cross_first:
                self.along_y(l, piece, role, lambda c: c.start())

    def ready(self, l, *pieces):
        p = self.p
        for piece in pieces:
            if not p.d.pieces[piece][3]:
                for role in range(4 if p.d.z_n > 1 else 1):
                    for m in range(1, p.d.y_n):
                        self.arrived(l, piece, p.line()[1][role], p.ypeer(m))

    def save(self, l, w):
        return pltpu.make_async_copy(self.full[w].at[l], self.o.w_save[w].at[l], self.o.w_sem.at[l, w])

    def end(self):
        p, o = self.p, self.o
        for l in range(p.d.layers):
            for w in range(4):
                own = self.full[w].at[l, p.z, p.y]
                if w in (QKV, UP):
                    src = o.in_qkv if w == QKV else o.in_up
                    for t in range(1, p.d.sp_n):
                        j = p.slot(t)
                        rcopy(src.at[l, j], own.at[p.s], o.s_send.at[l, w, j], o.s_recv.at[l, w, p.s], (p.r, j)).wait_send()
                elif w == OUT:
                    goal, _, stays = p.moved()

                    @pl.when(jnp.logical_not(stays))
                    def _():
                        rcopy(o.in_out.at[l], own, o.s_send.at[l, w, 0], o.s_recv.at[l, w, 0], goal).wait_send()

                self.save(l, w).wait()
            for piece in range(len(p.d.pieces)):
                for role in range(4 if p.d.z_n > 1 else 1):
                    for y in self.columns(piece):
                        self.along_z(l, piece, role, y, lambda c: c.wait_send())
                    if role == 0 or not p.d.pieces[piece][3]:
                        self.along_y(l, piece, role, lambda c: c.wait_send())


class Refs:
    pass


def mean_of(v):
    return jnp.mean(v, axis=-1, keepdims=True)


def norm_rows(v, gain):
    center = v - mean_of(v)
    return center * lax.rsqrt(mean_of(center * center) + EPS) * gain


def row_loop(tok, body, step=32):
    step = min(step, tok)

    @pl.loop(0, tok // step, unroll=True)
    def _(i):
        body(pl.ds(pl.multiple_of(i * step, step), step))


def lay_out(d, o):
    for i in range(d.sp_n):
        where = jnp.int32(0)
        for j in range(1, d.sp_n):
            where = jnp.where(o.in_order[0, j] == i, j, where)
        o.meta[0, i] = where
        o.meta[1, i] = o.in_order[0, i]
    start = jnp.int32(0)
    for b in range(d.docs):
        o.meta[2, b] = start
        start = start + o.in_lengths[0, b]


def up_columns(d, j, k):
    first = (k * d.sp_n + j) * d.hid_own
    return slice(first, first + d.hid_own), slice(k * d.hid_own, (k + 1) * d.hid_own)


def attention_forward(d, o, l):
    tok = d.tok
    slopes = []
    for h in range(d.heads):
        head = (lax.axis_index(AXES[1]) * d.heads + (h + 1)).astype(F32)
        slopes.append(jnp.exp2(jnp.full((1, 1), -8.0 / HEADS, F32) * head))
    for i in range(d.sp_n):
        here = o.meta[0, i]
        pos = i * tok + lax.broadcasted_iota(jnp.int32, (tok, 1), 0)
        start = jnp.zeros((tok, 1), jnp.int32)
        for b in range(1, d.docs):
            start = jnp.where(pos >= o.meta[2, b], o.meta[2, b], start)
        blocks = range(max(0, i - d.back), i + 1)
        for h in range(d.heads):
            lanes = slice(h * HD, (h + 1) * HD)
            query = o.qkv[0, here, :, :, lanes].reshape(tok, HD)
            scores = []
            for b in blocks:
                keys = o.qkv[0, o.meta[0, b], :, :, d.dh + h * HD : d.dh + (h + 1) * HD].reshape(tok, HD)
                key_pos = b * tok + lax.broadcasted_iota(jnp.int32, (tok, tok), 1)
                query_pos = i * tok + lax.broadcasted_iota(jnp.int32, (tok, tok), 0)
                score = nt(query, keys) * HD ** (-0.5) + slopes[h] * (key_pos - query_pos).astype(F32)
                allowed = key_pos >= start
                if b == i:
                    allowed = allowed & (key_pos <= query_pos)
                scores.append(jnp.where(allowed, score, MASKED))
            top = scores[0].max(axis=-1, keepdims=True)
            for score in scores[1:]:
                top = jnp.maximum(top, score.max(axis=-1, keepdims=True))
            expo = [jnp.exp(score - top) for score in scores]
            total = expo[0].sum(axis=-1, keepdims=True)
            for part in expo[1:]:
                total = total + part.sum(axis=-1, keepdims=True)
            inverse = 1.0 / total
            result = None
            for b, part in zip(blocks, expo):
                low = (part * inverse).astype(BF)
                o.probs[0, h, d.pairs.index((i, b))] = low
                values = o.qkv[0, o.meta[0, b], :, :, 2 * d.dh + h * HD : 2 * d.dh + (h + 1) * HD].reshape(tok, HD)
                term = nn(low, values)
                result = term if result is None else result + term
            o.sorted_att[i, :, :, lanes] = result.astype(BF).reshape(2, d.half, HD)


def fwd_kernel(d, names, *refs):
    o = Refs()
    for name, ref in zip(names, refs):
        setattr(o, name, ref)
    o.w_save = (o.o_wqkv, o.o_wout, o.o_wup, o.o_wdown)
    p = Place(d)
    fetch = Fetch(p, o)
    gather = Gather(p, o.ag_send, o.ag_recv)
    scatter = Scatter(p, o.part, o.near, o.far, o.near_send, o.near_recv, o.far_send, o.far_recv)
    small = SmallSum(p, o.in_gains, o.sp_in, o.mid_a, o.z_in, o.mid_b, o.y_in, o.sp_sem, o.z_sem, o.y_sem)

    def save(name, l):
        ref, out = getattr(o, name), getattr(o, "o_" + name)
        held = 0 if name in ONCE else l
        return pltpu.make_async_copy(ref.at[held], out.at[l], o.save_sem.at[l, SAVED.index(name)])

    def free(l, *names):
        if l > 0:
            for name in names:
                save(name, l - 1).wait()

    late = Gather(p, o.late_send, o.late_recv)
    keep_gl = pltpu.make_async_copy(o.gl, o.o_gl, o.late_sem.at[0])

    def run(slot):
        for op, l, piece in FORWARD_PLAN.get(slot, ()):
            if op == LATE_START:
                o.gl[p.s, piece] = o.in_cotangent[piece]
                late.start(o.gl, piece)
            elif op == LATE_ON:
                for step in range(2 + piece, d.sp_n, 2):
                    late.through(o.gl, step)
            elif op == LATE_END:
                late.rest(o.gl)
                keep_gl.start()
            elif op == RELAY_1:
                fetch.relay(l, piece, 1)
            elif op == RELAY_3:
                fetch.relay(l, piece, 3)
            else:
                act = {
                    SPREAD: fetch.spread,
                    OWN: fetch.own,
                    START_Z: fetch.start_z,
                    START_Y: fetch.start_y,
                    INNER: fetch.inner,
                    OUTER: fetch.outer,
                }[op]
                act(l, piece)

    def place(l):
        if d.whole_lanes:
            for j in range(d.sp_n):
                for i in range(3):
                    o.in_qkv[l, j, :, i * d.dh : (i + 1) * d.dh] = o.raw_qkv[l, i, :, j * d.dh : (j + 1) * d.dh]
                for k in range(d.dp_n):
                    whole, kept = up_columns(d, j, k)
                    o.in_up[l, j, :, kept] = o.raw_up[l, :, whole]

    place(0)
    p.barrier()
    for w in (QKV, OUT):
        fetch.spread(0, w)
    small.start(0)
    for l in range(1, d.layers):
        place(l)
    lay_out(d, o)
    for w in (UP, DOWN):
        fetch.spread(0, w)
    run(0)
    small.finish(0, o.mid_a)
    small.start(1)
    run(1)
    small.finish(1, o.mid_b)
    small.start(2)
    run(2)
    small.finish(2, o.o_gains)

    def norm_in(l, half, gain):
        def first(rows):
            v = o.in_tokens[half, rows].astype(F32)
            o.stream[0, half, rows] = v
            o.xin[0, p.s, half, rows] = norm_rows(v, gain).astype(BF)

        row_loop(d.half, first)

    for half in range(2):
        norm_in(0, half, o.o_gains[0:1, :])
        gather.start(o.xin.at[0], half)

    top = d.layers - 1
    for l in range(d.layers):
        gain_mid = o.o_gains[2 * l + 1 : 2 * l + 2, :]
        xin, xmid = o.xin.at[l], o.xmid.at[l]
        save(STREAM, l).start()
        run(3 + 10 * l)
        fetch.ready(l, 0)
        fetch.save(l, QKV).start()
        free(l, PROJ)
        third = 3 * d.dh // 3

        def project(pieces):
            block = pair(xin, pieces)
            for n in range(3):
                cols = slice(n * third, (n + 1) * third)
                weight = o.wqkv[l, :, :, :, :, cols].reshape(d.width, third)
                put_pair(o.qkv.at[0], pieces, cols, nn(block, weight))

        project(p.pieces(0))
        gather.near(xin)
        project(p.pieces(1))
        run(4 + 10 * l)

        @pl.loop(2, d.sp_n)
        def _(t):
            gather.far(xin, t)
            project(p.pieces(t))

        gather.end(xin)
        save(XIN, l).start()
        save(PROJ, l).start()
        run(5 + 10 * l)
        free(l, PROBS, ATT)
        attention_forward(d, o, l)
        save(PROBS, l).start()
        run(6 + 10 * l)
        fetch.ready(l, 1)
        fetch.save(l, OUT).start()

        def out_part(pieces):
            blocks = []
            for slot, half in pieces:
                block = o.sorted_att[o.meta[1, slot], half]
                o.att[0, slot, half] = block
                blocks.append(block)
            block = jnp.concatenate(blocks, axis=0)
            for n in range(d.n_width):
                cols = slice(n * d.chunk, (n + 1) * d.chunk)
                weight = o.wout[l, :, :, :, cols].reshape(d.dh, d.chunk)
                put_pair(o.part, pieces, cols, nn(block, weight))

        @pl.loop(2, d.sp_n)
        def _(t):
            out_part(p.pieces(t))
            scatter.put(t)

            @pl.when(t > 2)
            def _():
                scatter.cross(t - 1)

        out_part(p.pieces(1))
        scatter.put(1)
        scatter.cross(d.sp_n - 1)
        out_part(p.pieces(0))
        save(ATT, l).start()
        run(7 + 10 * l)

        def middle(half, rows):
            v = o.stream[l, half, rows] + scatter.total(half, rows)
            o.mid[l, half, rows] = v
            xmid[p.s, half, rows] = norm_rows(v, gain_mid).astype(BF)

        for half in range(2):
            scatter.arrive(half)
            row_loop(d.half, functools.partial(middle, half))
            gather.start(xmid, half)
            if half == 0:
                run(8 + 10 * l)
        scatter.end()
        save(MID, l).start()
        run(9 + 10 * l)
        fetch.ready(l, 2, 3)
        fetch.save(l, UP).start()
        free(l, HID, SLOPE)

        def up(pieces):
            block = pair(xmid, pieces)
            for n in range(d.n_hid):
                cols = slice(n * d.chunk, (n + 1) * d.chunk)
                weight = o.wup[l, :, :, :, :, cols].reshape(d.width, d.chunk)
                pre = nn(block, weight)
                phi = 0.5 * (1.0 + lax.erf(pre * (0.5**0.5)))
                put_pair(o.hid.at[0], pieces, cols, pre * phi)
                density = jnp.exp(-0.5 * pre * pre) * 0.3989422804014327
                put_pair(o.slope.at[0], pieces, cols, phi + pre * density)

        def down(pieces):
            hidden = pair(o.hid.at[0], pieces)
            for n in range(d.n_width):
                cols = slice(n * d.chunk, (n + 1) * d.chunk)
                weight = o.wdown[l, :, :, :, cols].reshape(d.hid, d.chunk)
                put_pair(o.part, pieces, cols, nn(hidden, weight))

        up(p.pieces(0))
        gather.near(xmid)
        up(p.pieces(1))
        run(10 + 10 * l)
        if l == 0:

            @pl.loop(2, d.sp_n)
            def _(t):
                gather.far(xmid, t)
                up(p.pieces(t))

        fetch.ready(l, 4, 5)
        fetch.save(l, DOWN).start()

        @pl.loop(2, d.sp_n)
        def _(t):
            if l > 0:
                gather.far(xmid, t)
                up(p.pieces(t))
                if l < top:

                    @pl.when(t > 2)
                    def _():
                        scatter.cross(t - 1)

            down(p.pieces(t))
            if l < top:
                scatter.put(t)
            if l == 0 and l < top:

                @pl.when(t > 2)
                def _():
                    scatter.cross(t - 1)

        down(p.pieces(1))
        if l < top:
            scatter.put(1)
            scatter.cross(d.sp_n - 1)
        down(p.pieces(0))
        gather.end(xmid)
        save(XMID, l).start()
        save(HID, l).start()
        save(SLOPE, l).start()
        if l == top:
            keep_part = pltpu.make_async_copy(o.part, o.o_part, o.late_sem.at[1])
            keep_part.start()
            continue
        run(11 + 10 * l)

        def last(half, rows):
            v = o.mid[l, half, rows] + scatter.total(half, rows)
            o.stream[l + 1, half, rows] = v
            o.xin[l + 1, p.s, half, rows] = norm_rows(v, o.o_gains[2 * l + 2 : 2 * l + 3, :]).astype(BF)

        for half in range(2):
            scatter.arrive(half)
            row_loop(d.half, functools.partial(last, half))
            gather.start(o.xin.at[l + 1], half)
            if half == 0:
                run(12 + 10 * l)
        scatter.end()

    keep_part.wait()
    fetch.end()
    late.end(o.gl)
    keep_gl.wait()
    for l in range(d.layers):
        for name in SAVED:
            if l == d.layers - 1 or name not in ONCE:
                save(name, l).wait()


class Reduce:
    def __init__(self, p, o):
        self.p, self.o = p, o
        self.grads = (o.g_qkv, o.g_out, o.g_up, o.g_down)
        self.sp_in = (o.x_qkv, o.x_out, o.x_up, None)
        self.result = (o.o_qkv, o.o_out, o.o_up, o.o_down)
        self.done = {}

    def grad(self, l, w):
        return self.o.g_up_odd if w == UP and l % 2 else self.grads[w]

    def z_first(self, l, term):
        return term in self.p.d.z_first[l]

    def ins(self, l, term):
        o = self.o
        return getattr(o, "y_in_%d_%d" % (l, term)), getattr(o, "z_in_%d_%d" % (l, term))

    def columns(self, l, term):
        p = self.p
        if self.z_first(l, term):
            return [(y, y) for y in [p.y] + [p.ypeer(m) for m in range(1, p.d.y_n)]]
        return [(p.y, 0)]

    def step(self, l, *terms):
        for term in terms:
            stages = (self.y_send, self.y_sum, self.inner, self.finish_z)
            if self.z_first(l, term):
                stages = (self.z_send, self.inner, self.z_sum, self.finish_y)
            count = self.done.get((l, term), 0)
            self.done[l, term] = count + 1
            stages[count](l, term)

    def groups(self, term):
        w, first, last = self.p.d.terms[term]
        if w in (QKV, UP):
            return [((j,), (j - first,)) for j in range(first, last)]
        rows = min(32, last - first)
        return [
            ((slice(j, j + rows),), (slice(j - first, j - first + rows),)) for j in range(first, last, rows)
        ]

    def y_copy(self, l, term, k):
        p, o = self.p, self.o
        w, first, last = p.d.terms[term]
        index = p.d.y_n - k - 1
        there = p.ypeer(k)
        into = self.ins(l, term)[0].at[index]
        if self.z_first(l, term):
            src, into = self.grad(l, w).at[p.z, there, first:last], into.at[0]
        else:
            src = self.grad(l, w).at[:, there, first:last]
        return rcopy(src, into, o.ry_send.at[l, term, k], o.ry_recv.at[l, term, index], p.dev(p.z, there))

    def y_send(self, l, term):
        for k in range(1, self.p.d.y_n):
            self.y_copy(l, term, k).start()

    def y_wait(self, l, term):
        for k in range(1, self.p.d.y_n):
            self.y_copy(l, term, self.p.d.y_n - k).wait_recv()

    def y_sum(self, l, term):
        p = self.p
        w = p.d.terms[term][0]
        y_in, _ = self.ins(l, term)
        self.y_wait(l, term)
        for z in range(p.d.z_n):
            for index, here in self.groups(term):
                value = self.grad(l, w)[(z, p.y) + index].astype(F32)
                for m in range(p.d.y_n - 1):
                    value = value + y_in[(m, z) + here].astype(F32)
                self.grad(l, w)[(z, p.y) + index] = value.astype(BF)
        self.z_send(l, term)

    def z_copy(self, l, term, column, z, goal, place, way):
        p, o = self.p, self.o
        w, first, last = p.d.terms[term]
        y, slot = column
        return rcopy(
            self.grad(l, w).at[z, y, first:last],
            self.ins(l, term)[1].at[place, slot],
            o.rz_send.at[l, term, slot, way],
            o.rz_recv.at[l, term, slot, place],
            p.dev(goal, p.y),
        )

    def z_goals(self, inside):
        at = self.p.line()[1]
        if inside:
            return ((at[3], at[2], 3), (at[2], at[2], 1), (at[1], at[1], 0))
        return ((at[1], at[1], 0), (at[2], at[1], 2), (at[3], at[2], 4))

    def both(self, inner, outer):
        inside, _ = self.p.line()
        pl.when(inside)(inner)
        pl.when(jnp.logical_not(inside))(outer)

    def z_send(self, l, term):
        if self.p.d.z_n == 1:
            return

        def send(inside, ways):
            for column in self.columns(l, term):
                for way in ways:
                    self.z_copy(l, term, column, *self.z_goals(inside)[way], way).start()

        self.both(lambda: send(True, (0,)), lambda: send(False, (0, 1, 2)))

    def z_wait(self, l, term, column, place):
        self.z_copy(l, term, column, self.p.z, self.p.z, place, 0).wait_recv()

    def inner(self, l, term):
        p = self.p
        if p.d.z_n == 1:
            return
        w = p.d.terms[term][0]
        _, z_in = self.ins(l, term)

        def relay():
            for way, places in ((1, (2,)), (2, (3, 4))):
                z, goal, place = self.z_goals(True)[way]
                for column in self.columns(l, term):
                    y, slot = column
                    for source in places:
                        self.z_wait(l, term, column, source)
                    for index, here in self.groups(term):
                        value = self.grad(l, w)[(z, y) + index].astype(F32)
                        for source in places:
                            value = value + z_in[(source, slot) + here].astype(F32)
                        self.grad(l, w)[(z, y) + index] = value.astype(BF)
                    self.z_copy(l, term, column, z, goal, place, way).start()

        pl.when(p.line()[0])(relay)

    def z_total(self, l, term, column, store):
        p = self.p
        w = p.d.terms[term][0]
        _, z_in = self.ins(l, term)
        y, slot = column

        def total(places):
            for source in places:
                self.z_wait(l, term, column, source)
            for index, here in self.groups(term):
                value = self.grad(l, w)[(p.z, y) + index].astype(F32)
                for source in places:
                    value = value + z_in[(source, slot) + here].astype(F32)
                store(y, index, here, value)

        if p.d.z_n == 1:
            total(())
        else:
            self.both(lambda: total((0, 1)), lambda: total((0,)))

    def z_sum(self, l, term):
        w = self.p.d.terms[term][0]

        def store(y, index, here, value):
            self.grad(l, w)[(self.p.z, y) + index] = value.astype(BF)

        for column in self.columns(l, term):
            self.z_total(l, term, column, store)
        self.y_send(l, term)

    def finish_z(self, l, term):
        def store(y, index, here, value):
            self.settle(l, term, index, value)

        self.z_total(l, term, self.columns(l, term)[0], store)
        self.pass_on(l, term)

    def finish_y(self, l, term):
        p = self.p
        w = p.d.terms[term][0]
        y_in, _ = self.ins(l, term)
        self.y_wait(l, term)
        for index, here in self.groups(term):
            value = self.grad(l, w)[(p.z, p.y) + index].astype(F32)
            for m in range(p.d.y_n - 1):
                value = value + y_in[(m, 0) + here].astype(F32)
            self.settle(l, term, index, value)
        self.pass_on(l, term)

    def settle(self, l, term, index, value):
        w = self.p.d.terms[term][0]
        if w == DOWN:
            self.result[w][(l,) + index] = value.astype(BF)
        else:
            self.grad(l, w)[(self.p.z, self.p.y) + index] = value.astype(BF)

    def s_copy(self, l, w, j, source):
        p, o = self.p, self.o
        return rcopy(
            self.grad(l, w).at[p.z, p.y, j], self.sp_in[w].at[l, source], o.rs_send.at[l, w, j], o.rs_recv.at[l, w, source], (p.r, j)
        )

    def out_copy(self, l, device):
        p, o = self.p, self.o
        return rcopy(
            self.grad(l, OUT).at[p.z, p.y], self.sp_in[OUT].at[l], o.rs_send.at[l, OUT, 0], o.rs_recv.at[l, OUT, 0], device
        )

    def keep(self, l, w, j, ref):
        d, result = self.p.d, self.result[w]
        if not d.whole_lanes:
            result[l, j] = ref[...]
        elif w == QKV:
            for i in range(3):
                result[l, i, :, j * d.dh : (j + 1) * d.dh] = ref[:, i * d.dh : (i + 1) * d.dh]
        else:
            for k in range(d.dp_n):
                whole, kept = up_columns(d, j, k)
                result[l, :, whole] = ref[:, kept]

    def pass_on(self, l, term):
        p = self.p
        w, first, last = p.d.terms[term]
        if w in (QKV, UP):
            for j in range(first, last):

                @pl.when(p.s == j)
                def _():
                    self.keep(l, w, j, self.grad(l, w).at[p.z, p.y, j])

                @pl.when(p.s != j)
                def _():
                    self.s_copy(l, w, j, p.s).start()

        elif w == OUT:
            _, source, stays = p.moved()

            @pl.when(stays)
            def _():
                self.result[w][l] = self.grad(l, w)[p.z, p.y]

            @pl.when(jnp.logical_not(stays))
            def _():
                self.out_copy(l, source).start()

    def sent(self, l, w):
        p = self.p
        for term, (kind, first, last) in enumerate(p.d.terms):
            if kind != w:
                continue
            for k in range(1, p.d.y_n):
                self.y_copy(l, term, k).wait_send()
            if p.d.z_n > 1:

                def wait(inside):
                    for column in self.columns(l, term):
                        for way in range(3):
                            self.z_copy(l, term, column, *self.z_goals(inside)[way], way).wait_send()

                self.both(lambda: wait(True), lambda: wait(False))
        if w in (QKV, UP):
            for t in range(1, p.d.sp_n):
                self.s_copy(l, w, p.slot(t), p.s).wait_send()
        elif w == OUT:
            _, source, stays = p.moved()

            @pl.when(jnp.logical_not(stays))
            def _():
                self.out_copy(l, source).wait_send()

    def last(self, l, w):
        p = self.p
        if w in (QKV, UP):
            for j in range(p.d.sp_n):

                @pl.when(p.s != j)
                def _():
                    self.s_copy(l, w, j, j).wait_recv()
                    self.keep(l, w, j, self.sp_in[w].at[l, j])
        elif w == OUT:
            _, source, stays = p.moved()

            @pl.when(jnp.logical_not(stays))
            def _():
                self.out_copy(l, source).wait_recv()
                self.result[w][l] = self.sp_in[w][l]


def norm_back(v, d_out, gain):
    center = v - mean_of(v)
    inverse = lax.rsqrt(mean_of(center * center) + EPS)
    unit = center * inverse
    gain_term = jnp.sum(d_out * unit, axis=0, keepdims=True)
    e = d_out * gain
    back = (e - mean_of(e) - unit * mean_of(e * unit)) * inverse
    return back, gain_term


def attention_backward(d, o):
    tok = d.tok
    for i in range(d.sp_n):
        here = o.meta[0, i]
        blocks = range(max(0, i - d.back), i + 1)
        for h in range(d.heads):
            lanes = slice(h * HD, (h + 1) * HD)
            key_lanes = slice(d.dh + h * HD, d.dh + (h + 1) * HD)
            value_lanes = slice(2 * d.dh + h * HD, 2 * d.dh + (h + 1) * HD)
            query = o.qkv[here, :, :, lanes].reshape(tok, HD)
            grad = o.d_att[here, :, :, lanes].reshape(tok, HD)
            d_probs, inner = [], None
            for b in blocks:
                low = o.probs[h, d.pairs.index((i, b))].astype(F32)
                term = nt(grad, o.qkv[o.meta[0, b], :, :, value_lanes].reshape(tok, HD))
                d_probs.append(term)
                weighted = jnp.sum(low * term, axis=-1, keepdims=True)
                inner = weighted if inner is None else inner + weighted
            d_query = None
            for b, term in zip(blocks, d_probs):
                low = o.probs[h, d.pairs.index((i, b))]
                d_score = (low.astype(F32) * (term - inner)).astype(BF)
                step = nn(d_score, o.qkv[o.meta[0, b], :, :, key_lanes].reshape(tok, HD))
                d_query = step if d_query is None else d_query + step
                d_key, d_value = tn(d_score, query), tn(low, grad)
                if b == i:
                    o.d_keys[b, :, lanes] = d_key
                    o.d_values[b, :, lanes] = d_value
                else:
                    o.d_keys[b, :, lanes] += d_key
                    o.d_values[b, :, lanes] += d_value
            o.sorted_dqkv[i, :, :, lanes] = (d_query * HD ** (-0.5)).astype(BF).reshape(2, d.half, HD)
    for b in range(d.sp_n):
        shape = (2, d.half, d.dh)
        o.sorted_dqkv[b, :, :, d.dh : 2 * d.dh] = (o.d_keys[b] * HD ** (-0.5)).astype(BF).reshape(shape)
        o.sorted_dqkv[b, :, :, 2 * d.dh :] = o.d_values[b].astype(BF).reshape(shape)


def bwd_kernel(d, names, *refs):
    o = Refs()
    for name, ref in zip(names, refs):
        setattr(o, name, ref)
    p = Place(d)
    gather = Gather(p, o.ag_send, o.ag_recv)
    scatter = Scatter(p, o.part, o.near, o.far, o.near_send, o.near_recv, o.far_send, o.far_recv)
    small = SmallSum(p, o.gain_sum, o.sp_in, o.mid_a, o.z_in, o.mid_b, o.y_in, o.sp_sem, o.z_sem, o.y_sem)
    reduce = Reduce(p, o)
    loads = WEIGHTS + SAVED

    def load(name, l):
        ref = o.mid if name == STREAM else getattr(o, name)
        return pltpu.make_async_copy(getattr(o, "i_" + name).at[l], ref, o.load_sem.at[loads.index(name)])

    def refill(l, *which):
        if l > 0:
            for name in which:
                load(name, l - 1).start()

    def run(slot):
        for layer, term in BACKWARD_PLAN.get(slot, ()):
            reduce.step(layer, term)

    top = d.layers - 1
    first_grad = pltpu.make_async_copy(o.i_gl, o.gl, o.late_sem.at[0])
    first_grad.start()
    for name in (W_DOWN, SLOPE, W_UP, HID, XMID, MID, W_OUT, PROJ, PROBS, ATT, W_QKV, XIN):
        load(name, top).start()
    p.barrier()
    lay_out(d, o)
    o.gain_sum[...] = jnp.zeros_like(o.gain_sum)

    first_grad.wait()
    for half in range(2):

        def begin(rows):
            o.o_grad[half, rows] = o.gl[p.s, half, rows].astype(F32)

        row_loop(d.half, begin)
    tokens = d.sp_n * d.tok

    def rows_of(ref, n, count):
        part = ref[n * d.z_n // count : (n + 1) * d.z_n // count]
        return part.reshape(d.chunk, part.shape[-1])

    def weight_grad(out, left_ref, right_ref, count, width):
        for n in range(count):
            left = left_ref[:, :, :, n * d.chunk : (n + 1) * d.chunk].reshape(tokens, d.chunk)
            value = tn(left, right_ref[...].reshape(tokens, width)).astype(BF)
            zs = slice(n * d.z_n // count, (n + 1) * d.z_n // count)
            out[zs] = value.reshape((d.z_n // count,) + out.shape[1:])

    for l in reversed(range(d.layers)):
        gain_in = o.in_gains[2 * l : 2 * l + 1, :]
        gain_mid = o.in_gains[2 * l + 1 : 2 * l + 2, :]
        run(0 + 14 * (top - l))
        load(W_DOWN, l).wait()
        load(SLOPE, l).wait()
        load(W_UP, l).wait()

        def pre_grad(pieces):
            block = pair(o.gl, pieces)
            for n in range(d.n_hid):
                cols = slice(n * d.chunk, (n + 1) * d.chunk)
                d_hidden = nt(block, rows_of(o.wdown, n, d.n_hid))
                put_pair(o.slope, pieces, cols, d_hidden * pair(o.slope, pieces, cols).astype(F32))

        def mid_grad(pieces):
            d_pre = pair(o.slope, pieces)
            for n in range(d.n_width):
                cols = slice(n * d.chunk, (n + 1) * d.chunk)
                put_pair(o.part, pieces, cols, nt(d_pre, rows_of(o.wup, n, d.n_width)))

        if l < top:
            pre_grad(p.pieces(0))
            gather.near(o.gl)
            pre_grad(p.pieces(1))
        run(1 + 14 * (top - l))

        @pl.loop(2, d.sp_n)
        def _(t):
            if l < top:
                gather.far(o.gl, t)
            pre_grad(p.pieces(t))

            @pl.when(t > 2)
            def _():
                scatter.cross(t - 1)

            mid_grad(p.pieces(t))
            scatter.put(t)

        if l == top:
            pre_grad(p.pieces(1))
        mid_grad(p.pieces(1))
        scatter.put(1)
        scatter.cross(d.sp_n - 1)
        if l == top:
            pre_grad(p.pieces(0))
        mid_grad(p.pieces(0))
        if l < top:
            gather.end(o.gl)
        refill(l, W_DOWN, W_UP)
        load(HID, l).wait()
        run(2 + 14 * (top - l))
        if l < top:
            reduce.sent(l + 1, DOWN)
        weight_grad(o.g_down, o.hid, o.gl, d.n_hid, d.width)
        run(3 + 14 * (top - l))
        refill(l, HID)
        load(MID, l).wait()

        def middle(half, rows):
            back, gain_term = norm_back(o.mid[half, rows], scatter.total(half, rows), gain_mid)
            o.gain_sum[2 * l + 1 : 2 * l + 2, :] += gain_term
            value = o.o_grad[half, rows] + back
            o.o_grad[half, rows] = value
            o.ml[p.s, half, rows] = value.astype(BF)

        for half in range(2):
            scatter.arrive(half)
            row_loop(d.half, functools.partial(middle, half))
            gather.start(o.ml, half)
            if half == 0:
                run(4 + 14 * (top - l))
        scatter.end()
        load(STREAM, l).start()
        load(XMID, l).wait()
        run(5 + 14 * (top - l))
        if l + 2 <= top:
            reduce.sent(l + 2, UP)
        weight_grad(reduce.grad(l, UP), o.xmid, o.slope, d.n_width, d.hid)
        run(6 + 14 * (top - l))
        refill(l, XMID, SLOPE)
        load(W_OUT, l).wait()

        def att_grad(pieces):
            weight = o.wout[...].reshape(d.dh, d.width)
            put_pair(o.d_att, pieces, slice(None), nt(pair(o.ml, pieces), weight))

        att_grad(p.pieces(0))
        gather.near(o.ml)
        att_grad(p.pieces(1))
        run(7 + 14 * (top - l))

        @pl.loop(2, d.sp_n)
        def _(t):
            gather.far(o.ml, t)
            att_grad(p.pieces(t))

        gather.end(o.ml)
        refill(l, W_OUT)
        run(8 + 14 * (top - l))
        load(PROJ, l).wait()
        load(PROBS, l).wait()
        attention_backward(d, o)
        refill(l, PROJ, PROBS)
        run(9 + 14 * (top - l))
        load(W_QKV, l).wait()

        def in_grad(pieces):
            blocks = []
            for slot, half in pieces:
                block = o.sorted_dqkv[o.meta[1, slot], half]
                o.d_qkv[slot, half] = block
                blocks.append(block)
            block = jnp.concatenate(blocks, axis=0)
            for n in range(d.n_width):
                cols = slice(n * d.chunk, (n + 1) * d.chunk)
                put_pair(o.part, pieces, cols, nt(block, rows_of(o.wqkv, n, d.n_width)))

        @pl.loop(2, d.sp_n)
        def _(t):
            in_grad(p.pieces(t))
            scatter.put(t)

            @pl.when(t > 2)
            def _():
                scatter.cross(t - 1)

        in_grad(p.pieces(1))
        scatter.put(1)
        scatter.cross(d.sp_n - 1)
        in_grad(p.pieces(0))
        run(10 + 14 * (top - l))
        refill(l, W_QKV)
        load(ATT, l).wait()
        if l < top:
            reduce.sent(l + 1, OUT)
        value = tn(o.att[...].reshape(tokens, d.dh), o.ml[...].reshape(tokens, d.width)).astype(BF)
        o.g_out[...] = value.reshape((d.z_n, d.y_n, d.rows, d.width))
        run(11 + 14 * (top - l))
        refill(l, ATT)
        load(XIN, l).wait()
        if l < top:
            reduce.sent(l + 1, QKV)
        weight_grad(o.g_qkv, o.xin, o.d_qkv, d.n_width, 3 * d.dh)
        run(12 + 14 * (top - l))
        refill(l, XIN)
        load(STREAM, l).wait()

        def lower(half, rows):
            back, gain_term = norm_back(o.mid[half, rows], scatter.total(half, rows), gain_in)
            o.gain_sum[2 * l : 2 * l + 1, :] += gain_term
            value = o.o_grad[half, rows] + back
            o.o_grad[half, rows] = value
            if l > 0:
                o.gl[p.s, half, rows] = value.astype(BF)

        for half in range(2):
            scatter.arrive(half)
            row_loop(d.half, functools.partial(lower, half))
            if l > 0:
                gather.start(o.gl, half)
            if half == 0:
                run(13 + 14 * (top - l))
        scatter.end()
        if l == 0:
            small.start(0)
        refill(l, MID)

    keep_part = pltpu.make_async_copy(o.i_part, o.part, o.late_sem.at[1])
    keep_part.start()
    load(MID, top).start()
    run(28)
    small.finish(0, o.mid_a)
    small.start(1)
    keep_part.wait()
    for t in range(d.sp_n - 1, 1, -1):
        scatter.near_copy(p.slot(t // 2 * 2) // 2, t % 2).start()
    scatter.put(1)
    run(29)
    for t in range(d.sp_n - 1, 1, -1):
        scatter.cross(t)
    run(30)
    small.finish(1, o.mid_b)
    small.start(2)
    run(31)
    load(MID, top).wait()

    def last(half, rows):
        o.o_output[half, rows] = (o.mid[half, rows] + scatter.total(half, rows)).astype(BF)

    for half in range(2):
        scatter.arrive(half)
        row_loop(d.half, functools.partial(last, half))
    scatter.end()
    run(32)
    small.finish(2, o.o_gains)
    for l in reversed(range(d.layers)):
        for w in (DOWN, UP, OUT, QKV):
            reduce.last(l, w)
    for w in (DOWN, UP, OUT, QKV):
        reduce.sent(0, w)
    if top > 0:
        reduce.sent(1, UP)


def finish_kernel(d, names, *refs):
    o = Refs()
    for name, ref in zip(names, refs):
        setattr(o, name, ref)
    arrays = (
        (o.o_qkv, o.a_qkv, o.b_qkv, o.r_qkv),
        (o.o_out, o.a_out, o.b_out, o.r_out),
        (o.o_up, o.a_up, o.b_up, o.r_up),
        (o.o_down, o.a_down, o.b_down, o.r_down),
        (o.o_grad, o.a_grad, o.a_grad, o.r_grad),
        (o.o_output, o.a_output, o.a_output, o.r_output),
    )
    copies = []
    reads = [pltpu.make_async_copy(a[0], a[1], o.in_sem.at[n]) for n, a in enumerate(arrays)]
    for copy in reads:
        copy.start()
    for n, (_, low, full, result) in enumerate(arrays):
        reads[n].wait()
        if full is not low:
            for l in range(d.layers):
                full[l] = low[l].astype(F32)
        copies.append(pltpu.make_async_copy(full, result, o.out_sem.at[n]))
        copies[-1].start()
    own = o.r_gains.shape[1]
    flat = lax.axis_index(AXES[0]) * d.sp_n + lax.axis_index(AXES[1])
    mine = jnp.zeros(o.r_gains.shape, F32)
    for k in range(d.width // own):
        mine = jnp.where(flat == k, o.o_gains[: o.r_gains.shape[0], k * own : (k + 1) * own], mine)
    o.r_gains[...] = mine
    for copy in copies:
        copy.wait()


ANY = pl.BlockSpec(memory_space=pl.ANY)
VM = pl.BlockSpec(memory_space=pltpu.VMEM)
SM = pl.BlockSpec(memory_space=pltpu.SMEM)


def call(kernel, d, inputs, outputs, scratch, identity):
    names = [i[0] for i in inputs] + [i[0] for i in outputs] + [i[0] for i in scratch]
    results = pl.pallas_call(
        functools.partial(kernel, d, names),
        out_shape=[jax.ShapeDtypeStruct(i[2], i[3]) for i in outputs],
        in_specs=[i[1] for i in inputs],
        out_specs=[i[1] for i in outputs],
        scratch_shapes=[i[1] for i in scratch],
        compiler_params=pltpu.CompilerParams(
            collective_id=identity, has_side_effects=identity is not None, vmem_limit_bytes=62 * 1024 * 1024
        ),
        name=kernel.__name__,
    )(*[i[2] for i in inputs])
    return dict(zip([i[0] for i in outputs], results))


def shards(dp_n, sp_n, tokens, cotangent, w_qkv, w_out, w_up, w_down, gains, piece_order, doc_lengths):
    _, tok, width = tokens.shape
    layers, _, rows, _ = w_qkv.shape
    ff = w_up.shape[-1]
    d = Dims(dp_n, sp_n, layers, tok, width, ff, doc_lengths.shape[1])
    r, s = lax.axis_index(AXES[0]), lax.axis_index(AXES[1])

    own = gains.shape[-1]
    padded = jnp.zeros((8, width), F32)
    padded = lax.dynamic_update_slice(
        padded, gains.reshape(2 * layers, own).astype(F32), (0, (r * sp_n + s) * own)
    )
    lay_scratch = []
    if d.whole_lanes:
        lay_scratch = [
            ("in_qkv", pltpu.VMEM((layers, sp_n, rows, 3 * d.dh), BF)),
            ("in_up", pltpu.VMEM((layers, sp_n, rows, d.hid), BF)),
        ]
        given = [("raw_qkv", VM, w_qkv), ("raw_up", VM, w_up)]
    else:
        in_qkv = w_qkv.reshape(layers, 3, rows, sp_n, d.dh).transpose(0, 3, 2, 1, 4)
        in_up = w_up.reshape(layers, rows, dp_n, sp_n, d.hid_own).transpose(0, 3, 1, 2, 4)
        given = [
            ("in_qkv", ANY, in_qkv.reshape(layers, sp_n, rows, 3 * d.dh)),
            ("in_up", ANY, in_up.reshape(layers, sp_n, rows, d.hid)),
        ]

    saved, weights = saved_shapes(d), weight_shapes(d)
    dma = pltpu.SemaphoreType.DMA
    fwd = call(
        fwd_kernel,
        d,
        [
            ("in_order", SM, piece_order),
            ("in_lengths", SM, doc_lengths),
            ("in_tokens", VM, tokens.reshape(2, d.half, width)),
            ("in_cotangent", VM, cotangent.reshape(2, d.half, width)),
            ("in_gains", VM, padded),
            ("in_out", ANY, w_out),
            ("in_down", ANY, w_down),
        ]
        + given,
        [("o_gains", VM, (8, width), F32)]
        + [("o_" + n, ANY, (layers,) + weights[n][0], BF) for n in WEIGHTS]
        + [("o_" + n, ANY, (layers,) + saved[n][0], saved[n][1]) for n in SAVED]
        + [("o_gl", ANY, (sp_n, 2, d.half, width), BF), ("o_part", ANY, (sp_n, 2, d.half, width), BF)],
        [(n, pltpu.VMEM((layers,) + weights[n][0], BF)) for n in WEIGHTS]
        + [(n, pltpu.VMEM((1 if n in ONCE else layers,) + saved[n][0], saved[n][1])) for n in SAVED]
        + [
            ("sorted_att", pltpu.VMEM(saved[ATT][0], BF)),
            ("meta", pltpu.SMEM((3, max(sp_n, d.docs)), jnp.int32)),
        ]
        + [
            ("gl", pltpu.VMEM((sp_n, 2, d.half, width), BF)),
            ("late_send", dma((2, sp_n, 2))),
            ("late_recv", dma((sp_n, 2))),
            ("late_sem", dma((2,))),
        ]
        + lay_scratch
        + small_scratch(d)
        + comm_scratch(d)
        + [
            ("s_send", dma((layers, 4, sp_n))),
            ("s_recv", dma((layers, 4, sp_n))),
            ("own_sem", dma((layers, 4))),
            ("b_send", dma((layers, len(d.pieces), d.z_n, d.y_n, 1 + d.y_n))),
            ("b_recv", dma((layers, len(d.pieces), d.z_n, d.y_n))),
            ("w_sem", dma((layers, 4))),
            ("save_sem", dma((layers, len(SAVED)))),
        ],
        0,
    )
    kinds = ("qkv", "out", "up", "down")
    blocks = [d.block_shape(w) for w in range(4)]
    results = [(layers,) + b for b in blocks]
    if d.whole_lanes:
        results[QKV], results[UP] = w_qkv.shape, w_up.shape
    bwd = call(
        bwd_kernel,
        d,
        [("in_order", SM, piece_order), ("in_lengths", SM, doc_lengths), ("i_gl", ANY, fwd["o_gl"]), ("i_part", ANY, fwd["o_part"]), ("in_gains", VM, fwd["o_gains"])]
        + [("i_" + n, ANY, fwd["o_" + n]) for n in WEIGHTS + SAVED],
        [("o_output", VM, (2, d.half, width), BF), ("o_grad", VM, (2, d.half, width), F32), ("o_gains", VM, (8, width), F32)]
        + [("o_" + k, VM, shape, BF) for k, shape in zip(kinds, results)],
        [(n, pltpu.VMEM(weights[n][0], BF)) for n in WEIGHTS]
        + [(n, pltpu.VMEM(saved[n][0], saved[n][1])) for n in SAVED if n != STREAM]
        + [
            ("gl", pltpu.VMEM((sp_n, 2, d.half, width), BF)),
            ("ml", pltpu.VMEM((sp_n, 2, d.half, width), BF)),
            ("d_att", pltpu.VMEM((sp_n, 2, d.half, d.dh), BF)),
            ("sorted_dqkv", pltpu.VMEM((sp_n, 2, d.half, 3 * d.dh), BF)),
            ("d_qkv", pltpu.VMEM((sp_n, 2, d.half, 3 * d.dh), BF)),
            ("d_keys", pltpu.VMEM((sp_n, tok, d.dh), F32)),
            ("d_values", pltpu.VMEM((sp_n, tok, d.dh), F32)),
            ("gain_sum", pltpu.VMEM((8, width), F32)),
            ("meta", pltpu.SMEM((3, max(sp_n, d.docs)), jnp.int32)),
        ]
        + [("g_" + k, pltpu.VMEM((d.z_n, d.y_n) + b, BF)) for k, b in zip(kinds, blocks)]
        + [("g_up_odd", pltpu.VMEM((d.z_n, d.y_n) + blocks[UP], BF))]
        + [i for l in range(layers) for t in range(len(d.terms)) for i in term_scratch(d, l, t)]
        + [("x_" + k, pltpu.VMEM((layers,) + b, BF)) for k, b in zip(kinds[:3], blocks)]
        + small_scratch(d)
        + comm_scratch(d)
        + [
            ("late_sem", dma((2,))),
            ("load_sem", dma((len(WEIGHTS + SAVED),))),
            ("ry_send", dma((layers, len(d.terms), d.y_n))),
            ("ry_recv", dma((layers, len(d.terms), d.y_n))),
            ("rz_send", dma((layers, len(d.terms), d.y_n, 3))),
            ("rz_recv", dma((layers, len(d.terms), d.y_n, 5))),
            ("rs_send", dma((layers, 4, sp_n))),
            ("rs_recv", dma((layers, 4, sp_n))),
        ],
        1,
    )
    done = call(
        finish_kernel,
        d,
        [("o_" + k, ANY, bwd["o_" + k]) for k in kinds + ("grad", "output")] + [("o_gains", VM, bwd["o_gains"])],
        [("r_" + k, ANY, bwd["o_" + k].shape, F32) for k in kinds]
        + [
            ("r_grad", ANY, bwd["o_grad"].shape, F32),
            ("r_output", ANY, bwd["o_output"].shape, BF),
            ("r_gains", VM, (2 * layers, own), F32),
        ],
        [("a_" + k, pltpu.VMEM(bwd["o_" + k].shape, BF)) for k in kinds]
        + [("b_" + k, pltpu.VMEM(bwd["o_" + k].shape, F32)) for k in kinds]
        + [("a_grad", pltpu.VMEM(bwd["o_grad"].shape, F32)), ("a_output", pltpu.VMEM(bwd["o_output"].shape, BF))]
        + [("in_sem", dma((6,))), ("out_sem", dma((6,)))],
        None,
    )
    grad_qkv, grad_out, grad_up, grad_down = (done["r_" + k] for k in kinds)
    if not d.whole_lanes:
        grad_qkv = grad_qkv.reshape(layers, sp_n, rows, 3, d.dh).transpose(0, 3, 2, 1, 4).reshape(w_qkv.shape)
        grad_up = grad_up.reshape(layers, sp_n, rows, dp_n, d.hid_own).transpose(0, 2, 3, 1, 4).reshape(w_up.shape)
    return (
        done["r_output"].reshape(tokens.shape),
        done["r_grad"].reshape(tokens.shape),
        grad_qkv,
        grad_out,
        grad_up,
        grad_down,
        done["r_gains"].reshape(gains.shape),
    )


def solution(mesh):
    dp, sp = AXES
    by_token, by_axis = P(dp, sp, None), P(dp, None)
    by_row, by_third = P(None, AXES, None), P(None, None, AXES)
    return jax.shard_map(
        functools.partial(shards, mesh.shape[dp], mesh.shape[sp]),
        mesh=mesh,
        in_specs=(by_token, by_token, by_third, by_row, by_row, by_row, by_third, by_axis, by_axis),
        out_specs=(by_token, by_token, by_third, by_row, by_row, by_row, by_third),
        check_vma=False,
    )
```

```python
import functools

import jax
import jax.numpy as jnp
from jax import lax
from jax.experimental import pallas as pl
from jax.experimental.pallas import tpu as pltpu
from jax.sharding import PartitionSpec as P

HEADS = 8
HD = 128
EPS = 1e-05
MASKED = -1e30
MESH = pl.DeviceIdType.MESH
BF = jnp.bfloat16
F32 = jnp.float32
AXES = ("dp", "sp")
QKV, OUT, UP, DOWN = range(4)
Q0, Q1, O0, U0, U1, D0, D1 = range(7)
SPREAD, OWN, START_Z, START_Y, RELAY_1, INNER, OUTER, RELAY_3, LATE_START, LATE_ON, LATE_END = range(11)


def nn(a, b):
    return lax.dot_general(a, b, (((1,), (0,)), ((), ())), preferred_element_type=F32)


def nt(a, b):
    return lax.dot_general(a, b, (((1,), (1,)), ((), ())), preferred_element_type=F32)


def tn(a, b):
    return lax.dot_general(a, b, (((0,), (0,)), ((), ())), preferred_element_type=F32)


FORWARD_PLAN = {
    0: ((OWN, 0, 3), (START_Y, 0, 5), (START_Z, 0, 4), (OWN, 0, 0), (OWN, 0, 1), (START_Y, 0, 0), (START_Z, 0, 0), (SPREAD, 1, 2),),
    1: ((INNER, 0, 0), (START_Z, 0, 1), (LATE_START, 0, 1), (RELAY_1, 0, 0),),
    2: ((OUTER, 0, 0), (OWN, 0, 2), (RELAY_3, 0, 0), (START_Y, 0, 2), (START_Z, 0, 3), (INNER, 0, 1),),
    3: ((START_Y, 0, 3), (RELAY_1, 0, 1), (SPREAD, 1, 3), (LATE_START, 0, 0), (START_Z, 0, 2), (OUTER, 0, 1),),
    4: ((START_Y, 0, 1), (OWN, 1, 3), (INNER, 0, 4), (RELAY_1, 0, 4), (SPREAD, 1, 0), (RELAY_3, 0, 1), (INNER, 0, 3),),
    5: ((RELAY_1, 0, 2), (START_Z, 0, 5), (SPREAD, 1, 1), (RELAY_3, 0, 4), (RELAY_1, 0, 3),),
    6: ((OWN, 1, 0), (INNER, 0, 2), (OWN, 1, 2), (OUTER, 0, 3),),
    7: ((RELAY_1, 0, 5), (RELAY_3, 0, 2), (INNER, 0, 5), (LATE_ON, 0, 0), (RELAY_3, 0, 3), (OWN, 1, 1), (OUTER, 0, 2), (START_Z, 1, 0),),
    8: ((START_Z, 1, 4), (START_Y, 1, 0), (LATE_ON, 0, 1),),
    9: ((OUTER, 0, 5), (START_Z, 1, 3), (OUTER, 0, 4), (START_Y, 1, 1),),
    10: ((START_Y, 0, 4), (START_Z, 1, 2), (START_Z, 1, 1), (START_Y, 1, 2), (LATE_END, 0, 0), (RELAY_1, 1, 0), (RELAY_3, 0, 5),),
    11: ((START_Y, 1, 5), (START_Y, 1, 4), (INNER, 1, 0), (OUTER, 1, 0),),
    12: ((RELAY_1, 1, 1), (START_Z, 1, 5),),
    13: ((RELAY_3, 1, 0), (RELAY_1, 1, 4), (INNER, 1, 3), (RELAY_1, 1, 5), (INNER, 1, 1),),
    14: ((INNER, 1, 2), (START_Y, 1, 3), (RELAY_3, 1, 1),),
    15: ((INNER, 1, 5), (INNER, 1, 4), (OUTER, 1, 1), (RELAY_1, 1, 2), (RELAY_1, 1, 3),),
    16: ((RELAY_3, 1, 4), (OUTER, 1, 3), (OUTER, 1, 2),),
    17: ((OUTER, 1, 5),),
    18: ((OUTER, 1, 4), (RELAY_3, 1, 2), (RELAY_3, 1, 5), (RELAY_3, 1, 3),),
}
BACKWARD_PLAN = {
    3: ((1, D0),),
    4: ((1, D1),),
    6: ((1, U1),),
    7: ((1, U0), (1, D0),),
    10: ((1, D1),),
    11: ((1, D0),),
    12: ((1, Q0), (1, D1), (1, U1),),
    13: ((1, Q1), (1, O0),),
    14: ((1, Q0), (1, U1),),
    15: ((1, U0), (1, D0),),
    16: ((1, D1),),
    17: ((0, D1), (0, D0), (1, Q1), (1, U0),),
    18: ((1, O0), (1, Q1),),
    19: ((1, Q0),),
    20: ((1, O0),),
    21: ((0, D1), (1, Q0),),
    22: ((1, Q1), (1, O0),),
    23: ((0, D1), (0, U1), (0, D0),),
    24: ((0, U0),),
    25: ((0, D1), (1, U0),),
    26: ((0, D0), (0, Q1), (0, U1), (0, Q0),),
    28: ((0, D0),),
    29: ((0, Q1), (0, U0), (0, Q1), (0, U1), (0, O0),),
    30: ((0, U0), (0, O0), (0, Q0),),
    31: ((0, O0), (0, U0), (0, U1), (0, Q1),),
    32: ((0, Q0), (1, U1), (0, O0), (0, Q0),),
}


class Dims:
    def __init__(self, dp_n, sp_n, layers, tok, width, ff, docs):
        self.dp_n, self.sp_n, self.layers, self.tok, self.width = dp_n, sp_n, layers, tok, width
        self.z_n = 4 if dp_n % 4 == 0 else 1
        self.y_n = dp_n // self.z_n
        self.x_n = sp_n // 2
        self.rows = width // (dp_n * sp_n)
        self.heads = HEADS // sp_n
        self.dh = width // sp_n
        self.hid = ff // sp_n
        self.hid_own = ff // (dp_n * sp_n)
        self.docs = docs
        self.whole_lanes = self.hid_own % 128 == 0
        self.chunk = min(256, tok)
        self.half = tok // 2
        self.n_width = width // self.chunk
        self.n_hid = self.hid // self.chunk
        self.back = self.x_n
        half, part = sp_n // 2, self.hid_own // 2
        self.pieces = (
            (QKV, 0, sp_n, False),
            (OUT, 0, self.rows, False),
            (UP, 0, half, False),
            (UP, half, sp_n, False),
            (DOWN, 0, part, False),
            (DOWN, part, self.hid_own, True),
        )
        self.terms = (
            (QKV, 0, half),
            (QKV, half, sp_n),
            (OUT, 0, self.rows),
            (UP, 0, half),
            (UP, half, sp_n),
            (DOWN, 0, part),
            (DOWN, part, self.hid_own),
        )
        self.z_first = [(Q1,)] + [(D1,)] * (layers - 1)
        self.pairs = [(i, b) for i in range(sp_n) for b in range(max(0, i - self.back), i + 1)]

    def block_shape(self, which):
        return {
            QKV: (self.sp_n, self.rows, 3 * self.dh),
            OUT: (self.rows, self.width),
            UP: (self.sp_n, self.rows, self.hid),
            DOWN: (self.hid_own, self.width),
        }[which]


class Place:
    def __init__(self, d):
        self.d = d
        self.r = lax.axis_index(AXES[0])
        self.s = lax.axis_index(AXES[1])
        self.z, self.y = self.r // d.y_n, self.r % d.y_n
        self.x, self.c = self.s // 2, self.s % 2
        self.partner = self.x * 2 + (self.c + 1) % 2

    def slot(self, step):
        return ((self.x + step // 2) % self.d.x_n) * 2 + (self.c + step % 2) % 2

    def pieces(self, step):
        if isinstance(step, int) and step < 2:
            return (self.slot(step), 0), (self.slot(step), 1)
        first = step // 2 * 2
        return (self.slot(first), step % 2), (self.slot(first + 1), step % 2)

    def zpeer(self, dz):
        return (self.z + dz) % self.d.z_n

    def ypeer(self, dy):
        return (self.y + dy) % self.d.y_n

    def line(self):
        high = self.z // 2
        inside = ((self.z + 1) // 2) % 2
        first = inside * 3 * high + (1 - inside) * (1 + high)
        return inside == 1, (self.z, first, 2 - high, 3 - 3 * high)

    def dev(self, z, y):
        return (z * self.d.y_n + y, self.s)

    def moved(self):
        d = self.d
        flat = self.r * d.sp_n + self.s
        goal = (flat % d.dp_n, flat // d.dp_n)
        mine = self.s * d.dp_n + self.r
        source = (mine // d.sp_n, mine % d.sp_n)
        stays = flat == mine
        return goal, source, stays

    def barrier(self):
        d = self.d
        sem = pltpu.get_barrier_semaphore()
        peers = [(self.r, self.slot(t)) for t in range(1, d.sp_n)]
        peers += [self.dev(self.zpeer(k), self.y) for k in range(1, d.z_n)]
        peers += [self.dev(self.z, self.ypeer(k)) for k in range(1, d.y_n)]
        for peer in peers:
            pl.semaphore_signal(sem, inc=1, device_id=peer, device_id_type=MESH)
        goal, source, stays = self.moved()

        @pl.when(jnp.logical_not(stays))
        def _():
            pl.semaphore_signal(sem, inc=1, device_id=goal, device_id_type=MESH)
            pl.semaphore_signal(sem, inc=1, device_id=source, device_id_type=MESH)
            pl.semaphore_wait(sem, len(peers) + 2)

        @pl.when(stays)
        def _():
            pl.semaphore_wait(sem, len(peers))


def rcopy(src, dst, send, recv, device):
    return pltpu.make_async_remote_copy(
        src_ref=src, dst_ref=dst, send_sem=send, recv_sem=recv, device_id=device, device_id_type=MESH
    )


def pair(ref, pieces, *cols):
    return jnp.concatenate([ref[(slot, half) + (slice(None),) + cols] for slot, half in pieces], axis=0)


def put_pair(ref, pieces, cols, value):
    rows = value.shape[0] // 2
    for k, (slot, half) in enumerate(pieces):
        ref[slot, half, :, cols] = value[k * rows : (k + 1) * rows].astype(ref.dtype)


class Gather:
    def __init__(self, p, send, recv):
        self.p, self.send, self.recv = p, send, recv

    def copy(self, buf, slot, half, way, goal):
        block = buf.at[slot, half]
        return rcopy(block, block, self.send.at[way, goal, half], self.recv.at[slot, half], (self.p.r, goal))

    def start(self, buf, half):
        p = self.p
        for dx in range(1, p.d.x_n):
            self.copy(buf, p.s, half, 0, p.slot(2 * dx)).start()
        self.copy(buf, p.s, half, 0, p.partner).start()

    def onward(self, buf, slot, half):
        block = buf.at[slot, half]
        p = self.p
        return rcopy(block, block, self.send.at[1, slot, half], self.recv.at[slot, half], (p.r, p.partner))

    def arrived(self, buf, slot, half):
        self.copy(buf, slot, half, 0, self.p.partner).wait_recv()

    def near(self, buf):
        for half in range(2):
            self.arrived(buf, self.p.partner, half)

    def through(self, buf, step):
        first, _ = self.p.pieces(step)
        self.arrived(buf, *first)
        self.onward(buf, *first).start()

    def rest(self, buf):
        self.near(buf)
        for step in range(2, self.p.d.sp_n):
            self.arrived(buf, *self.p.pieces(step)[1])

    def far(self, buf, step):
        first, second = self.p.pieces(step)
        self.arrived(buf, *first)
        self.onward(buf, *first).start()
        self.arrived(buf, *second)

    def end(self, buf):
        p = self.p
        for half in range(2):
            for dx in range(1, p.d.x_n):
                self.copy(buf, p.s, half, 0, p.slot(2 * dx)).wait_send()
                self.onward(buf, p.slot(2 * dx), half).wait_send()
            self.copy(buf, p.s, half, 0, p.partner).wait_send()


class Scatter:
    def __init__(self, p, part, near, far, near_send, near_recv, far_send, far_recv):
        self.p, self.part, self.near, self.far = p, part, near, far
        self.near_send, self.near_recv, self.far_send, self.far_recv = near_send, near_recv, far_send, far_recv

    def near_copy(self, x, half):
        p = self.p
        return rcopy(
            self.part.at[x * 2 + (p.c + 1) % 2, half],
            self.near.at[x, half],
            self.near_send.at[x, half],
            self.near_recv.at[x, half],
            (p.r, p.partner),
        )

    def far_copy(self, x, half, source):
        p = self.p
        goal = x * 2 + p.c
        return rcopy(
            self.part.at[goal, half],
            self.far.at[source, half],
            self.far_send.at[x, half],
            self.far_recv.at[source, half],
            (p.r, goal),
        )

    def put(self, step):
        if isinstance(step, int):
            if step == 1:
                for half in range(2):
                    self.near_copy(self.p.x, half).start()
        else:
            self.near_copy(self.p.slot(step // 2 * 2) // 2, step % 2).start()

    def cross(self, step):
        p = self.p
        slot, half = p.slot(step // 2 * 2), step % 2
        x = slot // 2
        self.near_copy(x, half).wait_recv()
        size = min(64, p.d.half)

        @pl.loop(0, p.d.half // size, unroll=True)
        def _(i):
            rows = pl.ds(pl.multiple_of(i * size, size), size)
            both = self.part[slot, half, rows].astype(F32) + self.near[x, half, rows].astype(F32)
            self.part[slot, half, rows] = both.astype(BF)

        self.far_copy(x, half, p.x).start()

    def arrive(self, half):
        p = self.p
        self.near_copy(p.x, half).wait_recv()
        for dx in range(1, p.d.x_n):
            x = (p.x + dx) % p.d.x_n
            self.far_copy(x, half, x).wait_recv()

    def total(self, half, rows):
        p = self.p
        value = self.part[p.s, half, rows].astype(F32) + self.near[p.x, half, rows].astype(F32)
        for dx in range(1, p.d.x_n):
            value = value + self.far[(p.x + dx) % p.d.x_n, half, rows].astype(F32)
        return value

    def end(self):
        p = self.p
        for half in range(2):
            for dx in range(p.d.x_n):
                x = (p.x + dx) % p.d.x_n
                self.near_copy(x, half).wait_send()
                if dx:
                    self.far_copy(x, half, p.x).wait_send()


class SmallSum:
    def __init__(self, p, first, sp_in, mid_a, z_in, mid_b, y_in, sp_sem, z_sem, y_sem):
        self.p = p
        self.bufs = ((first, sp_in, sp_sem), (mid_a, z_in, z_sem), (mid_b, y_in, y_sem))

    def plan(self, stage):
        p = self.p
        if stage == 0:
            return p.s, [(p.slot(t), (p.r, p.slot(t))) for t in range(1, p.d.sp_n)]
        if stage == 1:
            return p.z, [(p.zpeer(k), p.dev(p.zpeer(k), p.y)) for k in range(1, p.d.z_n)]
        return p.y, [(p.ypeer(k), p.dev(p.z, p.ypeer(k))) for k in range(1, p.d.y_n)]

    def start(self, stage):
        src, dst, sem = self.bufs[stage]
        own, peers = self.plan(stage)
        for index, device in peers:
            rcopy(src, dst.at[own], sem.at[0, index], sem.at[1, own], device).start()

    def finish(self, stage, result):
        src, dst, sem = self.bufs[stage]
        own, peers = self.plan(stage)
        value = src[...]
        for index, device in peers:
            rcopy(src, dst.at[index], sem.at[0, index], sem.at[1, index], device).wait_recv()
            value = value + dst[index]
        result[...] = value
        for index, device in peers:
            rcopy(src, dst.at[own], sem.at[0, index], sem.at[1, own], device).wait_send()


def small_scratch(d):
    return [
        ("sp_in", pltpu.VMEM((d.sp_n, 8, d.width), F32)),
        ("mid_a", pltpu.VMEM((8, d.width), F32)),
        ("z_in", pltpu.VMEM((d.z_n, 8, d.width), F32)),
        ("mid_b", pltpu.VMEM((8, d.width), F32)),
        ("y_in", pltpu.VMEM((d.y_n, 8, d.width), F32)),
        ("sp_sem", pltpu.SemaphoreType.DMA((2, d.sp_n))),
        ("z_sem", pltpu.SemaphoreType.DMA((2, d.z_n))),
        ("y_sem", pltpu.SemaphoreType.DMA((2, d.y_n))),
    ]


def comm_scratch(d):
    return [
        ("part", pltpu.VMEM((d.sp_n, 2, d.half, d.width), BF)),
        ("near", pltpu.VMEM((d.x_n, 2, d.half, d.width), BF)),
        ("far", pltpu.VMEM((d.x_n, 2, d.half, d.width), BF)),
        ("ag_send", pltpu.SemaphoreType.DMA((2, d.sp_n, 2))),
        ("ag_recv", pltpu.SemaphoreType.DMA((d.sp_n, 2))),
        ("near_send", pltpu.SemaphoreType.DMA((d.x_n, 2))),
        ("near_recv", pltpu.SemaphoreType.DMA((d.x_n, 2))),
        ("far_send", pltpu.SemaphoreType.DMA((d.x_n, 2))),
        ("far_recv", pltpu.SemaphoreType.DMA((d.x_n, 2))),
    ]


def term_scratch(d, l, term):
    w, first, last = d.terms[term]
    block = (last - first,) + d.block_shape(w)[1:]
    z_first = term in d.z_first[l]
    y_shape = (max(1, d.y_n - 1), 1 if z_first else d.z_n) + block
    z_shape = (5, d.y_n if z_first else 1) + block
    return [
        ("y_in_%d_%d" % (l, term), pltpu.VMEM(y_shape, BF)),
        ("z_in_%d_%d" % (l, term), pltpu.VMEM(z_shape, BF)),
    ]


SAVED = XIN, PROJ, ATT, PROBS, XMID, HID, SLOPE, STREAM, MID = (
    "xin",
    "qkv",
    "att",
    "probs",
    "xmid",
    "hid",
    "slope",
    "stream",
    "mid",
)
ONCE = (PROJ, ATT, PROBS, HID, SLOPE)
WEIGHTS = W_QKV, W_OUT, W_UP, W_DOWN = ("wqkv", "wout", "wup", "wdown")


def saved_shapes(d):
    full = (d.sp_n, 2, d.half)
    return {
        XIN: (full + (d.width,), BF),
        PROJ: (full + (3 * d.dh,), BF),
        ATT: (full + (d.dh,), BF),
        PROBS: ((d.heads, len(d.pairs), d.tok, d.tok), BF),
        XMID: (full + (d.width,), BF),
        HID: (full + (d.hid,), BF),
        SLOPE: (full + (d.hid,), BF),
        STREAM: ((2, d.half, d.width), F32),
        MID: ((2, d.half, d.width), F32),
    }


def weight_shapes(d):
    return {name: ((d.z_n, d.y_n) + d.block_shape(i), BF) for i, name in enumerate(WEIGHTS)}


class Fetch:
    def __init__(self, p, o):
        self.p, self.o = p, o
        self.full = (o.wqkv, o.wout, o.wup, o.wdown)

    def spread(self, l, w):
        p, o = self.p, self.o
        own = self.full[w].at[l, p.z, p.y]
        if w in (QKV, UP):
            src = o.in_qkv if w == QKV else o.in_up
            for t in range(1, p.d.sp_n):
                j = p.slot(t)
                rcopy(src.at[l, j], own.at[p.s], o.s_send.at[l, w, j], o.s_recv.at[l, w, p.s], (p.r, j)).start()
            pltpu.make_async_copy(src.at[l, p.s], own.at[p.s], o.own_sem.at[l, w]).start()
        elif w == DOWN:
            pltpu.make_async_copy(o.in_down.at[l], own, o.own_sem.at[l, w]).start()
        else:
            goal, _, stays = p.moved()

            @pl.when(stays)
            def _():
                pltpu.make_async_copy(o.in_out.at[l], own, o.own_sem.at[l, w]).start()

            @pl.when(jnp.logical_not(stays))
            def _():
                there = self.full[w].at[l, goal[0] // p.d.y_n, goal[0] % p.d.y_n]
                rcopy(o.in_out.at[l], there, o.s_send.at[l, w, 0], o.s_recv.at[l, w, 0], goal).start()

    def own(self, l, w):
        p, o = self.p, self.o
        own = self.full[w].at[l, p.z, p.y]
        if w in (QKV, UP):
            src = o.in_qkv if w == QKV else o.in_up
            pltpu.make_async_copy(src.at[l, p.s], own.at[p.s], o.own_sem.at[l, w]).wait()
            for t in range(1, p.d.sp_n):
                j = p.slot(t)
                rcopy(src.at[l, j], own.at[j], o.s_send.at[l, w, j], o.s_recv.at[l, w, j], (p.r, j)).wait_recv()
        elif w == DOWN:
            pltpu.make_async_copy(o.in_down.at[l], own, o.own_sem.at[l, w]).wait()
        else:
            goal, _, stays = p.moved()

            @pl.when(stays)
            def _():
                pltpu.make_async_copy(o.in_out.at[l], own, o.own_sem.at[l, w]).wait()

            @pl.when(jnp.logical_not(stays))
            def _():
                rcopy(o.in_out.at[l], own, o.s_send.at[l, w, 0], o.s_recv.at[l, w, 0], goal).wait_recv()

    def block(self, l, piece, z, y):
        w, first, last, _ = self.p.d.pieces[piece]
        return self.full[w].at[l, z, y, first:last]

    def columns(self, piece):
        p = self.p
        if self.p.d.pieces[piece][3]:
            return [p.y] + [p.ypeer(m) for m in range(1, p.d.y_n)]
        return [p.y]

    def copy(self, l, piece, z, y, way, device):
        o = self.o
        block = self.block(l, piece, z, y)
        return rcopy(block, block, o.b_send.at[l, piece, z, y, way], o.b_recv.at[l, piece, z, y], device)

    def arrived(self, l, piece, z, y):
        self.copy(l, piece, z, y, 0, (self.p.r, self.p.s)).wait_recv()

    def along_z(self, l, piece, role, y, act):
        p = self.p
        if p.d.z_n == 1 or role == 3:
            return
        inside, at = p.line()
        z = at[role]

        @pl.when(inside)
        def _():
            for way, goal in enumerate(((at[1], at[2]), (at[2], at[3]), (at[1],))[role]):
                act(self.copy(l, piece, z, y, way, p.dev(goal, p.y)))

        if role == 0:

            @pl.when(jnp.logical_not(inside))
            def _():
                act(self.copy(l, piece, z, y, 0, p.dev(at[1], p.y)))

    def along_y(self, l, piece, role, act):
        p = self.p
        z = p.line()[1][role]
        for m in range(1, p.d.y_n):
            act(self.copy(l, piece, z, p.y, 1 + m, p.dev(p.z, p.ypeer(m))))

    def start_z(self, l, *pieces):
        for piece in pieces:
            self.along_z(l, piece, 0, self.p.y, lambda c: c.start())

    def start_y(self, l, *pieces):
        for piece in pieces:
            self.along_y(l, piece, 0, lambda c: c.start())

    def inner(self, l, *pieces):
        if self.p.d.z_n > 1:

            @pl.when(self.p.line()[0])
            def _():
                for piece in pieces:
                    self.relay(l, piece, 2)

    def outer(self, l, *pieces):
        if self.p.d.z_n > 1:

            @pl.when(jnp.logical_not(self.p.line()[0]))
            def _():
                for piece in pieces:
                    self.relay(l, piece, 2)

    def relay(self, l, piece, *roles):
        p = self.p
        cross_first = p.d.pieces[piece][3]
        at = p.line()[1]
        for role in roles:
            if role == 1 and cross_first:
                for y in self.columns(piece)[1:]:
                    self.arrived(l, piece, p.z, y)
                    self.along_z(l, piece, 0, y, lambda c: c.start())
            if p.d.z_n == 1:
                continue
            for y in self.columns(piece):
                self.arrived(l, piece, at[role], y)
                self.along_z(l, piece, role, y, lambda c: c.start())
            if not cross_first:
                self.along_y(l, piece, role, lambda c: c.start())

    def ready(self, l, *pieces):
        p = self.p
        for piece in pieces:
            if not p.d.pieces[piece][3]:
                for role in range(4 if p.d.z_n > 1 else 1):
                    for m in range(1, p.d.y_n):
                        self.arrived(l, piece, p.line()[1][role], p.ypeer(m))

    def save(self, l, w):
        return pltpu.make_async_copy(self.full[w].at[l], self.o.w_save[w].at[l], self.o.w_sem.at[l, w])

    def end(self):
        p, o = self.p, self.o
        for l in range(p.d.layers):
            for w in range(4):
                own = self.full[w].at[l, p.z, p.y]
                if w in (QKV, UP):
                    src = o.in_qkv if w == QKV else o.in_up
                    for t in range(1, p.d.sp_n):
                        j = p.slot(t)
                        rcopy(src.at[l, j], own.at[p.s], o.s_send.at[l, w, j], o.s_recv.at[l, w, p.s], (p.r, j)).wait_send()
                elif w == OUT:
                    goal, _, stays = p.moved()

                    @pl.when(jnp.logical_not(stays))
                    def _():
                        rcopy(o.in_out.at[l], own, o.s_send.at[l, w, 0], o.s_recv.at[l, w, 0], goal).wait_send()

                self.save(l, w).wait()
            for piece in range(len(p.d.pieces)):
                for role in range(4 if p.d.z_n > 1 else 1):
                    for y in self.columns(piece):
                        self.along_z(l, piece, role, y, lambda c: c.wait_send())
                    if role == 0 or not p.d.pieces[piece][3]:
                        self.along_y(l, piece, role, lambda c: c.wait_send())


class Refs:
    pass


def mean_of(v):
    return jnp.mean(v, axis=-1, keepdims=True)


def norm_rows(v, gain):
    center = v - mean_of(v)
    return center * lax.rsqrt(mean_of(center * center) + EPS) * gain


def row_loop(tok, body, step=32):
    step = min(step, tok)

    @pl.loop(0, tok // step, unroll=True)
    def _(i):
        body(pl.ds(pl.multiple_of(i * step, step), step))


def lay_out(d, o):
    for i in range(d.sp_n):
        where = jnp.int32(0)
        for j in range(1, d.sp_n):
            where = jnp.where(o.in_order[0, j] == i, j, where)
        o.meta[0, i] = where
        o.meta[1, i] = o.in_order[0, i]
    start = jnp.int32(0)
    for b in range(d.docs):
        o.meta[2, b] = start
        start = start + o.in_lengths[0, b]


def up_columns(d, j, k):
    first = (k * d.sp_n + j) * d.hid_own
    return slice(first, first + d.hid_own), slice(k * d.hid_own, (k + 1) * d.hid_own)


def attention_forward(d, o, l):
    tok = d.tok
    slopes = []
    for h in range(d.heads):
        head = (lax.axis_index(AXES[1]) * d.heads + (h + 1)).astype(F32)
        slopes.append(jnp.exp2(jnp.full((1, 1), -8.0 / HEADS, F32) * head))
    for i in range(d.sp_n):
        here = o.meta[0, i]
        pos = i * tok + lax.broadcasted_iota(jnp.int32, (tok, 1), 0)
        start = jnp.zeros((tok, 1), jnp.int32)
        for b in range(1, d.docs):
            start = jnp.where(pos >= o.meta[2, b], o.meta[2, b], start)
        blocks = range(max(0, i - d.back), i + 1)
        for h in range(d.heads):
            lanes = slice(h * HD, (h + 1) * HD)
            query = o.qkv[0, here, :, :, lanes].reshape(tok, HD)
            scores = []
            for b in blocks:
                keys = o.qkv[0, o.meta[0, b], :, :, d.dh + h * HD : d.dh + (h + 1) * HD].reshape(tok, HD)
                key_pos = b * tok + lax.broadcasted_iota(jnp.int32, (tok, tok), 1)
                query_pos = i * tok + lax.broadcasted_iota(jnp.int32, (tok, tok), 0)
                score = nt(query, keys) * HD ** (-0.5) + slopes[h] * (key_pos - query_pos).astype(F32)
                allowed = key_pos >= start
                if b == i:
                    allowed = allowed & (key_pos <= query_pos)
                scores.append(jnp.where(allowed, score, MASKED))
            top = scores[0].max(axis=-1, keepdims=True)
            for score in scores[1:]:
                top = jnp.maximum(top, score.max(axis=-1, keepdims=True))
            expo = [jnp.exp(score - top) for score in scores]
            total = expo[0].sum(axis=-1, keepdims=True)
            for part in expo[1:]:
                total = total + part.sum(axis=-1, keepdims=True)
            inverse = 1.0 / total
            result = None
            for b, part in zip(blocks, expo):
                low = (part * inverse).astype(BF)
                o.probs[0, h, d.pairs.index((i, b))] = low
                values = o.qkv[0, o.meta[0, b], :, :, 2 * d.dh + h * HD : 2 * d.dh + (h + 1) * HD].reshape(tok, HD)
                term = nn(low, values)
                result = term if result is None else result + term
            o.sorted_att[i, :, :, lanes] = result.astype(BF).reshape(2, d.half, HD)


def fwd_kernel(d, names, *refs):
    o = Refs()
    for name, ref in zip(names, refs):
        setattr(o, name, ref)
    o.w_save = (o.o_wqkv, o.o_wout, o.o_wup, o.o_wdown)
    p = Place(d)
    fetch = Fetch(p, o)
    gather = Gather(p, o.ag_send, o.ag_recv)
    scatter = Scatter(p, o.part, o.near, o.far, o.near_send, o.near_recv, o.far_send, o.far_recv)
    small = SmallSum(p, o.in_gains, o.sp_in, o.mid_a, o.z_in, o.mid_b, o.y_in, o.sp_sem, o.z_sem, o.y_sem)

    def save(name, l):
        ref, out = getattr(o, name), getattr(o, "o_" + name)
        held = 0 if name in ONCE else l
        return pltpu.make_async_copy(ref.at[held], out.at[l], o.save_sem.at[l, SAVED.index(name)])

    def free(l, *names):
        if l > 0:
            for name in names:
                save(name, l - 1).wait()

    late = Gather(p, o.late_send, o.late_recv)
    keep_gl = pltpu.make_async_copy(o.gl, o.o_gl, o.late_sem.at[0])

    def run(slot):
        for op, l, piece in FORWARD_PLAN.get(slot, ()):
            if op == LATE_START:
                o.gl[p.s, piece] = o.in_cotangent[piece]
                late.start(o.gl, piece)
            elif op == LATE_ON:
                for step in range(2 + piece, d.sp_n, 2):
                    late.through(o.gl, step)
            elif op == LATE_END:
                late.rest(o.gl)
                keep_gl.start()
            elif op == RELAY_1:
                fetch.relay(l, piece, 1)
            elif op == RELAY_3:
                fetch.relay(l, piece, 3)
            else:
                act = {
                    SPREAD: fetch.spread,
                    OWN: fetch.own,
                    START_Z: fetch.start_z,
                    START_Y: fetch.start_y,
                    INNER: fetch.inner,
                    OUTER: fetch.outer,
                }[op]
                act(l, piece)

    def place(l):
        if d.whole_lanes:
            for j in range(d.sp_n):
                for i in range(3):
                    o.in_qkv[l, j, :, i * d.dh : (i + 1) * d.dh] = o.raw_qkv[l, i, :, j * d.dh : (j + 1) * d.dh]
                for k in range(d.dp_n):
                    whole, kept = up_columns(d, j, k)
                    o.in_up[l, j, :, kept] = o.raw_up[l, :, whole]

    place(0)
    p.barrier()
    for w in (QKV, OUT):
        fetch.spread(0, w)
    small.start(0)
    for l in range(1, d.layers):
        place(l)
    lay_out(d, o)
    for w in (UP, DOWN):
        fetch.spread(0, w)
    run(0)
    small.finish(0, o.mid_a)
    small.start(1)
    run(1)
    small.finish(1, o.mid_b)
    small.start(2)
    run(2)
    small.finish(2, o.o_gains)

    def norm_in(l, half, gain):
        def first(rows):
            v = o.in_tokens[half, rows].astype(F32)
            o.stream[0, half, rows] = v
            o.xin[0, p.s, half, rows] = norm_rows(v, gain).astype(BF)

        row_loop(d.half, first)

    for half in range(2):
        norm_in(0, half, o.o_gains[0:1, :])
        gather.start(o.xin.at[0], half)

    top = d.layers - 1
    for l in range(d.layers):
        gain_mid = o.o_gains[2 * l + 1 : 2 * l + 2, :]
        xin, xmid = o.xin.at[l], o.xmid.at[l]
        save(STREAM, l).start()
        run(3 + 10 * l)
        fetch.ready(l, 0)
        fetch.save(l, QKV).start()
        free(l, PROJ)
        third = 3 * d.dh // 3

        def project(pieces):
            block = pair(xin, pieces)
            for n in range(3):
                cols = slice(n * third, (n + 1) * third)
                weight = o.wqkv[l, :, :, :, :, cols].reshape(d.width, third)
                put_pair(o.qkv.at[0], pieces, cols, nn(block, weight))

        project(p.pieces(0))
        gather.near(xin)
        project(p.pieces(1))
        run(4 + 10 * l)

        @pl.loop(2, d.sp_n)
        def _(t):
            gather.far(xin, t)
            project(p.pieces(t))

        gather.end(xin)
        save(XIN, l).start()
        save(PROJ, l).start()
        run(5 + 10 * l)
        free(l, PROBS, ATT)
        attention_forward(d, o, l)
        save(PROBS, l).start()
        run(6 + 10 * l)
        fetch.ready(l, 1)
        fetch.save(l, OUT).start()

        def out_part(pieces):
            blocks = []
            for slot, half in pieces:
                block = o.sorted_att[o.meta[1, slot], half]
                o.att[0, slot, half] = block
                blocks.append(block)
            block = jnp.concatenate(blocks, axis=0)
            for n in range(d.n_width):
                cols = slice(n * d.chunk, (n + 1) * d.chunk)
                weight = o.wout[l, :, :, :, cols].reshape(d.dh, d.chunk)
                put_pair(o.part, pieces, cols, nn(block, weight))

        @pl.loop(2, d.sp_n)
        def _(t):
            out_part(p.pieces(t))
            scatter.put(t)

            @pl.when(t > 2)
            def _():
                scatter.cross(t - 1)

        out_part(p.pieces(1))
        scatter.put(1)
        scatter.cross(d.sp_n - 1)
        out_part(p.pieces(0))
        save(ATT, l).start()
        run(7 + 10 * l)

        def middle(half, rows):
            v = o.stream[l, half, rows] + scatter.total(half, rows)
            o.mid[l, half, rows] = v
            xmid[p.s, half, rows] = norm_rows(v, gain_mid).astype(BF)

        for half in range(2):
            scatter.arrive(half)
            row_loop(d.half, functools.partial(middle, half))
            gather.start(xmid, half)
            if half == 0:
                run(8 + 10 * l)
        scatter.end()
        save(MID, l).start()
        run(9 + 10 * l)
        fetch.ready(l, 2, 3)
        fetch.save(l, UP).start()
        free(l, HID, SLOPE)

        def up(pieces):
            block = pair(xmid, pieces)
            for n in range(d.n_hid):
                cols = slice(n * d.chunk, (n + 1) * d.chunk)
                weight = o.wup[l, :, :, :, :, cols].reshape(d.width, d.chunk)
                pre = nn(block, weight)
                phi = 0.5 * (1.0 + lax.erf(pre * (0.5**0.5)))
                put_pair(o.hid.at[0], pieces, cols, pre * phi)
                density = jnp.exp(-0.5 * pre * pre) * 0.3989422804014327
                put_pair(o.slope.at[0], pieces, cols, phi + pre * density)

        def down(pieces):
            hidden = pair(o.hid.at[0], pieces)
            for n in range(d.n_width):
                cols = slice(n * d.chunk, (n + 1) * d.chunk)
                weight = o.wdown[l, :, :, :, cols].reshape(d.hid, d.chunk)
                put_pair(o.part, pieces, cols, nn(hidden, weight))

        up(p.pieces(0))
        gather.near(xmid)
        up(p.pieces(1))
        run(10 + 10 * l)
        if l == 0:

            @pl.loop(2, d.sp_n)
            def _(t):
                gather.far(xmid, t)
                up(p.pieces(t))

        fetch.ready(l, 4, 5)
        fetch.save(l, DOWN).start()

        @pl.loop(2, d.sp_n)
        def _(t):
            if l > 0:
                gather.far(xmid, t)
                up(p.pieces(t))
                if l < top:

                    @pl.when(t > 2)
                    def _():
                        scatter.cross(t - 1)

            down(p.pieces(t))
            if l < top:
                scatter.put(t)
            if l == 0 and l < top:

                @pl.when(t > 2)
                def _():
                    scatter.cross(t - 1)

        down(p.pieces(1))
        if l < top:
            scatter.put(1)
            scatter.cross(d.sp_n - 1)
        down(p.pieces(0))
        gather.end(xmid)
        save(XMID, l).start()
        save(HID, l).start()
        save(SLOPE, l).start()
        if l == top:
            keep_part = pltpu.make_async_copy(o.part, o.o_part, o.late_sem.at[1])
            keep_part.start()
            continue
        run(11 + 10 * l)

        def last(half, rows):
            v = o.mid[l, half, rows] + scatter.total(half, rows)
            o.stream[l + 1, half, rows] = v
            o.xin[l + 1, p.s, half, rows] = norm_rows(v, o.o_gains[2 * l + 2 : 2 * l + 3, :]).astype(BF)

        for half in range(2):
            scatter.arrive(half)
            row_loop(d.half, functools.partial(last, half))
            gather.start(o.xin.at[l + 1], half)
            if half == 0:
                run(12 + 10 * l)
        scatter.end()

    keep_part.wait()
    fetch.end()
    late.end(o.gl)
    keep_gl.wait()
    for l in range(d.layers):
        for name in SAVED:
            if l == d.layers - 1 or name not in ONCE:
                save(name, l).wait()


class Reduce:
    def __init__(self, p, o):
        self.p, self.o = p, o
        self.grads = (o.g_qkv, o.g_out, o.g_up, o.g_down)
        self.sp_in = (o.x_qkv, o.x_out, o.x_up, None)
        self.result = (o.o_qkv, o.o_out, o.o_up, o.o_down)
        self.done = {}

    def grad(self, l, w):
        return self.o.g_up_odd if w == UP and l % 2 else self.grads[w]

    def z_first(self, l, term):
        return term in self.p.d.z_first[l]

    def ins(self, l, term):
        o = self.o
        return getattr(o, "y_in_%d_%d" % (l, term)), getattr(o, "z_in_%d_%d" % (l, term))

    def columns(self, l, term):
        p = self.p
        if self.z_first(l, term):
            return [(y, y) for y in [p.y] + [p.ypeer(m) for m in range(1, p.d.y_n)]]
        return [(p.y, 0)]

    def step(self, l, *terms):
        for term in terms:
            stages = (self.y_send, self.y_sum, self.inner, self.finish_z)
            if self.z_first(l, term):
                stages = (self.z_send, self.inner, self.z_sum, self.finish_y)
            count = self.done.get((l, term), 0)
            self.done[l, term] = count + 1
            stages[count](l, term)

    def groups(self, term):
        w, first, last = self.p.d.terms[term]
        if w in (QKV, UP):
            return [((j,), (j - first,)) for j in range(first, last)]
        rows = min(32, last - first)
        return [
            ((slice(j, j + rows),), (slice(j - first, j - first + rows),)) for j in range(first, last, rows)
        ]

    def y_copy(self, l, term, k):
        p, o = self.p, self.o
        w, first, last = p.d.terms[term]
        index = p.d.y_n - k - 1
        there = p.ypeer(k)
        into = self.ins(l, term)[0].at[index]
        if self.z_first(l, term):
            src, into = self.grad(l, w).at[p.z, there, first:last], into.at[0]
        else:
            src = self.grad(l, w).at[:, there, first:last]
        return rcopy(src, into, o.ry_send.at[l, term, k], o.ry_recv.at[l, term, index], p.dev(p.z, there))

    def y_send(self, l, term):
        for k in range(1, self.p.d.y_n):
            self.y_copy(l, term, k).start()

    def y_wait(self, l, term):
        for k in range(1, self.p.d.y_n):
            self.y_copy(l, term, self.p.d.y_n - k).wait_recv()

    def y_sum(self, l, term):
        p = self.p
        w = p.d.terms[term][0]
        y_in, _ = self.ins(l, term)
        self.y_wait(l, term)
        for z in range(p.d.z_n):
            for index, here in self.groups(term):
                value = self.grad(l, w)[(z, p.y) + index].astype(F32)
                for m in range(p.d.y_n - 1):
                    value = value + y_in[(m, z) + here].astype(F32)
                self.grad(l, w)[(z, p.y) + index] = value.astype(BF)
        self.z_send(l, term)

    def z_copy(self, l, term, column, z, goal, place, way):
        p, o = self.p, self.o
        w, first, last = p.d.terms[term]
        y, slot = column
        return rcopy(
            self.grad(l, w).at[z, y, first:last],
            self.ins(l, term)[1].at[place, slot],
            o.rz_send.at[l, term, slot, way],
            o.rz_recv.at[l, term, slot, place],
            p.dev(goal, p.y),
        )

    def z_goals(self, inside):
        at = self.p.line()[1]
        if inside:
            return ((at[3], at[2], 3), (at[2], at[2], 1), (at[1], at[1], 0))
        return ((at[1], at[1], 0), (at[2], at[1], 2), (at[3], at[2], 4))

    def both(self, inner, outer):
        inside, _ = self.p.line()
        pl.when(inside)(inner)
        pl.when(jnp.logical_not(inside))(outer)

    def z_send(self, l, term):
        if self.p.d.z_n == 1:
            return

        def send(inside, ways):
            for column in self.columns(l, term):
                for way in ways:
                    self.z_copy(l, term, column, *self.z_goals(inside)[way], way).start()

        self.both(lambda: send(True, (0,)), lambda: send(False, (0, 1, 2)))

    def z_wait(self, l, term, column, place):
        self.z_copy(l, term, column, self.p.z, self.p.z, place, 0).wait_recv()

    def inner(self, l, term):
        p = self.p
        if p.d.z_n == 1:
            return
        w = p.d.terms[term][0]
        _, z_in = self.ins(l, term)

        def relay():
            for way, places in ((1, (2,)), (2, (3, 4))):
                z, goal, place = self.z_goals(True)[way]
                for column in self.columns(l, term):
                    y, slot = column
                    for source in places:
                        self.z_wait(l, term, column, source)
                    for index, here in self.groups(term):
                        value = self.grad(l, w)[(z, y) + index].astype(F32)
                        for source in places:
                            value = value + z_in[(source, slot) + here].astype(F32)
                        self.grad(l, w)[(z, y) + index] = value.astype(BF)
                    self.z_copy(l, term, column, z, goal, place, way).start()

        pl.when(p.line()[0])(relay)

    def z_total(self, l, term, column, store):
        p = self.p
        w = p.d.terms[term][0]
        _, z_in = self.ins(l, term)
        y, slot = column

        def total(places):
            for source in places:
                self.z_wait(l, term, column, source)
            for index, here in self.groups(term):
                value = self.grad(l, w)[(p.z, y) + index].astype(F32)
                for source in places:
                    value = value + z_in[(source, slot) + here].astype(F32)
                store(y, index, here, value)

        if p.d.z_n == 1:
            total(())
        else:
            self.both(lambda: total((0, 1)), lambda: total((0,)))

    def z_sum(self, l, term):
        w = self.p.d.terms[term][0]

        def store(y, index, here, value):
            self.grad(l, w)[(self.p.z, y) + index] = value.astype(BF)

        for column in self.columns(l, term):
            self.z_total(l, term, column, store)
        self.y_send(l, term)

    def finish_z(self, l, term):
        def store(y, index, here, value):
            self.settle(l, term, index, value)

        self.z_total(l, term, self.columns(l, term)[0], store)
        self.pass_on(l, term)

    def finish_y(self, l, term):
        p = self.p
        w = p.d.terms[term][0]
        y_in, _ = self.ins(l, term)
        self.y_wait(l, term)
        for index, here in self.groups(term):
            value = self.grad(l, w)[(p.z, p.y) + index].astype(F32)
            for m in range(p.d.y_n - 1):
                value = value + y_in[(m, 0) + here].astype(F32)
            self.settle(l, term, index, value)
        self.pass_on(l, term)

    def settle(self, l, term, index, value):
        w = self.p.d.terms[term][0]
        if w == DOWN:
            self.result[w][(l,) + index] = value.astype(BF)
        else:
            self.grad(l, w)[(self.p.z, self.p.y) + index] = value.astype(BF)

    def s_copy(self, l, w, j, source):
        p, o = self.p, self.o
        return rcopy(
            self.grad(l, w).at[p.z, p.y, j], self.sp_in[w].at[l, source], o.rs_send.at[l, w, j], o.rs_recv.at[l, w, source], (p.r, j)
        )

    def out_copy(self, l, device):
        p, o = self.p, self.o
        return rcopy(
            self.grad(l, OUT).at[p.z, p.y], self.sp_in[OUT].at[l], o.rs_send.at[l, OUT, 0], o.rs_recv.at[l, OUT, 0], device
        )

    def keep(self, l, w, j, ref):
        d, result = self.p.d, self.result[w]
        if not d.whole_lanes:
            result[l, j] = ref[...]
        elif w == QKV:
            for i in range(3):
                result[l, i, :, j * d.dh : (j + 1) * d.dh] = ref[:, i * d.dh : (i + 1) * d.dh]
        else:
            for k in range(d.dp_n):
                whole, kept = up_columns(d, j, k)
                result[l, :, whole] = ref[:, kept]

    def pass_on(self, l, term):
        p = self.p
        w, first, last = p.d.terms[term]
        if w in (QKV, UP):
            for j in range(first, last):

                @pl.when(p.s == j)
                def _():
                    self.keep(l, w, j, self.grad(l, w).at[p.z, p.y, j])

                @pl.when(p.s != j)
                def _():
                    self.s_copy(l, w, j, p.s).start()

        elif w == OUT:
            _, source, stays = p.moved()

            @pl.when(stays)
            def _():
                self.result[w][l] = self.grad(l, w)[p.z, p.y]

            @pl.when(jnp.logical_not(stays))
            def _():
                self.out_copy(l, source).start()

    def sent(self, l, w):
        p = self.p
        for term, (kind, first, last) in enumerate(p.d.terms):
            if kind != w:
                continue
            for k in range(1, p.d.y_n):
                self.y_copy(l, term, k).wait_send()
            if p.d.z_n > 1:

                def wait(inside):
                    for column in self.columns(l, term):
                        for way in range(3):
                            self.z_copy(l, term, column, *self.z_goals(inside)[way], way).wait_send()

                self.both(lambda: wait(True), lambda: wait(False))
        if w in (QKV, UP):
            for t in range(1, p.d.sp_n):
                self.s_copy(l, w, p.slot(t), p.s).wait_send()
        elif w == OUT:
            _, source, stays = p.moved()

            @pl.when(jnp.logical_not(stays))
            def _():
                self.out_copy(l, source).wait_send()

    def last(self, l, w):
        p = self.p
        if w in (QKV, UP):
            for j in range(p.d.sp_n):

                @pl.when(p.s != j)
                def _():
                    self.s_copy(l, w, j, j).wait_recv()
                    self.keep(l, w, j, self.sp_in[w].at[l, j])
        elif w == OUT:
            _, source, stays = p.moved()

            @pl.when(jnp.logical_not(stays))
            def _():
                self.out_copy(l, source).wait_recv()
                self.result[w][l] = self.sp_in[w][l]


def norm_back(v, d_out, gain):
    center = v - mean_of(v)
    inverse = lax.rsqrt(mean_of(center * center) + EPS)
    unit = center * inverse
    gain_term = jnp.sum(d_out * unit, axis=0, keepdims=True)
    e = d_out * gain
    back = (e - mean_of(e) - unit * mean_of(e * unit)) * inverse
    return back, gain_term


def attention_backward(d, o):
    tok = d.tok
    for i in range(d.sp_n):
        here = o.meta[0, i]
        blocks = range(max(0, i - d.back), i + 1)
        for h in range(d.heads):
            lanes = slice(h * HD, (h + 1) * HD)
            key_lanes = slice(d.dh + h * HD, d.dh + (h + 1) * HD)
            value_lanes = slice(2 * d.dh + h * HD, 2 * d.dh + (h + 1) * HD)
            query = o.qkv[here, :, :, lanes].reshape(tok, HD)
            grad = o.d_att[here, :, :, lanes].reshape(tok, HD)
            d_probs, inner = [], None
            for b in blocks:
                low = o.probs[h, d.pairs.index((i, b))].astype(F32)
                term = nt(grad, o.qkv[o.meta[0, b], :, :, value_lanes].reshape(tok, HD))
                d_probs.append(term)
                weighted = jnp.sum(low * term, axis=-1, keepdims=True)
                inner = weighted if inner is None else inner + weighted
            d_query = None
            for b, term in zip(blocks, d_probs):
                low = o.probs[h, d.pairs.index((i, b))]
                d_score = (low.astype(F32) * (term - inner)).astype(BF)
                step = nn(d_score, o.qkv[o.meta[0, b], :, :, key_lanes].reshape(tok, HD))
                d_query = step if d_query is None else d_query + step
                d_key, d_value = tn(d_score, query), tn(low, grad)
                if b == i:
                    o.d_keys[b, :, lanes] = d_key
                    o.d_values[b, :, lanes] = d_value
                else:
                    o.d_keys[b, :, lanes] += d_key
                    o.d_values[b, :, lanes] += d_value
            o.sorted_dqkv[i, :, :, lanes] = (d_query * HD ** (-0.5)).astype(BF).reshape(2, d.half, HD)
    for b in range(d.sp_n):
        shape = (2, d.half, d.dh)
        o.sorted_dqkv[b, :, :, d.dh : 2 * d.dh] = (o.d_keys[b] * HD ** (-0.5)).astype(BF).reshape(shape)
        o.sorted_dqkv[b, :, :, 2 * d.dh :] = o.d_values[b].astype(BF).reshape(shape)


def bwd_kernel(d, names, *refs):
    o = Refs()
    for name, ref in zip(names, refs):
        setattr(o, name, ref)
    p = Place(d)
    gather = Gather(p, o.ag_send, o.ag_recv)
    scatter = Scatter(p, o.part, o.near, o.far, o.near_send, o.near_recv, o.far_send, o.far_recv)
    small = SmallSum(p, o.gain_sum, o.sp_in, o.mid_a, o.z_in, o.mid_b, o.y_in, o.sp_sem, o.z_sem, o.y_sem)
    reduce = Reduce(p, o)
    loads = WEIGHTS + SAVED

    def load(name, l):
        ref = o.mid if name == STREAM else getattr(o, name)
        return pltpu.make_async_copy(getattr(o, "i_" + name).at[l], ref, o.load_sem.at[loads.index(name)])

    def refill(l, *which):
        if l > 0:
            for name in which:
                load(name, l - 1).start()

    def run(slot):
        for layer, term in BACKWARD_PLAN.get(slot, ()):
            reduce.step(layer, term)

    top = d.layers - 1
    first_grad = pltpu.make_async_copy(o.i_gl, o.gl, o.late_sem.at[0])
    first_grad.start()
    for name in (W_DOWN, SLOPE, W_UP, HID, XMID, MID, W_OUT, PROJ, PROBS, ATT, W_QKV, XIN):
        load(name, top).start()
    p.barrier()
    lay_out(d, o)
    o.gain_sum[...] = jnp.zeros_like(o.gain_sum)

    first_grad.wait()
    for half in range(2):

        def begin(rows):
            o.o_grad[half, rows] = o.gl[p.s, half, rows].astype(F32)

        row_loop(d.half, begin)
    tokens = d.sp_n * d.tok

    def rows_of(ref, n, count):
        part = ref[n * d.z_n // count : (n + 1) * d.z_n // count]
        return part.reshape(d.chunk, part.shape[-1])

    def weight_grad(out, left_ref, right_ref, count, width):
        for n in range(count):
            left = left_ref[:, :, :, n * d.chunk : (n + 1) * d.chunk].reshape(tokens, d.chunk)
            value = tn(left, right_ref[...].reshape(tokens, width)).astype(BF)
            zs = slice(n * d.z_n // count, (n + 1) * d.z_n // count)
            out[zs] = value.reshape((d.z_n // count,) + out.shape[1:])

    for l in reversed(range(d.layers)):
        gain_in = o.in_gains[2 * l : 2 * l + 1, :]
        gain_mid = o.in_gains[2 * l + 1 : 2 * l + 2, :]
        run(0 + 14 * (top - l))
        load(W_DOWN, l).wait()
        load(SLOPE, l).wait()
        load(W_UP, l).wait()

        def pre_grad(pieces):
            block = pair(o.gl, pieces)
            for n in range(d.n_hid):
                cols = slice(n * d.chunk, (n + 1) * d.chunk)
                d_hidden = nt(block, rows_of(o.wdown, n, d.n_hid))
                put_pair(o.slope, pieces, cols, d_hidden * pair(o.slope, pieces, cols).astype(F32))

        def mid_grad(pieces):
            d_pre = pair(o.slope, pieces)
            for n in range(d.n_width):
                cols = slice(n * d.chunk, (n + 1) * d.chunk)
                put_pair(o.part, pieces, cols, nt(d_pre, rows_of(o.wup, n, d.n_width)))

        if l < top:
            pre_grad(p.pieces(0))
            gather.near(o.gl)
            pre_grad(p.pieces(1))
        run(1 + 14 * (top - l))

        @pl.loop(2, d.sp_n)
        def _(t):
            if l < top:
                gather.far(o.gl, t)
            pre_grad(p.pieces(t))

            @pl.when(t > 2)
            def _():
                scatter.cross(t - 1)

            mid_grad(p.pieces(t))
            scatter.put(t)

        if l == top:
            pre_grad(p.pieces(1))
        mid_grad(p.pieces(1))
        scatter.put(1)
        scatter.cross(d.sp_n - 1)
        if l == top:
            pre_grad(p.pieces(0))
        mid_grad(p.pieces(0))
        if l < top:
            gather.end(o.gl)
        refill(l, W_DOWN, W_UP)
        load(HID, l).wait()
        run(2 + 14 * (top - l))
        if l < top:
            reduce.sent(l + 1, DOWN)
        weight_grad(o.g_down, o.hid, o.gl, d.n_hid, d.width)
        run(3 + 14 * (top - l))
        refill(l, HID)
        load(MID, l).wait()

        def middle(half, rows):
            back, gain_term = norm_back(o.mid[half, rows], scatter.total(half, rows), gain_mid)
            o.gain_sum[2 * l + 1 : 2 * l + 2, :] += gain_term
            value = o.o_grad[half, rows] + back
            o.o_grad[half, rows] = value
            o.ml[p.s, half, rows] = value.astype(BF)

        for half in range(2):
            scatter.arrive(half)
            row_loop(d.half, functools.partial(middle, half))
            gather.start(o.ml, half)
            if half == 0:
                run(4 + 14 * (top - l))
        scatter.end()
        load(STREAM, l).start()
        load(XMID, l).wait()
        run(5 + 14 * (top - l))
        if l + 2 <= top:
            reduce.sent(l + 2, UP)
        weight_grad(reduce.grad(l, UP), o.xmid, o.slope, d.n_width, d.hid)
        run(6 + 14 * (top - l))
        refill(l, XMID, SLOPE)
        load(W_OUT, l).wait()

        def att_grad(pieces):
            weight = o.wout[...].reshape(d.dh, d.width)
            put_pair(o.d_att, pieces, slice(None), nt(pair(o.ml, pieces), weight))

        att_grad(p.pieces(0))
        gather.near(o.ml)
        att_grad(p.pieces(1))
        run(7 + 14 * (top - l))

        @pl.loop(2, d.sp_n)
        def _(t):
            gather.far(o.ml, t)
            att_grad(p.pieces(t))

        gather.end(o.ml)
        refill(l, W_OUT)
        run(8 + 14 * (top - l))
        load(PROJ, l).wait()
        load(PROBS, l).wait()
        attention_backward(d, o)
        refill(l, PROJ, PROBS)
        run(9 + 14 * (top - l))
        load(W_QKV, l).wait()

        def in_grad(pieces):
            blocks = []
            for slot, half in pieces:
                block = o.sorted_dqkv[o.meta[1, slot], half]
                o.d_qkv[slot, half] = block
                blocks.append(block)
            block = jnp.concatenate(blocks, axis=0)
            for n in range(d.n_width):
                cols = slice(n * d.chunk, (n + 1) * d.chunk)
                put_pair(o.part, pieces, cols, nt(block, rows_of(o.wqkv, n, d.n_width)))

        @pl.loop(2, d.sp_n)
        def _(t):
            in_grad(p.pieces(t))
            scatter.put(t)

            @pl.when(t > 2)
            def _():
                scatter.cross(t - 1)

        in_grad(p.pieces(1))
        scatter.put(1)
        scatter.cross(d.sp_n - 1)
        in_grad(p.pieces(0))
        run(10 + 14 * (top - l))
        refill(l, W_QKV)
        load(ATT, l).wait()
        if l < top:
            reduce.sent(l + 1, OUT)
        value = tn(o.att[...].reshape(tokens, d.dh), o.ml[...].reshape(tokens, d.width)).astype(BF)
        o.g_out[...] = value.reshape((d.z_n, d.y_n, d.rows, d.width))
        run(11 + 14 * (top - l))
        refill(l, ATT)
        load(XIN, l).wait()
        if l < top:
            reduce.sent(l + 1, QKV)
        weight_grad(o.g_qkv, o.xin, o.d_qkv, d.n_width, 3 * d.dh)
        run(12 + 14 * (top - l))
        refill(l, XIN)
        load(STREAM, l).wait()

        def lower(half, rows):
            back, gain_term = norm_back(o.mid[half, rows], scatter.total(half, rows), gain_in)
            o.gain_sum[2 * l : 2 * l + 1, :] += gain_term
            value = o.o_grad[half, rows] + back
            o.o_grad[half, rows] = value
            if l > 0:
                o.gl[p.s, half, rows] = value.astype(BF)

        for half in range(2):
            scatter.arrive(half)
            row_loop(d.half, functools.partial(lower, half))
            if l > 0:
                gather.start(o.gl, half)
            if half == 0:
                run(13 + 14 * (top - l))
        scatter.end()
        if l == 0:
            small.start(0)
        refill(l, MID)

    keep_part = pltpu.make_async_copy(o.i_part, o.part, o.late_sem.at[1])
    keep_part.start()
    load(MID, top).start()
    run(28)
    small.finish(0, o.mid_a)
    small.start(1)
    keep_part.wait()
    for t in range(d.sp_n - 1, 1, -1):
        scatter.near_copy(p.slot(t // 2 * 2) // 2, t % 2).start()
    scatter.put(1)
    run(29)
    for t in range(d.sp_n - 1, 1, -1):
        scatter.cross(t)
    run(30)
    small.finish(1, o.mid_b)
    small.start(2)
    run(31)
    load(MID, top).wait()

    def last(half, rows):
        o.o_output[half, rows] = (o.mid[half, rows] + scatter.total(half, rows)).astype(BF)

    for half in range(2):
        scatter.arrive(half)
        row_loop(d.half, functools.partial(last, half))
    scatter.end()
    run(32)
    small.finish(2, o.o_gains)
    for l in reversed(range(d.layers)):
        for w in (DOWN, UP, OUT, QKV):
            reduce.last(l, w)
    for w in (DOWN, UP, OUT, QKV):
        reduce.sent(0, w)
    if top > 0:
        reduce.sent(1, UP)


def finish_kernel(d, names, *refs):
    o = Refs()
    for name, ref in zip(names, refs):
        setattr(o, name, ref)
    arrays = (
        (o.o_qkv, o.a_qkv, o.b_qkv, o.r_qkv),
        (o.o_out, o.a_out, o.b_out, o.r_out),
        (o.o_up, o.a_up, o.b_up, o.r_up),
        (o.o_down, o.a_down, o.b_down, o.r_down),
        (o.o_grad, o.a_grad, o.a_grad, o.r_grad),
        (o.o_output, o.a_output, o.a_output, o.r_output),
    )
    copies = []
    reads = [pltpu.make_async_copy(a[0], a[1], o.in_sem.at[n]) for n, a in enumerate(arrays)]
    for copy in reads:
        copy.start()
    for n, (_, low, full, result) in enumerate(arrays):
        reads[n].wait()
        if full is not low:
            for l in range(d.layers):
                full[l] = low[l].astype(F32)
        copies.append(pltpu.make_async_copy(full, result, o.out_sem.at[n]))
        copies[-1].start()
    own = o.r_gains.shape[1]
    flat = lax.axis_index(AXES[0]) * d.sp_n + lax.axis_index(AXES[1])
    mine = jnp.zeros(o.r_gains.shape, F32)
    for k in range(d.width // own):
        mine = jnp.where(flat == k, o.o_gains[: o.r_gains.shape[0], k * own : (k + 1) * own], mine)
    o.r_gains[...] = mine
    for copy in copies:
        copy.wait()


ANY = pl.BlockSpec(memory_space=pl.ANY)
VM = pl.BlockSpec(memory_space=pltpu.VMEM)
SM = pl.BlockSpec(memory_space=pltpu.SMEM)


def call(kernel, d, inputs, outputs, scratch, identity):
    names = [i[0] for i in inputs] + [i[0] for i in outputs] + [i[0] for i in scratch]
    results = pl.pallas_call(
        functools.partial(kernel, d, names),
        out_shape=[jax.ShapeDtypeStruct(i[2], i[3]) for i in outputs],
        in_specs=[i[1] for i in inputs],
        out_specs=[i[1] for i in outputs],
        scratch_shapes=[i[1] for i in scratch],
        compiler_params=pltpu.CompilerParams(
            collective_id=identity, has_side_effects=identity is not None, vmem_limit_bytes=62 * 1024 * 1024
        ),
        name=kernel.__name__,
    )(*[i[2] for i in inputs])
    return dict(zip([i[0] for i in outputs], results))


def shards(dp_n, sp_n, tokens, cotangent, w_qkv, w_out, w_up, w_down, gains, piece_order, doc_lengths):
    _, tok, width = tokens.shape
    layers, _, rows, _ = w_qkv.shape
    ff = w_up.shape[-1]
    d = Dims(dp_n, sp_n, layers, tok, width, ff, doc_lengths.shape[1])
    r, s = lax.axis_index(AXES[0]), lax.axis_index(AXES[1])

    own = gains.shape[-1]
    padded = jnp.zeros((8, width), F32)
    padded = lax.dynamic_update_slice(
        padded, gains.reshape(2 * layers, own).astype(F32), (0, (r * sp_n + s) * own)
    )
    lay_scratch = []
    if d.whole_lanes:
        lay_scratch = [
            ("in_qkv", pltpu.VMEM((layers, sp_n, rows, 3 * d.dh), BF)),
            ("in_up", pltpu.VMEM((layers, sp_n, rows, d.hid), BF)),
        ]
        given = [("raw_qkv", VM, w_qkv), ("raw_up", VM, w_up)]
    else:
        in_qkv = w_qkv.reshape(layers, 3, rows, sp_n, d.dh).transpose(0, 3, 2, 1, 4)
        in_up = w_up.reshape(layers, rows, dp_n, sp_n, d.hid_own).transpose(0, 3, 1, 2, 4)
        given = [
            ("in_qkv", ANY, in_qkv.reshape(layers, sp_n, rows, 3 * d.dh)),
            ("in_up", ANY, in_up.reshape(layers, sp_n, rows, d.hid)),
        ]

    saved, weights = saved_shapes(d), weight_shapes(d)
    dma = pltpu.SemaphoreType.DMA
    fwd = call(
        fwd_kernel,
        d,
        [
            ("in_order", SM, piece_order),
            ("in_lengths", SM, doc_lengths),
            ("in_tokens", VM, tokens.reshape(2, d.half, width)),
            ("in_cotangent", VM, cotangent.reshape(2, d.half, width)),
            ("in_gains", VM, padded),
            ("in_out", ANY, w_out),
            ("in_down", ANY, w_down),
        ]
        + given,
        [("o_gains", VM, (8, width), F32)]
        + [("o_" + n, ANY, (layers,) + weights[n][0], BF) for n in WEIGHTS]
        + [("o_" + n, ANY, (layers,) + saved[n][0], saved[n][1]) for n in SAVED]
        + [("o_gl", ANY, (sp_n, 2, d.half, width), BF), ("o_part", ANY, (sp_n, 2, d.half, width), BF)],
        [(n, pltpu.VMEM((layers,) + weights[n][0], BF)) for n in WEIGHTS]
        + [(n, pltpu.VMEM((1 if n in ONCE else layers,) + saved[n][0], saved[n][1])) for n in SAVED]
        + [
            ("sorted_att", pltpu.VMEM(saved[ATT][0], BF)),
            ("meta", pltpu.SMEM((3, max(sp_n, d.docs)), jnp.int32)),
        ]
        + [
            ("gl", pltpu.VMEM((sp_n, 2, d.half, width), BF)),
            ("late_send", dma((2, sp_n, 2))),
            ("late_recv", dma((sp_n, 2))),
            ("late_sem", dma((2,))),
        ]
        + lay_scratch
        + small_scratch(d)
        + comm_scratch(d)
        + [
            ("s_send", dma((layers, 4, sp_n))),
            ("s_recv", dma((layers, 4, sp_n))),
            ("own_sem", dma((layers, 4))),
            ("b_send", dma((layers, len(d.pieces), d.z_n, d.y_n, 1 + d.y_n))),
            ("b_recv", dma((layers, len(d.pieces), d.z_n, d.y_n))),
            ("w_sem", dma((layers, 4))),
            ("save_sem", dma((layers, len(SAVED)))),
        ],
        0,
    )
    kinds = ("qkv", "out", "up", "down")
    blocks = [d.block_shape(w) for w in range(4)]
    results = [(layers,) + b for b in blocks]
    if d.whole_lanes:
        results[QKV], results[UP] = w_qkv.shape, w_up.shape
    bwd = call(
        bwd_kernel,
        d,
        [("in_order", SM, piece_order), ("in_lengths", SM, doc_lengths), ("i_gl", ANY, fwd["o_gl"]), ("i_part", ANY, fwd["o_part"]), ("in_gains", VM, fwd["o_gains"])]
        + [("i_" + n, ANY, fwd["o_" + n]) for n in WEIGHTS + SAVED],
        [("o_output", VM, (2, d.half, width), BF), ("o_grad", VM, (2, d.half, width), F32), ("o_gains", VM, (8, width), F32)]
        + [("o_" + k, VM, shape, BF) for k, shape in zip(kinds, results)],
        [(n, pltpu.VMEM(weights[n][0], BF)) for n in WEIGHTS]
        + [(n, pltpu.VMEM(saved[n][0], saved[n][1])) for n in SAVED if n != STREAM]
        + [
            ("gl", pltpu.VMEM((sp_n, 2, d.half, width), BF)),
            ("ml", pltpu.VMEM((sp_n, 2, d.half, width), BF)),
            ("d_att", pltpu.VMEM((sp_n, 2, d.half, d.dh), BF)),
            ("sorted_dqkv", pltpu.VMEM((sp_n, 2, d.half, 3 * d.dh), BF)),
            ("d_qkv", pltpu.VMEM((sp_n, 2, d.half, 3 * d.dh), BF)),
            ("d_keys", pltpu.VMEM((sp_n, tok, d.dh), F32)),
            ("d_values", pltpu.VMEM((sp_n, tok, d.dh), F32)),
            ("gain_sum", pltpu.VMEM((8, width), F32)),
            ("meta", pltpu.SMEM((3, max(sp_n, d.docs)), jnp.int32)),
        ]
        + [("g_" + k, pltpu.VMEM((d.z_n, d.y_n) + b, BF)) for k, b in zip(kinds, blocks)]
        + [("g_up_odd", pltpu.VMEM((d.z_n, d.y_n) + blocks[UP], BF))]
        + [i for l in range(layers) for t in range(len(d.terms)) for i in term_scratch(d, l, t)]
        + [("x_" + k, pltpu.VMEM((layers,) + b, BF)) for k, b in zip(kinds[:3], blocks)]
        + small_scratch(d)
        + comm_scratch(d)
        + [
            ("late_sem", dma((2,))),
            ("load_sem", dma((len(WEIGHTS + SAVED),))),
            ("ry_send", dma((layers, len(d.terms), d.y_n))),
            ("ry_recv", dma((layers, len(d.terms), d.y_n))),
            ("rz_send", dma((layers, len(d.terms), d.y_n, 3))),
            ("rz_recv", dma((layers, len(d.terms), d.y_n, 5))),
            ("rs_send", dma((layers, 4, sp_n))),
            ("rs_recv", dma((layers, 4, sp_n))),
        ],
        1,
    )
    done = call(
        finish_kernel,
        d,
        [("o_" + k, ANY, bwd["o_" + k]) for k in kinds + ("grad", "output")] + [("o_gains", VM, bwd["o_gains"])],
        [("r_" + k, ANY, bwd["o_" + k].shape, F32) for k in kinds]
        + [
            ("r_grad", ANY, bwd["o_grad"].shape, F32),
            ("r_output", ANY, bwd["o_output"].shape, BF),
            ("r_gains", VM, (2 * layers, own), F32),
        ],
        [("a_" + k, pltpu.VMEM(bwd["o_" + k].shape, BF)) for k in kinds]
        + [("b_" + k, pltpu.VMEM(bwd["o_" + k].shape, F32)) for k in kinds]
        + [("a_grad", pltpu.VMEM(bwd["o_grad"].shape, F32)), ("a_output", pltpu.VMEM(bwd["o_output"].shape, BF))]
        + [("in_sem", dma((6,))), ("out_sem", dma((6,)))],
        None,
    )
    grad_qkv, grad_out, grad_up, grad_down = (done["r_" + k] for k in kinds)
    if not d.whole_lanes:
        grad_qkv = grad_qkv.reshape(layers, sp_n, rows, 3, d.dh).transpose(0, 3, 2, 1, 4).reshape(w_qkv.shape)
        grad_up = grad_up.reshape(layers, sp_n, rows, dp_n, d.hid_own).transpose(0, 2, 3, 1, 4).reshape(w_up.shape)
    return (
        done["r_output"].reshape(tokens.shape),
        done["r_grad"].reshape(tokens.shape),
        grad_qkv,
        grad_out,
        grad_up,
        grad_down,
        done["r_gains"].reshape(gains.shape),
    )


def solution(mesh):
    dp, sp = AXES
    by_token, by_axis = P(dp, sp, None), P(dp, None)
    by_row, by_third = P(None, AXES, None), P(None, None, AXES)
    return jax.shard_map(
        functools.partial(shards, mesh.shape[dp], mesh.shape[sp]),
        mesh=mesh,
        in_specs=(by_token, by_token, by_third, by_row, by_row, by_row, by_third, by_axis, by_axis),
        out_specs=(by_token, by_token, by_third, by_row, by_row, by_row, by_third),
        check_vma=False,
    )
```

```python
import functools

import jax
import jax.numpy as jnp
from jax import lax
from jax.experimental import pallas as pl
from jax.experimental.pallas import tpu as pltpu
from jax.sharding import PartitionSpec as P

HEADS = 8
HD = 128
EPS = 1e-05
MASKED = -1e30
MESH = pl.DeviceIdType.MESH
BF = jnp.bfloat16
F32 = jnp.float32
AXES = ("dp", "sp")
QKV, OUT, UP, DOWN = range(4)
Q0, Q1, O0, U0, U1, D0, D1 = range(7)
SPREAD, OWN, START_Z, START_Y, RELAY_1, INNER, OUTER, RELAY_3, LATE_START, LATE_ON, LATE_END = range(11)


def nn(a, b):
    return lax.dot_general(a, b, (((1,), (0,)), ((), ())), preferred_element_type=F32)


def nt(a, b):
    return lax.dot_general(a, b, (((1,), (1,)), ((), ())), preferred_element_type=F32)


def tn(a, b):
    return lax.dot_general(a, b, (((0,), (0,)), ((), ())), preferred_element_type=F32)


FORWARD_PLAN = {
    0: ((OWN, 0, 3), (START_Y, 0, 5), (START_Z, 0, 4), (OWN, 0, 0), (OWN, 0, 1), (START_Y, 0, 0), (START_Z, 0, 0), (SPREAD, 1, 2),),
    1: ((INNER, 0, 0), (START_Z, 0, 1), (LATE_START, 0, 1), (RELAY_1, 0, 0),),
    2: ((OUTER, 0, 0), (OWN, 0, 2), (RELAY_3, 0, 0), (START_Y, 0, 2), (START_Z, 0, 3), (INNER, 0, 1),),
    3: ((START_Y, 0, 3), (RELAY_1, 0, 1), (SPREAD, 1, 3), (LATE_START, 0, 0), (START_Z, 0, 2), (OUTER, 0, 1),),
    4: ((START_Y, 0, 1), (OWN, 1, 3), (INNER, 0, 4), (RELAY_1, 0, 4), (SPREAD, 1, 0), (RELAY_3, 0, 1), (INNER, 0, 3),),
    5: ((RELAY_1, 0, 2), (START_Z, 0, 5), (SPREAD, 1, 1), (RELAY_3, 0, 4), (RELAY_1, 0, 3),),
    6: ((OWN, 1, 0), (INNER, 0, 2), (OWN, 1, 2), (OUTER, 0, 3),),
    7: ((RELAY_1, 0, 5), (RELAY_3, 0, 2), (INNER, 0, 5), (LATE_ON, 0, 0), (RELAY_3, 0, 3), (OWN, 1, 1), (OUTER, 0, 2), (START_Z, 1, 0),),
    8: ((START_Z, 1, 4), (START_Y, 1, 0), (LATE_ON, 0, 1),),
    9: ((OUTER, 0, 5), (START_Z, 1, 3), (OUTER, 0, 4), (START_Y, 1, 1),),
    10: ((START_Y, 0, 4), (START_Z, 1, 2), (START_Z, 1, 1), (START_Y, 1, 2), (LATE_END, 0, 0), (RELAY_1, 1, 0), (RELAY_3, 0, 5),),
    11: ((START_Y, 1, 5), (START_Y, 1, 4), (INNER, 1, 0), (OUTER, 1, 0),),
    12: ((RELAY_1, 1, 1), (START_Z, 1, 5),),
    13: ((RELAY_3, 1, 0), (RELAY_1, 1, 4), (INNER, 1, 3), (RELAY_1, 1, 5), (INNER, 1, 1),),
    14: ((INNER, 1, 2), (START_Y, 1, 3), (RELAY_3, 1, 1),),
    15: ((INNER, 1, 5), (INNER, 1, 4), (OUTER, 1, 1), (RELAY_1, 1, 2), (RELAY_1, 1, 3),),
    16: ((RELAY_3, 1, 4), (OUTER, 1, 3), (OUTER, 1, 2),),
    17: ((OUTER, 1, 5),),
    18: ((OUTER, 1, 4), (RELAY_3, 1, 2), (RELAY_3, 1, 5), (RELAY_3, 1, 3),),
}
BACKWARD_PLAN = {
    3: ((1, D0),),
    4: ((1, D1),),
    6: ((1, U1),),
    7: ((1, U0), (1, D0),),
    10: ((1, D1),),
    11: ((1, D0),),
    12: ((1, Q0), (1, D1), (1, U1),),
    13: ((1, Q1), (1, O0),),
    14: ((1, Q0), (1, U1),),
    15: ((1, U0), (1, D0),),
    16: ((1, D1),),
    17: ((0, D1), (0, D0), (1, Q1), (1, U0),),
    18: ((1, O0), (1, Q1),),
    19: ((1, Q0),),
    20: ((1, O0),),
    21: ((0, D1), (1, Q0),),
    22: ((1, Q1), (1, O0),),
    23: ((0, D1), (0, U1), (0, D0),),
    24: ((0, U0),),
    25: ((0, D1), (1, U0),),
    26: ((0, D0), (0, Q1), (0, U1), (0, Q0),),
    28: ((0, D0),),
    29: ((0, Q1), (0, U0), (0, Q1), (0, U1), (0, O0),),
    30: ((0, U0), (0, O0), (0, Q0),),
    31: ((0, O0), (0, U0), (0, U1), (0, Q1),),
    32: ((0, Q0), (1, U1), (0, O0), (0, Q0),),
}


class Dims:
    def __init__(self, dp_n, sp_n, layers, tok, width, ff, docs):
        self.dp_n, self.sp_n, self.layers, self.tok, self.width = dp_n, sp_n, layers, tok, width
        self.z_n = 4 if dp_n % 4 == 0 else 1
        self.y_n = dp_n // self.z_n
        self.x_n = sp_n // 2
        self.rows = width // (dp_n * sp_n)
        self.heads = HEADS // sp_n
        self.dh = width // sp_n
        self.hid = ff // sp_n
        self.hid_own = ff // (dp_n * sp_n)
        self.docs = docs
        self.whole_lanes = self.hid_own % 128 == 0
        self.chunk = min(256, tok)
        self.half = tok // 2
        self.n_width = width // self.chunk
        self.n_hid = self.hid // self.chunk
        self.back = self.x_n
        half, part = sp_n // 2, self.hid_own // 2
        self.pieces = (
            (QKV, 0, sp_n, False),
            (OUT, 0, self.rows, False),
            (UP, 0, half, False),
            (UP, half, sp_n, False),
            (DOWN, 0, part, False),
            (DOWN, part, self.hid_own, True),
        )
        self.terms = (
            (QKV, 0, half),
            (QKV, half, sp_n),
            (OUT, 0, self.rows),
            (UP, 0, half),
            (UP, half, sp_n),
            (DOWN, 0, part),
            (DOWN, part, self.hid_own),
        )
        self.z_first = [(Q1,)] + [(D1,)] * (layers - 1)
        self.pairs = [(i, b) for i in range(sp_n) for b in range(max(0, i - self.back), i + 1)]

    def block_shape(self, which):
        return {
            QKV: (self.sp_n, self.rows, 3 * self.dh),
            OUT: (self.rows, self.width),
            UP: (self.sp_n, self.rows, self.hid),
            DOWN: (self.hid_own, self.width),
        }[which]


class Place:
    def __init__(self, d):
        self.d = d
        self.r = lax.axis_index(AXES[0])
        self.s = lax.axis_index(AXES[1])
        self.z, self.y = self.r // d.y_n, self.r % d.y_n
        self.x, self.c = self.s // 2, self.s % 2
        self.partner = self.x * 2 + (self.c + 1) % 2

    def slot(self, step):
        return ((self.x + step // 2) % self.d.x_n) * 2 + (self.c + step % 2) % 2

    def pieces(self, step):
        if isinstance(step, int) and step < 2:
            return (self.slot(step), 0), (self.slot(step), 1)
        first = step // 2 * 2
        return (self.slot(first), step % 2), (self.slot(first + 1), step % 2)

    def zpeer(self, dz):
        return (self.z + dz) % self.d.z_n

    def ypeer(self, dy):
        return (self.y + dy) % self.d.y_n

    def line(self):
        high = self.z // 2
        inside = ((self.z + 1) // 2) % 2
        first = inside * 3 * high + (1 - inside) * (1 + high)
        return inside == 1, (self.z, first, 2 - high, 3 - 3 * high)

    def dev(self, z, y):
        return (z * self.d.y_n + y, self.s)

    def moved(self):
        d = self.d
        flat = self.r * d.sp_n + self.s
        goal = (flat % d.dp_n, flat // d.dp_n)
        mine = self.s * d.dp_n + self.r
        source = (mine // d.sp_n, mine % d.sp_n)
        stays = flat == mine
        return goal, source, stays

    def barrier(self):
        d = self.d
        sem = pltpu.get_barrier_semaphore()
        peers = [(self.r, self.slot(t)) for t in range(1, d.sp_n)]
        peers += [self.dev(self.zpeer(k), self.y) for k in range(1, d.z_n)]
        peers += [self.dev(self.z, self.ypeer(k)) for k in range(1, d.y_n)]
        for peer in peers:
            pl.semaphore_signal(sem, inc=1, device_id=peer, device_id_type=MESH)
        goal, source, stays = self.moved()

        @pl.when(jnp.logical_not(stays))
        def _():
            pl.semaphore_signal(sem, inc=1, device_id=goal, device_id_type=MESH)
            pl.semaphore_signal(sem, inc=1, device_id=source, device_id_type=MESH)
            pl.semaphore_wait(sem, len(peers) + 2)

        @pl.when(stays)
        def _():
            pl.semaphore_wait(sem, len(peers))


def rcopy(src, dst, send, recv, device):
    return pltpu.make_async_remote_copy(
        src_ref=src, dst_ref=dst, send_sem=send, recv_sem=recv, device_id=device, device_id_type=MESH
    )


def pair(ref, pieces, *cols):
    return jnp.concatenate([ref[(slot, half) + (slice(None),) + cols] for slot, half in pieces], axis=0)


def put_pair(ref, pieces, cols, value):
    rows = value.shape[0] // 2
    for k, (slot, half) in enumerate(pieces):
        ref[slot, half, :, cols] = value[k * rows : (k + 1) * rows].astype(ref.dtype)


class Gather:
    def __init__(self, p, send, recv):
        self.p, self.send, self.recv = p, send, recv

    def copy(self, buf, slot, half, way, goal):
        block = buf.at[slot, half]
        return rcopy(block, block, self.send.at[way, goal, half], self.recv.at[slot, half], (self.p.r, goal))

    def start(self, buf, half):
        p = self.p
        for dx in range(1, p.d.x_n):
            self.copy(buf, p.s, half, 0, p.slot(2 * dx)).start()
        self.copy(buf, p.s, half, 0, p.partner).start()

    def onward(self, buf, slot, half):
        block = buf.at[slot, half]
        p = self.p
        return rcopy(block, block, self.send.at[1, slot, half], self.recv.at[slot, half], (p.r, p.partner))

    def arrived(self, buf, slot, half):
        self.copy(buf, slot, half, 0, self.p.partner).wait_recv()

    def near(self, buf):
        for half in range(2):
            self.arrived(buf, self.p.partner, half)

    def through(self, buf, step):
        first, _ = self.p.pieces(step)
        self.arrived(buf, *first)
        self.onward(buf, *first).start()

    def rest(self, buf):
        self.near(buf)
        for step in range(2, self.p.d.sp_n):
            self.arrived(buf, *self.p.pieces(step)[1])

    def far(self, buf, step):
        first, second = self.p.pieces(step)
        self.arrived(buf, *first)
        self.onward(buf, *first).start()
        self.arrived(buf, *second)

    def end(self, buf):
        p = self.p
        for half in range(2):
            for dx in range(1, p.d.x_n):
                self.copy(buf, p.s, half, 0, p.slot(2 * dx)).wait_send()
                self.onward(buf, p.slot(2 * dx), half).wait_send()
            self.copy(buf, p.s, half, 0, p.partner).wait_send()


class Scatter:
    def __init__(self, p, part, near, far, near_send, near_recv, far_send, far_recv):
        self.p, self.part, self.near, self.far = p, part, near, far
        self.near_send, self.near_recv, self.far_send, self.far_recv = near_send, near_recv, far_send, far_recv

    def near_copy(self, x, half):
        p = self.p
        return rcopy(
            self.part.at[x * 2 + (p.c + 1) % 2, half],
            self.near.at[x, half],
            self.near_send.at[x, half],
            self.near_recv.at[x, half],
            (p.r, p.partner),
        )

    def far_copy(self, x, half, source):
        p = self.p
        goal = x * 2 + p.c
        return rcopy(
            self.part.at[goal, half],
            self.far.at[source, half],
            self.far_send.at[x, half],
            self.far_recv.at[source, half],
            (p.r, goal),
        )

    def put(self, step):
        if isinstance(step, int):
            if step == 1:
                for half in range(2):
                    self.near_copy(self.p.x, half).start()
        else:
            self.near_copy(self.p.slot(step // 2 * 2) // 2, step % 2).start()

    def cross(self, step):
        p = self.p
        slot, half = p.slot(step // 2 * 2), step % 2
        x = slot // 2
        self.near_copy(x, half).wait_recv()
        size = min(64, p.d.half)

        @pl.loop(0, p.d.half // size, unroll=True)
        def _(i):
            rows = pl.ds(pl.multiple_of(i * size, size), size)
            both = self.part[slot, half, rows].astype(F32) + self.near[x, half, rows].astype(F32)
            self.part[slot, half, rows] = both.astype(BF)

        self.far_copy(x, half, p.x).start()

    def arrive(self, half):
        p = self.p
        self.near_copy(p.x, half).wait_recv()
        for dx in range(1, p.d.x_n):
            x = (p.x + dx) % p.d.x_n
            self.far_copy(x, half, x).wait_recv()

    def total(self, half, rows):
        p = self.p
        value = self.part[p.s, half, rows].astype(F32) + self.near[p.x, half, rows].astype(F32)
        for dx in range(1, p.d.x_n):
            value = value + self.far[(p.x + dx) % p.d.x_n, half, rows].astype(F32)
        return value

    def end(self):
        p = self.p
        for half in range(2):
            for dx in range(p.d.x_n):
                x = (p.x + dx) % p.d.x_n
                self.near_copy(x, half).wait_send()
                if dx:
                    self.far_copy(x, half, p.x).wait_send()


class SmallSum:
    def __init__(self, p, first, sp_in, mid_a, z_in, mid_b, y_in, sp_sem, z_sem, y_sem):
        self.p = p
        self.bufs = ((first, sp_in, sp_sem), (mid_a, z_in, z_sem), (mid_b, y_in, y_sem))

    def plan(self, stage):
        p = self.p
        if stage == 0:
            return p.s, [(p.slot(t), (p.r, p.slot(t))) for t in range(1, p.d.sp_n)]
        if stage == 1:
            return p.z, [(p.zpeer(k), p.dev(p.zpeer(k), p.y)) for k in range(1, p.d.z_n)]
        return p.y, [(p.ypeer(k), p.dev(p.z, p.ypeer(k))) for k in range(1, p.d.y_n)]

    def start(self, stage):
        src, dst, sem = self.bufs[stage]
        own, peers = self.plan(stage)
        for index, device in peers:
            rcopy(src, dst.at[own], sem.at[0, index], sem.at[1, own], device).start()

    def finish(self, stage, result):
        src, dst, sem = self.bufs[stage]
        own, peers = self.plan(stage)
        value = src[...]
        for index, device in peers:
            rcopy(src, dst.at[index], sem.at[0, index], sem.at[1, index], device).wait_recv()
            value = value + dst[index]
        result[...] = value
        for index, device in peers:
            rcopy(src, dst.at[own], sem.at[0, index], sem.at[1, own], device).wait_send()


def small_scratch(d):
    return [
        ("sp_in", pltpu.VMEM((d.sp_n, 8, d.width), F32)),
        ("mid_a", pltpu.VMEM((8, d.width), F32)),
        ("z_in", pltpu.VMEM((d.z_n, 8, d.width), F32)),
        ("mid_b", pltpu.VMEM((8, d.width), F32)),
        ("y_in", pltpu.VMEM((d.y_n, 8, d.width), F32)),
        ("sp_sem", pltpu.SemaphoreType.DMA((2, d.sp_n))),
        ("z_sem", pltpu.SemaphoreType.DMA((2, d.z_n))),
        ("y_sem", pltpu.SemaphoreType.DMA((2, d.y_n))),
    ]


def comm_scratch(d):
    return [
        ("part", pltpu.VMEM((d.sp_n, 2, d.half, d.width), BF)),
        ("near", pltpu.VMEM((d.x_n, 2, d.half, d.width), BF)),
        ("far", pltpu.VMEM((d.x_n, 2, d.half, d.width), BF)),
        ("ag_send", pltpu.SemaphoreType.DMA((2, d.sp_n, 2))),
        ("ag_recv", pltpu.SemaphoreType.DMA((d.sp_n, 2))),
        ("near_send", pltpu.SemaphoreType.DMA((d.x_n, 2))),
        ("near_recv", pltpu.SemaphoreType.DMA((d.x_n, 2))),
        ("far_send", pltpu.SemaphoreType.DMA((d.x_n, 2))),
        ("far_recv", pltpu.SemaphoreType.DMA((d.x_n, 2))),
    ]


def term_scratch(d, l, term):
    w, first, last = d.terms[term]
    block = (last - first,) + d.block_shape(w)[1:]
    z_first = term in d.z_first[l]
    y_shape = (max(1, d.y_n - 1), 1 if z_first else d.z_n) + block
    z_shape = (5, d.y_n if z_first else 1) + block
    return [
        ("y_in_%d_%d" % (l, term), pltpu.VMEM(y_shape, BF)),
        ("z_in_%d_%d" % (l, term), pltpu.VMEM(z_shape, BF)),
    ]


SAVED = XIN, PROJ, ATT, PROBS, XMID, HID, SLOPE, STREAM, MID = (
    "xin",
    "qkv",
    "att",
    "probs",
    "xmid",
    "hid",
    "slope",
    "stream",
    "mid",
)
ONCE = (PROJ, ATT, PROBS, HID, SLOPE)
WEIGHTS = W_QKV, W_OUT, W_UP, W_DOWN = ("wqkv", "wout", "wup", "wdown")


def saved_shapes(d):
    full = (d.sp_n, 2, d.half)
    return {
        XIN: (full + (d.width,), BF),
        PROJ: (full + (3 * d.dh,), BF),
        ATT: (full + (d.dh,), BF),
        PROBS: ((d.heads, len(d.pairs), d.tok, d.tok), BF),
        XMID: (full + (d.width,), BF),
        HID: (full + (d.hid,), BF),
        SLOPE: (full + (d.hid,), BF),
        STREAM: ((2, d.half, d.width), F32),
        MID: ((2, d.half, d.width), F32),
    }


def weight_shapes(d):
    return {name: ((d.z_n, d.y_n) + d.block_shape(i), BF) for i, name in enumerate(WEIGHTS)}


class Fetch:
    def __init__(self, p, o):
        self.p, self.o = p, o
        self.full = (o.wqkv, o.wout, o.wup, o.wdown)

    def spread(self, l, w):
        p, o = self.p, self.o
        own = self.full[w].at[l, p.z, p.y]
        if w in (QKV, UP):
            src = o.in_qkv if w == QKV else o.in_up
            for t in range(1, p.d.sp_n):
                j = p.slot(t)
                rcopy(src.at[l, j], own.at[p.s], o.s_send.at[l, w, j], o.s_recv.at[l, w, p.s], (p.r, j)).start()
            pltpu.make_async_copy(src.at[l, p.s], own.at[p.s], o.own_sem.at[l, w]).start()
        elif w == DOWN:
            pltpu.make_async_copy(o.in_down.at[l], own, o.own_sem.at[l, w]).start()
        else:
            goal, _, stays = p.moved()

            @pl.when(stays)
            def _():
                pltpu.make_async_copy(o.in_out.at[l], own, o.own_sem.at[l, w]).start()

            @pl.when(jnp.logical_not(stays))
            def _():
                there = self.full[w].at[l, goal[0] // p.d.y_n, goal[0] % p.d.y_n]
                rcopy(o.in_out.at[l], there, o.s_send.at[l, w, 0], o.s_recv.at[l, w, 0], goal).start()

    def own(self, l, w):
        p, o = self.p, self.o
        own = self.full[w].at[l, p.z, p.y]
        if w in (QKV, UP):
            src = o.in_qkv if w == QKV else o.in_up
            pltpu.make_async_copy(src.at[l, p.s], own.at[p.s], o.own_sem.at[l, w]).wait()
            for t in range(1, p.d.sp_n):
                j = p.slot(t)
                rcopy(src.at[l, j], own.at[j], o.s_send.at[l, w, j], o.s_recv.at[l, w, j], (p.r, j)).wait_recv()
        elif w == DOWN:
            pltpu.make_async_copy(o.in_down.at[l], own, o.own_sem.at[l, w]).wait()
        else:
            goal, _, stays = p.moved()

            @pl.when(stays)
            def _():
                pltpu.make_async_copy(o.in_out.at[l], own, o.own_sem.at[l, w]).wait()

            @pl.when(jnp.logical_not(stays))
            def _():
                rcopy(o.in_out.at[l], own, o.s_send.at[l, w, 0], o.s_recv.at[l, w, 0], goal).wait_recv()

    def block(self, l, piece, z, y):
        w, first, last, _ = self.p.d.pieces[piece]
        return self.full[w].at[l, z, y, first:last]

    def columns(self, piece):
        p = self.p
        if self.p.d.pieces[piece][3]:
            return [p.y] + [p.ypeer(m) for m in range(1, p.d.y_n)]
        return [p.y]

    def copy(self, l, piece, z, y, way, device):
        o = self.o
        block = self.block(l, piece, z, y)
        return rcopy(block, block, o.b_send.at[l, piece, z, y, way], o.b_recv.at[l, piece, z, y], device)

    def arrived(self, l, piece, z, y):
        self.copy(l, piece, z, y, 0, (self.p.r, self.p.s)).wait_recv()

    def along_z(self, l, piece, role, y, act):
        p = self.p
        if p.d.z_n == 1 or role == 3:
            return
        inside, at = p.line()
        z = at[role]

        @pl.when(inside)
        def _():
            for way, goal in enumerate(((at[1], at[2]), (at[2], at[3]), (at[1],))[role]):
                act(self.copy(l, piece, z, y, way, p.dev(goal, p.y)))

        if role == 0:

            @pl.when(jnp.logical_not(inside))
            def _():
                act(self.copy(l, piece, z, y, 0, p.dev(at[1], p.y)))

    def along_y(self, l, piece, role, act):
        p = self.p
        z = p.line()[1][role]
        for m in range(1, p.d.y_n):
            act(self.copy(l, piece, z, p.y, 1 + m, p.dev(p.z, p.ypeer(m))))

    def start_z(self, l, *pieces):
        for piece in pieces:
            self.along_z(l, piece, 0, self.p.y, lambda c: c.start())

    def start_y(self, l, *pieces):
        for piece in pieces:
            self.along_y(l, piece, 0, lambda c: c.start())

    def inner(self, l, *pieces):
        if self.p.d.z_n > 1:

            @pl.when(self.p.line()[0])
            def _():
                for piece in pieces:
                    self.relay(l, piece, 2)

    def outer(self, l, *pieces):
        if self.p.d.z_n > 1:

            @pl.when(jnp.logical_not(self.p.line()[0]))
            def _():
                for piece in pieces:
                    self.relay(l, piece, 2)

    def relay(self, l, piece, *roles):
        p = self.p
        cross_first = p.d.pieces[piece][3]
        at = p.line()[1]
        for role in roles:
            if role == 1 and cross_first:
                for y in self.columns(piece)[1:]:
                    self.arrived(l, piece, p.z, y)
                    self.along_z(l, piece, 0, y, lambda c: c.start())
            if p.d.z_n == 1:
                continue
            for y in self.columns(piece):
                self.arrived(l, piece, at[role], y)
                self.along_z(l, piece, role, y, lambda c: c.start())
            if not cross_first:
                self.along_y(l, piece, role, lambda c: c.start())

    def ready(self, l, *pieces):
        p = self.p
        for piece in pieces:
            if not p.d.pieces[piece][3]:
                for role in range(4 if p.d.z_n > 1 else 1):
                    for m in range(1, p.d.y_n):
                        self.arrived(l, piece, p.line()[1][role], p.ypeer(m))

    def save(self, l, w):
        return pltpu.make_async_copy(self.full[w].at[l], self.o.w_save[w].at[l], self.o.w_sem.at[l, w])

    def end(self):
        p, o = self.p, self.o
        for l in range(p.d.layers):
            for w in range(4):
                own = self.full[w].at[l, p.z, p.y]
                if w in (QKV, UP):
                    src = o.in_qkv if w == QKV else o.in_up
                    for t in range(1, p.d.sp_n):
                        j = p.slot(t)
                        rcopy(src.at[l, j], own.at[p.s], o.s_send.at[l, w, j], o.s_recv.at[l, w, p.s], (p.r, j)).wait_send()
                elif w == OUT:
                    goal, _, stays = p.moved()

                    @pl.when(jnp.logical_not(stays))
                    def _():
                        rcopy(o.in_out.at[l], own, o.s_send.at[l, w, 0], o.s_recv.at[l, w, 0], goal).wait_send()

                self.save(l, w).wait()
            for piece in range(len(p.d.pieces)):
                for role in range(4 if p.d.z_n > 1 else 1):
                    for y in self.columns(piece):
                        self.along_z(l, piece, role, y, lambda c: c.wait_send())
                    if role == 0 or not p.d.pieces[piece][3]:
                        self.along_y(l, piece, role, lambda c: c.wait_send())


class Refs:
    pass


def mean_of(v):
    return jnp.mean(v, axis=-1, keepdims=True)


def norm_rows(v, gain):
    center = v - mean_of(v)
    return center * lax.rsqrt(mean_of(center * center) + EPS) * gain


def row_loop(tok, body, step=32):
    step = min(step, tok)

    @pl.loop(0, tok // step, unroll=True)
    def _(i):
        body(pl.ds(pl.multiple_of(i * step, step), step))


def lay_out(d, o):
    for i in range(d.sp_n):
        where = jnp.int32(0)
        for j in range(1, d.sp_n):
            where = jnp.where(o.in_order[0, j] == i, j, where)
        o.meta[0, i] = where
        o.meta[1, i] = o.in_order[0, i]
    start = jnp.int32(0)
    for b in range(d.docs):
        o.meta[2, b] = start
        start = start + o.in_lengths[0, b]


def up_columns(d, j, k):
    first = (k * d.sp_n + j) * d.hid_own
    return slice(first, first + d.hid_own), slice(k * d.hid_own, (k + 1) * d.hid_own)


def attention_forward(d, o, l):
    tok = d.tok
    slopes = []
    for h in range(d.heads):
        head = (lax.axis_index(AXES[1]) * d.heads + (h + 1)).astype(F32)
        slopes.append(jnp.exp2(jnp.full((1, 1), -8.0 / HEADS, F32) * head))
    for i in range(d.sp_n):
        here = o.meta[0, i]
        pos = i * tok + lax.broadcasted_iota(jnp.int32, (tok, 1), 0)
        start = jnp.zeros((tok, 1), jnp.int32)
        for b in range(1, d.docs):
            start = jnp.where(pos >= o.meta[2, b], o.meta[2, b], start)
        blocks = range(max(0, i - d.back), i + 1)
        for h in range(d.heads):
            lanes = slice(h * HD, (h + 1) * HD)
            query = o.qkv[0, here, :, :, lanes].reshape(tok, HD)
            scores = []
            for b in blocks:
                keys = o.qkv[0, o.meta[0, b], :, :, d.dh + h * HD : d.dh + (h + 1) * HD].reshape(tok, HD)
                key_pos = b * tok + lax.broadcasted_iota(jnp.int32, (tok, tok), 1)
                query_pos = i * tok + lax.broadcasted_iota(jnp.int32, (tok, tok), 0)
                score = nt(query, keys) * HD ** (-0.5) + slopes[h] * (key_pos - query_pos).astype(F32)
                allowed = key_pos >= start
                if b == i:
                    allowed = allowed & (key_pos <= query_pos)
                scores.append(jnp.where(allowed, score, MASKED))
            top = scores[0].max(axis=-1, keepdims=True)
            for score in scores[1:]:
                top = jnp.maximum(top, score.max(axis=-1, keepdims=True))
            expo = [jnp.exp(score - top) for score in scores]
            total = expo[0].sum(axis=-1, keepdims=True)
            for part in expo[1:]:
                total = total + part.sum(axis=-1, keepdims=True)
            inverse = 1.0 / total
            result = None
            for b, part in zip(blocks, expo):
                low = (part * inverse).astype(BF)
                o.probs[0, h, d.pairs.index((i, b))] = low
                values = o.qkv[0, o.meta[0, b], :, :, 2 * d.dh + h * HD : 2 * d.dh + (h + 1) * HD].reshape(tok, HD)
                term = nn(low, values)
                result = term if result is None else result + term
            o.sorted_att[i, :, :, lanes] = result.astype(BF).reshape(2, d.half, HD)


def fwd_kernel(d, names, *refs):
    o = Refs()
    for name, ref in zip(names, refs):
        setattr(o, name, ref)
    o.w_save = (o.o_wqkv, o.o_wout, o.o_wup, o.o_wdown)
    p = Place(d)
    fetch = Fetch(p, o)
    gather = Gather(p, o.ag_send, o.ag_recv)
    scatter = Scatter(p, o.part, o.near, o.far, o.near_send, o.near_recv, o.far_send, o.far_recv)
    small = SmallSum(p, o.in_gains, o.sp_in, o.mid_a, o.z_in, o.mid_b, o.y_in, o.sp_sem, o.z_sem, o.y_sem)

    def save(name, l):
        ref, out = getattr(o, name), getattr(o, "o_" + name)
        held = 0 if name in ONCE else l
        return pltpu.make_async_copy(ref.at[held], out.at[l], o.save_sem.at[l, SAVED.index(name)])

    def free(l, *names):
        if l > 0:
            for name in names:
                save(name, l - 1).wait()

    late = Gather(p, o.late_send, o.late_recv)
    keep_gl = pltpu.make_async_copy(o.gl, o.o_gl, o.late_sem.at[0])

    def run(slot):
        for op, l, piece in FORWARD_PLAN.get(slot, ()):
            if op == LATE_START:
                o.gl[p.s, piece] = o.in_cotangent[piece]
                late.start(o.gl, piece)
            elif op == LATE_ON:
                for step in range(2 + piece, d.sp_n, 2):
                    late.through(o.gl, step)
            elif op == LATE_END:
                late.rest(o.gl)
                keep_gl.start()
            elif op == RELAY_1:
                fetch.relay(l, piece, 1)
            elif op == RELAY_3:
                fetch.relay(l, piece, 3)
            else:
                act = {
                    SPREAD: fetch.spread,
                    OWN: fetch.own,
                    START_Z: fetch.start_z,
                    START_Y: fetch.start_y,
                    INNER: fetch.inner,
                    OUTER: fetch.outer,
                }[op]
                act(l, piece)

    def place(l):
        if d.whole_lanes:
            for j in range(d.sp_n):
                for i in range(3):
                    o.in_qkv[l, j, :, i * d.dh : (i + 1) * d.dh] = o.raw_qkv[l, i, :, j * d.dh : (j + 1) * d.dh]
                for k in range(d.dp_n):
                    whole, kept = up_columns(d, j, k)
                    o.in_up[l, j, :, kept] = o.raw_up[l, :, whole]

    place(0)
    p.barrier()
    for w in (QKV, OUT):
        fetch.spread(0, w)
    small.start(0)
    for l in range(1, d.layers):
        place(l)
    lay_out(d, o)
    for w in (UP, DOWN):
        fetch.spread(0, w)
    run(0)
    small.finish(0, o.mid_a)
    small.start(1)
    run(1)
    small.finish(1, o.mid_b)
    small.start(2)
    run(2)
    small.finish(2, o.o_gains)

    def norm_in(l, half, gain):
        def first(rows):
            v = o.in_tokens[half, rows].astype(F32)
            o.stream[0, half, rows] = v
            o.xin[0, p.s, half, rows] = norm_rows(v, gain).astype(BF)

        row_loop(d.half, first)

    for half in range(2):
        norm_in(0, half, o.o_gains[0:1, :])
        gather.start(o.xin.at[0], half)

    top = d.layers - 1
    for l in range(d.layers):
        gain_mid = o.o_gains[2 * l + 1 : 2 * l + 2, :]
        xin, xmid = o.xin.at[l], o.xmid.at[l]
        save(STREAM, l).start()
        run(3 + 10 * l)
        fetch.ready(l, 0)
        fetch.save(l, QKV).start()
        free(l, PROJ)
        third = 3 * d.dh // 3

        def project(pieces):
            block = pair(xin, pieces)
            for n in range(3):
                cols = slice(n * third, (n + 1) * third)
                weight = o.wqkv[l, :, :, :, :, cols].reshape(d.width, third)
                put_pair(o.qkv.at[0], pieces, cols, nn(block, weight))

        project(p.pieces(0))
        gather.near(xin)
        project(p.pieces(1))
        run(4 + 10 * l)

        @pl.loop(2, d.sp_n, unroll=True)
        def _(t):
            gather.far(xin, t)
            project(p.pieces(t))

        gather.end(xin)
        save(XIN, l).start()
        save(PROJ, l).start()
        run(5 + 10 * l)
        free(l, PROBS, ATT)
        attention_forward(d, o, l)
        save(PROBS, l).start()
        run(6 + 10 * l)
        fetch.ready(l, 1)
        fetch.save(l, OUT).start()

        def out_part(pieces):
            blocks = []
            for slot, half in pieces:
                block = o.sorted_att[o.meta[1, slot], half]
                o.att[0, slot, half] = block
                blocks.append(block)
            block = jnp.concatenate(blocks, axis=0)
            for n in range(d.n_width):
                cols = slice(n * d.chunk, (n + 1) * d.chunk)
                weight = o.wout[l, :, :, :, cols].reshape(d.dh, d.chunk)
                put_pair(o.part, pieces, cols, nn(block, weight))

        @pl.loop(2, d.sp_n, unroll=True)
        def _(t):
            out_part(p.pieces(t))
            scatter.put(t)

            @pl.when(t > 2)
            def _():
                scatter.cross(t - 1)

        out_part(p.pieces(1))
        scatter.put(1)
        scatter.cross(d.sp_n - 1)
        out_part(p.pieces(0))
        save(ATT, l).start()
        run(7 + 10 * l)

        def middle(half, rows):
            v = o.stream[l, half, rows] + scatter.total(half, rows)
            o.mid[l, half, rows] = v
            xmid[p.s, half, rows] = norm_rows(v, gain_mid).astype(BF)

        for half in range(2):
            scatter.arrive(half)
            row_loop(d.half, functools.partial(middle, half))
            gather.start(xmid, half)
            if half == 0:
                run(8 + 10 * l)
        scatter.end()
        save(MID, l).start()
        run(9 + 10 * l)
        fetch.ready(l, 2, 3)
        fetch.save(l, UP).start()
        free(l, HID, SLOPE)

        def up(pieces):
            block = pair(xmid, pieces)
            for n in range(d.n_hid):
                cols = slice(n * d.chunk, (n + 1) * d.chunk)
                weight = o.wup[l, :, :, :, :, cols].reshape(d.width, d.chunk)
                pre = nn(block, weight)
                phi = 0.5 * (1.0 + lax.erf(pre * (0.5**0.5)))
                put_pair(o.hid.at[0], pieces, cols, pre * phi)
                density = jnp.exp(-0.5 * pre * pre) * 0.3989422804014327
                put_pair(o.slope.at[0], pieces, cols, phi + pre * density)

        def down(pieces):
            hidden = pair(o.hid.at[0], pieces)
            for n in range(d.n_width):
                cols = slice(n * d.chunk, (n + 1) * d.chunk)
                weight = o.wdown[l, :, :, :, cols].reshape(d.hid, d.chunk)
                put_pair(o.part, pieces, cols, nn(hidden, weight))

        up(p.pieces(0))
        gather.near(xmid)
        up(p.pieces(1))
        run(10 + 10 * l)
        if l == 0:

            @pl.loop(2, d.sp_n)
            def _(t):
                gather.far(xmid, t)
                up(p.pieces(t))

        fetch.ready(l, 4, 5)
        fetch.save(l, DOWN).start()

        @pl.loop(2, d.sp_n)
        def _(t):
            if l > 0:
                gather.far(xmid, t)
                up(p.pieces(t))
                if l < top:

                    @pl.when(t > 2)
                    def _():
                        scatter.cross(t - 1)

            down(p.pieces(t))
            if l < top:
                scatter.put(t)
            if l == 0 and l < top:

                @pl.when(t > 2)
                def _():
                    scatter.cross(t - 1)

        down(p.pieces(1))
        if l < top:
            scatter.put(1)
            scatter.cross(d.sp_n - 1)
        down(p.pieces(0))
        gather.end(xmid)
        save(XMID, l).start()
        save(HID, l).start()
        save(SLOPE, l).start()
        if l == top:
            keep_part = pltpu.make_async_copy(o.part, o.o_part, o.late_sem.at[1])
            keep_part.start()
            continue
        run(11 + 10 * l)

        def last(half, rows):
            v = o.mid[l, half, rows] + scatter.total(half, rows)
            o.stream[l + 1, half, rows] = v
            o.xin[l + 1, p.s, half, rows] = norm_rows(v, o.o_gains[2 * l + 2 : 2 * l + 3, :]).astype(BF)

        for half in range(2):
            scatter.arrive(half)
            row_loop(d.half, functools.partial(last, half))
            gather.start(o.xin.at[l + 1], half)
            if half == 0:
                run(12 + 10 * l)
        scatter.end()

    keep_part.wait()
    fetch.end()
    late.end(o.gl)
    keep_gl.wait()
    for l in range(d.layers):
        for name in SAVED:
            if l == d.layers - 1 or name not in ONCE:
                save(name, l).wait()


class Reduce:
    def __init__(self, p, o):
        self.p, self.o = p, o
        self.grads = (o.g_qkv, o.g_out, o.g_up, o.g_down)
        self.sp_in = (o.x_qkv, o.x_out, o.x_up, None)
        self.result = (o.o_qkv, o.o_out, o.o_up, o.o_down)
        self.done = {}

    def grad(self, l, w):
        return self.o.g_up_odd if w == UP and l % 2 else self.grads[w]

    def z_first(self, l, term):
        return term in self.p.d.z_first[l]

    def ins(self, l, term):
        o = self.o
        return getattr(o, "y_in_%d_%d" % (l, term)), getattr(o, "z_in_%d_%d" % (l, term))

    def columns(self, l, term):
        p = self.p
        if self.z_first(l, term):
            return [(y, y) for y in [p.y] + [p.ypeer(m) for m in range(1, p.d.y_n)]]
        return [(p.y, 0)]

    def step(self, l, *terms):
        for term in terms:
            stages = (self.y_send, self.y_sum, self.inner, self.finish_z)
            if self.z_first(l, term):
                stages = (self.z_send, self.inner, self.z_sum, self.finish_y)
            count = self.done.get((l, term), 0)
            self.done[l, term] = count + 1
            stages[count](l, term)

    def groups(self, term):
        w, first, last = self.p.d.terms[term]
        if w in (QKV, UP):
            return [((j,), (j - first,)) for j in range(first, last)]
        rows = min(32, last - first)
        return [
            ((slice(j, j + rows),), (slice(j - first, j - first + rows),)) for j in range(first, last, rows)
        ]

    def y_copy(self, l, term, k):
        p, o = self.p, self.o
        w, first, last = p.d.terms[term]
        index = p.d.y_n - k - 1
        there = p.ypeer(k)
        into = self.ins(l, term)[0].at[index]
        if self.z_first(l, term):
            src, into = self.grad(l, w).at[p.z, there, first:last], into.at[0]
        else:
            src = self.grad(l, w).at[:, there, first:last]
        return rcopy(src, into, o.ry_send.at[l, term, k], o.ry_recv.at[l, term, index], p.dev(p.z, there))

    def y_send(self, l, term):
        for k in range(1, self.p.d.y_n):
            self.y_copy(l, term, k).start()

    def y_wait(self, l, term):
        for k in range(1, self.p.d.y_n):
            self.y_copy(l, term, self.p.d.y_n - k).wait_recv()

    def y_sum(self, l, term):
        p = self.p
        w = p.d.terms[term][0]
        y_in, _ = self.ins(l, term)
        self.y_wait(l, term)
        for z in range(p.d.z_n):
            for index, here in self.groups(term):
                value = self.grad(l, w)[(z, p.y) + index].astype(F32)
                for m in range(p.d.y_n - 1):
                    value = value + y_in[(m, z) + here].astype(F32)
                self.grad(l, w)[(z, p.y) + index] = value.astype(BF)
        self.z_send(l, term)

    def z_copy(self, l, term, column, z, goal, place, way):
        p, o = self.p, self.o
        w, first, last = p.d.terms[term]
        y, slot = column
        return rcopy(
            self.grad(l, w).at[z, y, first:last],
            self.ins(l, term)[1].at[place, slot],
            o.rz_send.at[l, term, slot, way],
            o.rz_recv.at[l, term, slot, place],
            p.dev(goal, p.y),
        )

    def z_goals(self, inside):
        at = self.p.line()[1]
        if inside:
            return ((at[3], at[2], 3), (at[2], at[2], 1), (at[1], at[1], 0))
        return ((at[1], at[1], 0), (at[2], at[1], 2), (at[3], at[2], 4))

    def both(self, inner, outer):
        inside, _ = self.p.line()
        pl.when(inside)(inner)
        pl.when(jnp.logical_not(inside))(outer)

    def z_send(self, l, term):
        if self.p.d.z_n == 1:
            return

        def send(inside, ways):
            for column in self.columns(l, term):
                for way in ways:
                    self.z_copy(l, term, column, *self.z_goals(inside)[way], way).start()

        self.both(lambda: send(True, (0,)), lambda: send(False, (0, 1, 2)))

    def z_wait(self, l, term, column, place):
        self.z_copy(l, term, column, self.p.z, self.p.z, place, 0).wait_recv()

    def inner(self, l, term):
        p = self.p
        if p.d.z_n == 1:
            return
        w = p.d.terms[term][0]
        _, z_in = self.ins(l, term)

        def relay():
            for way, places in ((1, (2,)), (2, (3, 4))):
                z, goal, place = self.z_goals(True)[way]
                for column in self.columns(l, term):
                    y, slot = column
                    for source in places:
                        self.z_wait(l, term, column, source)
                    for index, here in self.groups(term):
                        value = self.grad(l, w)[(z, y) + index].astype(F32)
                        for source in places:
                            value = value + z_in[(source, slot) + here].astype(F32)
                        self.grad(l, w)[(z, y) + index] = value.astype(BF)
                    self.z_copy(l, term, column, z, goal, place, way).start()

        pl.when(p.line()[0])(relay)

    def z_total(self, l, term, column, store):
        p = self.p
        w = p.d.terms[term][0]
        _, z_in = self.ins(l, term)
        y, slot = column

        def total(places):
            for source in places:
                self.z_wait(l, term, column, source)
            for index, here in self.groups(term):
                value = self.grad(l, w)[(p.z, y) + index].astype(F32)
                for source in places:
                    value = value + z_in[(source, slot) + here].astype(F32)
                store(y, index, here, value)

        if p.d.z_n == 1:
            total(())
        else:
            self.both(lambda: total((0, 1)), lambda: total((0,)))

    def z_sum(self, l, term):
        w = self.p.d.terms[term][0]

        def store(y, index, here, value):
            self.grad(l, w)[(self.p.z, y) + index] = value.astype(BF)

        for column in self.columns(l, term):
            self.z_total(l, term, column, store)
        self.y_send(l, term)

    def finish_z(self, l, term):
        def store(y, index, here, value):
            self.settle(l, term, index, value)

        self.z_total(l, term, self.columns(l, term)[0], store)
        self.pass_on(l, term)

    def finish_y(self, l, term):
        p = self.p
        w = p.d.terms[term][0]
        y_in, _ = self.ins(l, term)
        self.y_wait(l, term)
        for index, here in self.groups(term):
            value = self.grad(l, w)[(p.z, p.y) + index].astype(F32)
            for m in range(p.d.y_n - 1):
                value = value + y_in[(m, 0) + here].astype(F32)
            self.settle(l, term, index, value)
        self.pass_on(l, term)

    def settle(self, l, term, index, value):
        w = self.p.d.terms[term][0]
        if w == DOWN:
            self.result[w][(l,) + index] = value.astype(BF)
        else:
            self.grad(l, w)[(self.p.z, self.p.y) + index] = value.astype(BF)

    def s_copy(self, l, w, j, source):
        p, o = self.p, self.o
        return rcopy(
            self.grad(l, w).at[p.z, p.y, j], self.sp_in[w].at[l, source], o.rs_send.at[l, w, j], o.rs_recv.at[l, w, source], (p.r, j)
        )

    def out_copy(self, l, device):
        p, o = self.p, self.o
        return rcopy(
            self.grad(l, OUT).at[p.z, p.y], self.sp_in[OUT].at[l], o.rs_send.at[l, OUT, 0], o.rs_recv.at[l, OUT, 0], device
        )

    def keep(self, l, w, j, ref):
        d, result = self.p.d, self.result[w]
        if not d.whole_lanes:
            result[l, j] = ref[...]
        elif w == QKV:
            for i in range(3):
                result[l, i, :, j * d.dh : (j + 1) * d.dh] = ref[:, i * d.dh : (i + 1) * d.dh]
        else:
            for k in range(d.dp_n):
                whole, kept = up_columns(d, j, k)
                result[l, :, whole] = ref[:, kept]

    def pass_on(self, l, term):
        p = self.p
        w, first, last = p.d.terms[term]
        if w in (QKV, UP):
            for j in range(first, last):

                @pl.when(p.s == j)
                def _():
                    self.keep(l, w, j, self.grad(l, w).at[p.z, p.y, j])

                @pl.when(p.s != j)
                def _():
                    self.s_copy(l, w, j, p.s).start()

        elif w == OUT:
            _, source, stays = p.moved()

            @pl.when(stays)
            def _():
                self.result[w][l] = self.grad(l, w)[p.z, p.y]

            @pl.when(jnp.logical_not(stays))
            def _():
                self.out_copy(l, source).start()

    def sent(self, l, w):
        p = self.p
        for term, (kind, first, last) in enumerate(p.d.terms):
            if kind != w:
                continue
            for k in range(1, p.d.y_n):
                self.y_copy(l, term, k).wait_send()
            if p.d.z_n > 1:

                def wait(inside):
                    for column in self.columns(l, term):
                        for way in range(3):
                            self.z_copy(l, term, column, *self.z_goals(inside)[way], way).wait_send()

                self.both(lambda: wait(True), lambda: wait(False))
        if w in (QKV, UP):
            for t in range(1, p.d.sp_n):
                self.s_copy(l, w, p.slot(t), p.s).wait_send()
        elif w == OUT:
            _, source, stays = p.moved()

            @pl.when(jnp.logical_not(stays))
            def _():
                self.out_copy(l, source).wait_send()

    def last(self, l, w):
        p = self.p
        if w in (QKV, UP):
            for j in range(p.d.sp_n):

                @pl.when(p.s != j)
                def _():
                    self.s_copy(l, w, j, j).wait_recv()
                    self.keep(l, w, j, self.sp_in[w].at[l, j])
        elif w == OUT:
            _, source, stays = p.moved()

            @pl.when(jnp.logical_not(stays))
            def _():
                self.out_copy(l, source).wait_recv()
                self.result[w][l] = self.sp_in[w][l]


def norm_back(v, d_out, gain):
    center = v - mean_of(v)
    inverse = lax.rsqrt(mean_of(center * center) + EPS)
    unit = center * inverse
    gain_term = jnp.sum(d_out * unit, axis=0, keepdims=True)
    e = d_out * gain
    back = (e - mean_of(e) - unit * mean_of(e * unit)) * inverse
    return back, gain_term


def attention_backward(d, o):
    tok = d.tok
    for i in range(d.sp_n):
        here = o.meta[0, i]
        blocks = range(max(0, i - d.back), i + 1)
        for h in range(d.heads):
            lanes = slice(h * HD, (h + 1) * HD)
            key_lanes = slice(d.dh + h * HD, d.dh + (h + 1) * HD)
            value_lanes = slice(2 * d.dh + h * HD, 2 * d.dh + (h + 1) * HD)
            query = o.qkv[here, :, :, lanes].reshape(tok, HD)
            grad = o.d_att[here, :, :, lanes].reshape(tok, HD)
            d_probs, inner = [], None
            for b in blocks:
                low = o.probs[h, d.pairs.index((i, b))].astype(F32)
                term = nt(grad, o.qkv[o.meta[0, b], :, :, value_lanes].reshape(tok, HD))
                d_probs.append(term)
                weighted = jnp.sum(low * term, axis=-1, keepdims=True)
                inner = weighted if inner is None else inner + weighted
            d_query = None
            for b, term in zip(blocks, d_probs):
                low = o.probs[h, d.pairs.index((i, b))]
                d_score = (low.astype(F32) * (term - inner)).astype(BF)
                step = nn(d_score, o.qkv[o.meta[0, b], :, :, key_lanes].reshape(tok, HD))
                d_query = step if d_query is None else d_query + step
                d_key, d_value = tn(d_score, query), tn(low, grad)
                if b == i:
                    o.d_keys[b, :, lanes] = d_key
                    o.d_values[b, :, lanes] = d_value
                else:
                    o.d_keys[b, :, lanes] += d_key
                    o.d_values[b, :, lanes] += d_value
            o.sorted_dqkv[i, :, :, lanes] = (d_query * HD ** (-0.5)).astype(BF).reshape(2, d.half, HD)
    for b in range(d.sp_n):
        shape = (2, d.half, d.dh)
        o.sorted_dqkv[b, :, :, d.dh : 2 * d.dh] = (o.d_keys[b] * HD ** (-0.5)).astype(BF).reshape(shape)
        o.sorted_dqkv[b, :, :, 2 * d.dh :] = o.d_values[b].astype(BF).reshape(shape)


def bwd_kernel(d, names, *refs):
    o = Refs()
    for name, ref in zip(names, refs):
        setattr(o, name, ref)
    p = Place(d)
    gather = Gather(p, o.ag_send, o.ag_recv)
    scatter = Scatter(p, o.part, o.near, o.far, o.near_send, o.near_recv, o.far_send, o.far_recv)
    small = SmallSum(p, o.gain_sum, o.sp_in, o.mid_a, o.z_in, o.mid_b, o.y_in, o.sp_sem, o.z_sem, o.y_sem)
    reduce = Reduce(p, o)
    loads = WEIGHTS + SAVED

    def load(name, l):
        ref = o.mid if name == STREAM else getattr(o, name)
        return pltpu.make_async_copy(getattr(o, "i_" + name).at[l], ref, o.load_sem.at[loads.index(name)])

    def refill(l, *which):
        if l > 0:
            for name in which:
                load(name, l - 1).start()

    def run(slot):
        for layer, term in BACKWARD_PLAN.get(slot, ()):
            reduce.step(layer, term)

    top = d.layers - 1
    first_grad = pltpu.make_async_copy(o.i_gl, o.gl, o.late_sem.at[0])
    first_grad.start()
    for name in (W_DOWN, SLOPE, W_UP, HID, XMID, MID, W_OUT, PROJ, PROBS, ATT, W_QKV, XIN):
        load(name, top).start()
    p.barrier()
    lay_out(d, o)
    o.gain_sum[...] = jnp.zeros_like(o.gain_sum)

    first_grad.wait()
    for half in range(2):

        def begin(rows):
            o.o_grad[half, rows] = o.gl[p.s, half, rows].astype(F32)

        row_loop(d.half, begin)
    tokens = d.sp_n * d.tok

    def rows_of(ref, n, count):
        part = ref[n * d.z_n // count : (n + 1) * d.z_n // count]
        return part.reshape(d.chunk, part.shape[-1])

    def weight_grad(out, left_ref, right_ref, count, width):
        for n in range(count):
            left = left_ref[:, :, :, n * d.chunk : (n + 1) * d.chunk].reshape(tokens, d.chunk)
            value = tn(left, right_ref[...].reshape(tokens, width)).astype(BF)
            zs = slice(n * d.z_n // count, (n + 1) * d.z_n // count)
            out[zs] = value.reshape((d.z_n // count,) + out.shape[1:])

    for l in reversed(range(d.layers)):
        gain_in = o.in_gains[2 * l : 2 * l + 1, :]
        gain_mid = o.in_gains[2 * l + 1 : 2 * l + 2, :]
        run(0 + 14 * (top - l))
        load(W_DOWN, l).wait()
        load(SLOPE, l).wait()
        load(W_UP, l).wait()

        def pre_grad(pieces):
            block = pair(o.gl, pieces)
            for n in range(d.n_hid):
                cols = slice(n * d.chunk, (n + 1) * d.chunk)
                d_hidden = nt(block, rows_of(o.wdown, n, d.n_hid))
                put_pair(o.slope, pieces, cols, d_hidden * pair(o.slope, pieces, cols).astype(F32))

        def mid_grad(pieces):
            d_pre = pair(o.slope, pieces)
            for n in range(d.n_width):
                cols = slice(n * d.chunk, (n + 1) * d.chunk)
                put_pair(o.part, pieces, cols, nt(d_pre, rows_of(o.wup, n, d.n_width)))

        if l < top:
            pre_grad(p.pieces(0))
            gather.near(o.gl)
            pre_grad(p.pieces(1))
        run(1 + 14 * (top - l))

        @pl.loop(2, d.sp_n)
        def _(t):
            if l < top:
                gather.far(o.gl, t)
            pre_grad(p.pieces(t))

            @pl.when(t > 2)
            def _():
                scatter.cross(t - 1)

            mid_grad(p.pieces(t))
            scatter.put(t)

        if l == top:
            pre_grad(p.pieces(1))
        mid_grad(p.pieces(1))
        scatter.put(1)
        scatter.cross(d.sp_n - 1)
        if l == top:
            pre_grad(p.pieces(0))
        mid_grad(p.pieces(0))
        if l < top:
            gather.end(o.gl)
        refill(l, W_DOWN, W_UP)
        load(HID, l).wait()
        run(2 + 14 * (top - l))
        if l < top:
            reduce.sent(l + 1, DOWN)
        weight_grad(o.g_down, o.hid, o.gl, d.n_hid, d.width)
        run(3 + 14 * (top - l))
        refill(l, HID)
        load(MID, l).wait()

        def middle(half, rows):
            back, gain_term = norm_back(o.mid[half, rows], scatter.total(half, rows), gain_mid)
            o.gain_sum[2 * l + 1 : 2 * l + 2, :] += gain_term
            value = o.o_grad[half, rows] + back
            o.o_grad[half, rows] = value
            o.ml[p.s, half, rows] = value.astype(BF)

        for half in range(2):
            scatter.arrive(half)
            row_loop(d.half, functools.partial(middle, half))
            gather.start(o.ml, half)
            if half == 0:
                run(4 + 14 * (top - l))
        scatter.end()
        load(STREAM, l).start()
        load(XMID, l).wait()
        run(5 + 14 * (top - l))
        if l + 2 <= top:
            reduce.sent(l + 2, UP)
        weight_grad(reduce.grad(l, UP), o.xmid, o.slope, d.n_width, d.hid)
        run(6 + 14 * (top - l))
        refill(l, XMID, SLOPE)
        load(W_OUT, l).wait()

        def att_grad(pieces):
            weight = o.wout[...].reshape(d.dh, d.width)
            put_pair(o.d_att, pieces, slice(None), nt(pair(o.ml, pieces), weight))

        att_grad(p.pieces(0))
        gather.near(o.ml)
        att_grad(p.pieces(1))
        run(7 + 14 * (top - l))

        @pl.loop(2, d.sp_n, unroll=True)
        def _(t):
            gather.far(o.ml, t)
            att_grad(p.pieces(t))

        gather.end(o.ml)
        refill(l, W_OUT)
        run(8 + 14 * (top - l))
        load(PROJ, l).wait()
        load(PROBS, l).wait()
        attention_backward(d, o)
        refill(l, PROJ, PROBS)
        run(9 + 14 * (top - l))
        load(W_QKV, l).wait()

        def in_grad(pieces):
            blocks = []
            for slot, half in pieces:
                block = o.sorted_dqkv[o.meta[1, slot], half]
                o.d_qkv[slot, half] = block
                blocks.append(block)
            block = jnp.concatenate(blocks, axis=0)
            for n in range(d.n_width):
                cols = slice(n * d.chunk, (n + 1) * d.chunk)
                put_pair(o.part, pieces, cols, nt(block, rows_of(o.wqkv, n, d.n_width)))

        @pl.loop(2, d.sp_n, unroll=True)
        def _(t):
            in_grad(p.pieces(t))
            scatter.put(t)

            @pl.when(t > 2)
            def _():
                scatter.cross(t - 1)

        in_grad(p.pieces(1))
        scatter.put(1)
        scatter.cross(d.sp_n - 1)
        in_grad(p.pieces(0))
        run(10 + 14 * (top - l))
        refill(l, W_QKV)
        load(ATT, l).wait()
        if l < top:
            reduce.sent(l + 1, OUT)
        value = tn(o.att[...].reshape(tokens, d.dh), o.ml[...].reshape(tokens, d.width)).astype(BF)
        o.g_out[...] = value.reshape((d.z_n, d.y_n, d.rows, d.width))
        run(11 + 14 * (top - l))
        refill(l, ATT)
        load(XIN, l).wait()
        if l < top:
            reduce.sent(l + 1, QKV)
        weight_grad(o.g_qkv, o.xin, o.d_qkv, d.n_width, 3 * d.dh)
        run(12 + 14 * (top - l))
        refill(l, XIN)
        load(STREAM, l).wait()

        def lower(half, rows):
            back, gain_term = norm_back(o.mid[half, rows], scatter.total(half, rows), gain_in)
            o.gain_sum[2 * l : 2 * l + 1, :] += gain_term
            value = o.o_grad[half, rows] + back
            o.o_grad[half, rows] = value
            if l > 0:
                o.gl[p.s, half, rows] = value.astype(BF)

        for half in range(2):
            scatter.arrive(half)
            row_loop(d.half, functools.partial(lower, half))
            if l > 0:
                gather.start(o.gl, half)
            if half == 0:
                run(13 + 14 * (top - l))
        scatter.end()
        if l == 0:
            small.start(0)
        refill(l, MID)

    keep_part = pltpu.make_async_copy(o.i_part, o.part, o.late_sem.at[1])
    keep_part.start()
    load(MID, top).start()
    run(28)
    small.finish(0, o.mid_a)
    small.start(1)
    keep_part.wait()
    for t in range(d.sp_n - 1, 1, -1):
        scatter.near_copy(p.slot(t // 2 * 2) // 2, t % 2).start()
    scatter.put(1)
    run(29)
    for t in range(d.sp_n - 1, 1, -1):
        scatter.cross(t)
    run(30)
    small.finish(1, o.mid_b)
    small.start(2)
    run(31)
    load(MID, top).wait()

    def last(half, rows):
        o.o_output[half, rows] = (o.mid[half, rows] + scatter.total(half, rows)).astype(BF)

    for half in range(2):
        scatter.arrive(half)
        row_loop(d.half, functools.partial(last, half))
    scatter.end()
    run(32)
    small.finish(2, o.o_gains)
    for l in reversed(range(d.layers)):
        for w in (DOWN, UP, OUT, QKV):
            reduce.last(l, w)
    for w in (DOWN, UP, OUT, QKV):
        reduce.sent(0, w)
    if top > 0:
        reduce.sent(1, UP)


def finish_kernel(d, names, *refs):
    o = Refs()
    for name, ref in zip(names, refs):
        setattr(o, name, ref)
    arrays = (
        (o.o_qkv, o.a_qkv, o.b_qkv, o.r_qkv),
        (o.o_out, o.a_out, o.b_out, o.r_out),
        (o.o_up, o.a_up, o.b_up, o.r_up),
        (o.o_down, o.a_down, o.b_down, o.r_down),
        (o.o_grad, o.a_grad, o.a_grad, o.r_grad),
        (o.o_output, o.a_output, o.a_output, o.r_output),
    )
    copies = []
    reads = [pltpu.make_async_copy(a[0], a[1], o.in_sem.at[n]) for n, a in enumerate(arrays)]
    for copy in reads:
        copy.start()
    for n, (_, low, full, result) in enumerate(arrays):
        reads[n].wait()
        if full is not low:
            for l in range(d.layers):
                full[l] = low[l].astype(F32)
        copies.append(pltpu.make_async_copy(full, result, o.out_sem.at[n]))
        copies[-1].start()
    own = o.r_gains.shape[1]
    flat = lax.axis_index(AXES[0]) * d.sp_n + lax.axis_index(AXES[1])
    mine = jnp.zeros(o.r_gains.shape, F32)
    for k in range(d.width // own):
        mine = jnp.where(flat == k, o.o_gains[: o.r_gains.shape[0], k * own : (k + 1) * own], mine)
    o.r_gains[...] = mine
    for copy in copies:
        copy.wait()


ANY = pl.BlockSpec(memory_space=pl.ANY)
VM = pl.BlockSpec(memory_space=pltpu.VMEM)
SM = pl.BlockSpec(memory_space=pltpu.SMEM)


def call(kernel, d, inputs, outputs, scratch, identity):
    names = [i[0] for i in inputs] + [i[0] for i in outputs] + [i[0] for i in scratch]
    results = pl.pallas_call(
        functools.partial(kernel, d, names),
        out_shape=[jax.ShapeDtypeStruct(i[2], i[3]) for i in outputs],
        in_specs=[i[1] for i in inputs],
        out_specs=[i[1] for i in outputs],
        scratch_shapes=[i[1] for i in scratch],
        compiler_params=pltpu.CompilerParams(
            collective_id=identity, has_side_effects=identity is not None, vmem_limit_bytes=62 * 1024 * 1024
        ),
        name=kernel.__name__,
    )(*[i[2] for i in inputs])
    return dict(zip([i[0] for i in outputs], results))


def shards(dp_n, sp_n, tokens, cotangent, w_qkv, w_out, w_up, w_down, gains, piece_order, doc_lengths):
    _, tok, width = tokens.shape
    layers, _, rows, _ = w_qkv.shape
    ff = w_up.shape[-1]
    d = Dims(dp_n, sp_n, layers, tok, width, ff, doc_lengths.shape[1])
    r, s = lax.axis_index(AXES[0]), lax.axis_index(AXES[1])

    own = gains.shape[-1]
    padded = jnp.zeros((8, width), F32)
    padded = lax.dynamic_update_slice(
        padded, gains.reshape(2 * layers, own).astype(F32), (0, (r * sp_n + s) * own)
    )
    lay_scratch = []
    if d.whole_lanes:
        lay_scratch = [
            ("in_qkv", pltpu.VMEM((layers, sp_n, rows, 3 * d.dh), BF)),
            ("in_up", pltpu.VMEM((layers, sp_n, rows, d.hid), BF)),
        ]
        given = [("raw_qkv", VM, w_qkv), ("raw_up", VM, w_up)]
    else:
        in_qkv = w_qkv.reshape(layers, 3, rows, sp_n, d.dh).transpose(0, 3, 2, 1, 4)
        in_up = w_up.reshape(layers, rows, dp_n, sp_n, d.hid_own).transpose(0, 3, 1, 2, 4)
        given = [
            ("in_qkv", ANY, in_qkv.reshape(layers, sp_n, rows, 3 * d.dh)),
            ("in_up", ANY, in_up.reshape(layers, sp_n, rows, d.hid)),
        ]

    saved, weights = saved_shapes(d), weight_shapes(d)
    dma = pltpu.SemaphoreType.DMA
    fwd = call(
        fwd_kernel,
        d,
        [
            ("in_order", SM, piece_order),
            ("in_lengths", SM, doc_lengths),
            ("in_tokens", VM, tokens.reshape(2, d.half, width)),
            ("in_cotangent", VM, cotangent.reshape(2, d.half, width)),
            ("in_gains", VM, padded),
            ("in_out", ANY, w_out),
            ("in_down", ANY, w_down),
        ]
        + given,
        [("o_gains", VM, (8, width), F32)]
        + [("o_" + n, ANY, (layers,) + weights[n][0], BF) for n in WEIGHTS]
        + [("o_" + n, ANY, (layers,) + saved[n][0], saved[n][1]) for n in SAVED]
        + [("o_gl", ANY, (sp_n, 2, d.half, width), BF), ("o_part", ANY, (sp_n, 2, d.half, width), BF)],
        [(n, pltpu.VMEM((layers,) + weights[n][0], BF)) for n in WEIGHTS]
        + [(n, pltpu.VMEM((1 if n in ONCE else layers,) + saved[n][0], saved[n][1])) for n in SAVED]
        + [
            ("sorted_att", pltpu.VMEM(saved[ATT][0], BF)),
            ("meta", pltpu.SMEM((3, max(sp_n, d.docs)), jnp.int32)),
        ]
        + [
            ("gl", pltpu.VMEM((sp_n, 2, d.half, width), BF)),
            ("late_send", dma((2, sp_n, 2))),
            ("late_recv", dma((sp_n, 2))),
            ("late_sem", dma((2,))),
        ]
        + lay_scratch
        + small_scratch(d)
        + comm_scratch(d)
        + [
            ("s_send", dma((layers, 4, sp_n))),
            ("s_recv", dma((layers, 4, sp_n))),
            ("own_sem", dma((layers, 4))),
            ("b_send", dma((layers, len(d.pieces), d.z_n, d.y_n, 1 + d.y_n))),
            ("b_recv", dma((layers, len(d.pieces), d.z_n, d.y_n))),
            ("w_sem", dma((layers, 4))),
            ("save_sem", dma((layers, len(SAVED)))),
        ],
        0,
    )
    kinds = ("qkv", "out", "up", "down")
    blocks = [d.block_shape(w) for w in range(4)]
    results = [(layers,) + b for b in blocks]
    if d.whole_lanes:
        results[QKV], results[UP] = w_qkv.shape, w_up.shape
    bwd = call(
        bwd_kernel,
        d,
        [("in_order", SM, piece_order), ("in_lengths", SM, doc_lengths), ("i_gl", ANY, fwd["o_gl"]), ("i_part", ANY, fwd["o_part"]), ("in_gains", VM, fwd["o_gains"])]
        + [("i_" + n, ANY, fwd["o_" + n]) for n in WEIGHTS + SAVED],
        [("o_output", VM, (2, d.half, width), BF), ("o_grad", VM, (2, d.half, width), F32), ("o_gains", VM, (8, width), F32)]
        + [("o_" + k, VM, shape, BF) for k, shape in zip(kinds, results)],
        [(n, pltpu.VMEM(weights[n][0], BF)) for n in WEIGHTS]
        + [(n, pltpu.VMEM(saved[n][0], saved[n][1])) for n in SAVED if n != STREAM]
        + [
            ("gl", pltpu.VMEM((sp_n, 2, d.half, width), BF)),
            ("ml", pltpu.VMEM((sp_n, 2, d.half, width), BF)),
            ("d_att", pltpu.VMEM((sp_n, 2, d.half, d.dh), BF)),
            ("sorted_dqkv", pltpu.VMEM((sp_n, 2, d.half, 3 * d.dh), BF)),
            ("d_qkv", pltpu.VMEM((sp_n, 2, d.half, 3 * d.dh), BF)),
            ("d_keys", pltpu.VMEM((sp_n, tok, d.dh), F32)),
            ("d_values", pltpu.VMEM((sp_n, tok, d.dh), F32)),
            ("gain_sum", pltpu.VMEM((8, width), F32)),
            ("meta", pltpu.SMEM((3, max(sp_n, d.docs)), jnp.int32)),
        ]
        + [("g_" + k, pltpu.VMEM((d.z_n, d.y_n) + b, BF)) for k, b in zip(kinds, blocks)]
        + [("g_up_odd", pltpu.VMEM((d.z_n, d.y_n) + blocks[UP], BF))]
        + [i for l in range(layers) for t in range(len(d.terms)) for i in term_scratch(d, l, t)]
        + [("x_" + k, pltpu.VMEM((layers,) + b, BF)) for k, b in zip(kinds[:3], blocks)]
        + small_scratch(d)
        + comm_scratch(d)
        + [
            ("late_sem", dma((2,))),
            ("load_sem", dma((len(WEIGHTS + SAVED),))),
            ("ry_send", dma((layers, len(d.terms), d.y_n))),
            ("ry_recv", dma((layers, len(d.terms), d.y_n))),
            ("rz_send", dma((layers, len(d.terms), d.y_n, 3))),
            ("rz_recv", dma((layers, len(d.terms), d.y_n, 5))),
            ("rs_send", dma((layers, 4, sp_n))),
            ("rs_recv", dma((layers, 4, sp_n))),
        ],
        1,
    )
    done = call(
        finish_kernel,
        d,
        [("o_" + k, ANY, bwd["o_" + k]) for k in kinds + ("grad", "output")] + [("o_gains", VM, bwd["o_gains"])],
        [("r_" + k, ANY, bwd["o_" + k].shape, F32) for k in kinds]
        + [
            ("r_grad", ANY, bwd["o_grad"].shape, F32),
            ("r_output", ANY, bwd["o_output"].shape, BF),
            ("r_gains", VM, (2 * layers, own), F32),
        ],
        [("a_" + k, pltpu.VMEM(bwd["o_" + k].shape, BF)) for k in kinds]
        + [("b_" + k, pltpu.VMEM(bwd["o_" + k].shape, F32)) for k in kinds]
        + [("a_grad", pltpu.VMEM(bwd["o_grad"].shape, F32)), ("a_output", pltpu.VMEM(bwd["o_output"].shape, BF))]
        + [("in_sem", dma((6,))), ("out_sem", dma((6,)))],
        None,
    )
    grad_qkv, grad_out, grad_up, grad_down = (done["r_" + k] for k in kinds)
    if not d.whole_lanes:
        grad_qkv = grad_qkv.reshape(layers, sp_n, rows, 3, d.dh).transpose(0, 3, 2, 1, 4).reshape(w_qkv.shape)
        grad_up = grad_up.reshape(layers, sp_n, rows, dp_n, d.hid_own).transpose(0, 2, 3, 1, 4).reshape(w_up.shape)
    return (
        done["r_output"].reshape(tokens.shape),
        done["r_grad"].reshape(tokens.shape),
        grad_qkv,
        grad_out,
        grad_up,
        grad_down,
        done["r_gains"].reshape(gains.shape),
    )


def solution(mesh):
    dp, sp = AXES
    by_token, by_axis = P(dp, sp, None), P(dp, None)
    by_row, by_third = P(None, AXES, None), P(None, None, AXES)
    return jax.shard_map(
        functools.partial(shards, mesh.shape[dp], mesh.shape[sp]),
        mesh=mesh,
        in_specs=(by_token, by_token, by_third, by_row, by_row, by_row, by_third, by_axis, by_axis),
        out_specs=(by_token, by_token, by_third, by_row, by_row, by_row, by_third),
        check_vma=False,
    )
```
